512 devices in a mesh: grp: 4 (over y_lo, core), dp: 32 (over z, x), mp: 4 (over y_hi).
Axes of the slice: x: 4, y: 8 (y_hi: 4, y_lo: 2; y = y_hi * 2 + y_lo), z: 8, core: 2. Of those that a mesh axis runs over, the one named last changes fastest.
Arguments:
- hidden: bfloat16 [14336, 4096], P('dp', ('grp', 'mp')), may hold values from -64 to 64
- wq: bfloat16 [4096, 4096], P('dp', ('grp', 'mp')), may hold values from -2 to 2
- kv_enc: bfloat16 [448, 2, 128, 4096], P('dp', None, 'mp', 'grp'), may hold values from -48 to 48
- group_neighbours: int32 [224, 2], replicated, may hold values from 0 to 447, as said below
- gain: float32 [4096], P(('grp', 'mp')), may hold values from 0.5 to 1.5
- d_mixed: bfloat16 [14336, 4096], P('dp', ('grp', 'mp')), may hold values from -6 to 6
Outputs:
- mixed: bfloat16 [14336, 4096], P('dp', ('grp', 'mp'))
- grad_queries: bfloat16 [14336, 4096], P('dp', ('grp', 'mp'))
- grad_kv: bfloat16 [448, 2, 128, 4096], P('dp', None, 'mp', 'grp')
- grad_wq: bfloat16 [4096, 4096], P('dp', ('grp', 'mp'))
The draws below stay inside these ranges and needn't reach their ends.
Inputs may be any that keep to these rules, and one draw needn't show every extreme that they name: `group_neighbours`: every neighbour is named by exactly one slot. Number the blocks of 7 groups and the blocks of 14 neighbours alike, as many as dp devices; one block of groups takes either none or exactly 1 neighbours from one block of neighbours, and every block of neighbours gives some to at least one block of groups.
All inputs are finite; a program needn't handle non-finite values.
Results may differ from the reference program's by a relative error of at most 0.022.
Values may be sent and summed in bfloat16 or wider, within the bound.
No kernel may reach another device: no remote copies, remote signals or barrier semaphores. Data moves between devices by JAX's collectives and lax.ppermute only.
A program may use at most 64 MiB of HBM per device.

```python
import math
import jax
import jax.numpy as jnp
from jax import lax

GROUP_LEN = 64
NEIGHBOURS = 2
NEIGH_LEN = 128
HEADS = 32
HEAD_DIM = 128
DMODEL = 4096
TOK_DEV = 448
NEIGH_DEV = 14
GROUPS = 224
TOKENS = 14336
NEIGH_ALL = 448
FEAT = 4096


def shared_draw(key, align, top):
    n_blocks = NEIGH_ALL // NEIGH_DEV
    width = HEADS * HEAD_DIM
    rho = jax.random.permutation(jax.random.fold_in(key, 1), n_blocks)
    taus = jax.vmap(lambda sub: jax.random.permutation(sub, NEIGH_DEV))(jax.random.split(jax.random.fold_in(key, 2), n_blocks))
    source = jnp.arange(n_blocks, dtype=jnp.int32)[:, None]
    within = jnp.arange(NEIGH_DEV, dtype=jnp.int32)[None, :]
    target = (rho[source] + within) % n_blocks
    ident = source * NEIGH_DEV + taus.astype(jnp.int32)
    mixer = jax.random.permutation(jax.random.fold_in(key, 3), NEIGH_ALL).astype(jnp.int32)
    order_key = target.reshape(-1) * NEIGH_ALL + mixer
    order = jnp.argsort(order_key, stable=True)
    picks = ident.reshape(-1)[order].reshape(GROUPS, NEIGHBOURS).astype(jnp.int32)

    def base(sub, shape):
        normal_part = jnp.clip(jax.random.normal(sub, shape, jnp.float32), -4.0, 4.0)
        return normal_part
    pairing = jax.random.permutation(jax.random.fold_in(key, 11), n_blocks)
    token_block = jnp.arange(TOKENS, dtype=jnp.int32) // TOK_DEV
    column_block = jnp.arange(DMODEL, dtype=jnp.int32) // (DMODEL // n_blocks)
    boost = jnp.where(pairing[token_block][:, None] == column_block[None, :], 4.0, 1.0)
    hidden = base(jax.random.fold_in(key, 4), (TOKENS, DMODEL)) * boost
    wq = base(jax.random.fold_in(key, 12), (DMODEL, width)) * DMODEL ** (-0.5)
    keys = base(jax.random.fold_in(key, 5), (NEIGH_ALL, NEIGH_LEN, width))
    half_log = 0.5 * math.log(top)
    head_scale = jnp.exp(jax.random.uniform(jax.random.fold_in(key, 6), (HEADS,), jnp.float32, 0.0, half_log))
    row_scale = jnp.exp(jax.random.uniform(jax.random.fold_in(key, 7), (NEIGH_ALL, NEIGH_LEN, 1), jnp.float32, 0.0, half_log))
    values = base(jax.random.fold_in(key, 8), (NEIGH_ALL, NEIGH_LEN, width)) * jnp.repeat(head_scale, HEAD_DIM)[None, None, :] * row_scale
    first = picks[:, 0]
    anchor = keys[first, 0]
    table = jnp.array([10.0, 16.0, 24.0], jnp.float32)
    strength = table[jax.random.randint(jax.random.fold_in(key, 9), (GROUPS, HEADS), 0, 3)]
    rows = jnp.arange(GROUPS, dtype=jnp.int32) * GROUP_LEN
    group_ids = jnp.arange(GROUPS, dtype=jnp.int32)
    hidden = hidden.at[rows].set(hidden[rows])
    wq = wq.at[group_ids].set(wq[group_ids] + align * jnp.repeat(strength, HEAD_DIM, axis=1) * anchor / 64.0)
    keys = keys.at[first, 1].set(keys[first, 1])
    return (picks, hidden, wq, jnp.stack([keys, values], axis=1))


def draw_group_neighbours(key, part):
    picks, _, _, _ = shared_draw(key, 0.0, 10.0)
    return picks


def draw_hidden(key, part):
    align, top = (0.0, 10.0)
    _, hidden, _, _ = shared_draw(key, align, top)
    return hidden.astype(jnp.bfloat16)


def draw_wq(key, part):
    align, top = (0.0, 10.0)
    _, _, wq, _ = shared_draw(key, align, top)
    return wq.astype(jnp.bfloat16)


def draw_kv_enc(key, part):
    align, top = (0.0, 10.0)
    _, _, _, pairs = shared_draw(key, align, top)
    return pairs.astype(jnp.bfloat16)


def shard_levels(rng, shape, cuts, smallest, high):
    level = 1.0
    for dim, shards_of in cuts:
        draws = jax.random.uniform(jax.random.fold_in(jax.random.fold_in(rng, 6), dim), (shards_of,), jnp.float32, smallest / len(cuts), high / len(cuts))
        level = level * jnp.repeat(jnp.exp(draws), shape[dim] // shards_of).reshape((-1,) + (1,) * (len(shape) - 1 - dim))
    return level


def scatter_about(stream_key, extent, scale, reach, pieces=(), kind=jnp.bfloat16):
    entries = jax.random.normal(stream_key, extent, jnp.float32) * scale
    if len(pieces) > 0:
        entries = shard_levels(stream_key, extent, pieces, -0.22, 0.18) * entries
    return jnp.clip(entries, min=-reach, max=reach).astype(kind)


def setup_inputs(seed: int = 0) -> dict:
    splits = jax.random.split(jax.random.key(seed), 7)
    hidden = draw_hidden(jax.random.fold_in(splits[6], 71), 0)
    wq = draw_wq(jax.random.fold_in(splits[6], 71), 0)
    kv_enc = draw_kv_enc(jax.random.fold_in(splits[6], 71), 0)
    group_neighbours = draw_group_neighbours(jax.random.fold_in(splits[6], 71), 0)
    gain = jnp.clip(1.0 + 0.1 * jax.random.normal(splits[4], (FEAT,), jnp.float32), 0.5, 1.5)
    d_mixed = scatter_about(splits[5], (TOKENS, FEAT), 1.0, 6.0, ((0, 32), (1, 16)))
    return dict(hidden=hidden, wq=wq, kv_enc=kv_enc, group_neighbours=group_neighbours, gain=gain, d_mixed=d_mixed)


def group_pass(query_rows, near, cot_rows, gain):
    scale = HEAD_DIM ** (-0.5)
    width = HEADS * HEAD_DIM
    span = NEIGHBOURS * NEIGH_LEN
    keys = near[:, 0].reshape(span, HEADS, HEAD_DIM).astype(jnp.float32)
    values = near[:, 1].reshape(span, HEADS, HEAD_DIM).astype(jnp.float32)
    qh = query_rows.reshape(GROUP_LEN, HEADS, HEAD_DIM).astype(jnp.float32)
    scores = jnp.einsum('ihd,thd->hit', qh, keys) * scale
    top = lax.optimization_barrier(jnp.max(scores, axis=-1, keepdims=True))
    expo = jnp.exp(scores - top)
    probs = expo / lax.optimization_barrier(jnp.sum(expo, axis=-1, keepdims=True))
    weights = probs.astype(jnp.bfloat16).astype(jnp.float32)
    heads_out = jnp.einsum('hit,thd->ihd', weights, values)
    attended = heads_out.reshape(GROUP_LEN, width)
    inverse = lax.rsqrt(lax.optimization_barrier(jnp.sum(attended * attended, axis=-1)) / width + 1e-06)
    mixed = (attended * inverse[:, None] * gain).astype(jnp.bfloat16)
    grad_in = cot_rows.astype(jnp.float32) * gain
    grad_dot = lax.optimization_barrier(jnp.sum(grad_in * attended, axis=-1))
    grad_att = inverse[:, None] * (grad_in - attended * (grad_dot * inverse * inverse / width)[:, None])
    grad_b = grad_att.astype(jnp.bfloat16).astype(jnp.float32).reshape(GROUP_LEN, HEADS, HEAD_DIM)
    grad_probs = jnp.einsum('ihd,thd->hit', grad_b, values)
    delta = jnp.swapaxes(lax.optimization_barrier(jnp.sum(grad_b * heads_out, axis=-1)), 0, 1)
    grad_scores = (probs * (grad_probs - delta[:, :, None])).astype(jnp.bfloat16).astype(jnp.float32)
    grad_q = (jnp.einsum('hit,thd->ihd', grad_scores, keys) * scale).astype(jnp.bfloat16)
    grad_k = (jnp.einsum('hit,ihd->thd', grad_scores, qh) * scale).astype(jnp.bfloat16)
    grad_v = jnp.einsum('hit,ihd->thd', weights, grad_b).astype(jnp.bfloat16)
    grad_k = grad_k.reshape(NEIGHBOURS, NEIGH_LEN, width)
    grad_v = grad_v.reshape(NEIGHBOURS, NEIGH_LEN, width)
    return (mixed, grad_q.reshape(GROUP_LEN, width), jnp.stack([grad_k, grad_v], axis=1))

def reference(hidden, wq, kv_enc, group_neighbours, gain, d_mixed):
    width = HEADS * HEAD_DIM
    queries = jnp.dot(hidden, wq, preferred_element_type=jnp.float32).astype(jnp.bfloat16)
    query_blocks = queries.reshape(GROUPS, GROUP_LEN, width)
    cot_blocks = d_mixed.reshape(GROUPS, GROUP_LEN, width)

    def one_group(items):
        query_rows, picks, cot_rows = items
        near = jnp.take(kv_enc, picks, axis=0)
        return group_pass(query_rows, near, cot_rows, gain)
    mixed, grad_q, grad_near = lax.map(one_group, (query_blocks, group_neighbours, cot_blocks))
    flat_ids = group_neighbours.reshape(-1).astype(jnp.int32)
    grad_kv = jnp.zeros((NEIGH_ALL, 2, NEIGH_LEN, width), jnp.bfloat16)
    grad_kv = grad_kv.at[flat_ids].set(grad_near.reshape(NEIGH_ALL, 2, NEIGH_LEN, width))
    grad_q = grad_q.reshape(TOKENS, width)
    grad_wq = lax.dot_general(hidden, grad_q, (((0,), (0,)), ((), ())), preferred_element_type=jnp.float32).astype(jnp.bfloat16)
    return (mixed.reshape(TOKENS, width), grad_q, grad_kv, grad_wq)
```

```python
import jax
import jax.numpy as jnp
from jax import lax
from jax.sharding import Mesh
from jax.sharding import PartitionSpec as P

GROUP_LEN = 64
NEIGHBOURS = 2
HEADS = 32
HEAD_DIM = 128
DP = ("dz", "dx")
GRP = ("yl", "co")


def lookup(position, length, count):
    select = position[None, :] == jnp.arange(length, dtype=jnp.int32)[:, None]
    rows = jnp.sum(jnp.where(select, jnp.arange(count, dtype=jnp.int32)[None, :], 0), axis=1)
    return (rows, jnp.any(select, axis=1))


def relayout(block):
    shape = block.shape
    flat = block.reshape((shape[0] * shape[1],) + shape[2:])
    moved = lax.all_to_all(flat, DP + ("mp",), split_axis=0, concat_axis=0, tiled=True)
    return moved.reshape(shape)


def gather_weight(wq):
    near = lax.all_gather(wq, "dz", axis=0)
    both = lax.all_gather(near, "dx", axis=1)
    return both.reshape(-1, wq.shape[1])


def gather_hidden(hidden):
    line = lax.all_gather(hidden, ("yl", "mp"), axis=0)
    both = lax.all_gather(line, "co", axis=0)
    rows, width = hidden.shape
    n_co, n_line = both.shape[:2]
    n_yl = lax.axis_size("yl")
    blocks = both.reshape(n_co, n_yl, n_line // n_yl, rows, width)
    return blocks.transpose(3, 1, 0, 2, 4).reshape(rows, -1)


def total_over_heads(pair):
    axes = GRP + ("mp",)
    count = lax.axis_size(axes)
    flat = jnp.stack(pair).reshape(-1, 128)
    spread = jnp.broadcast_to(flat[None], (count,) + flat.shape)
    moved = lax.all_to_all(spread, axes, split_axis=0, concat_axis=0, tiled=True)
    return jnp.sum(moved, axis=0).reshape(2, -1)


def scatter_weight(partial):
    n_z, n_x = lax.axis_size("dz"), lax.axis_size("dx")
    blocks = partial.reshape(n_z, n_x, -1, partial.shape[1])
    column = lax.psum_scatter(blocks, "dx", scatter_dimension=1, tiled=False)
    return lax.psum_scatter(column, "dz", scatter_dimension=0, tiled=False)


def shards(hidden, wq, kv_enc, group_neighbours, gain, d_mixed):
    n_dp = lax.axis_size(DP)
    n_mp = lax.axis_size("mp")
    me_dp = lax.axis_index(DP)
    neigh_dev, _, quarter, enc_width = kv_enc.shape
    dec_width = wq.shape[1]
    heads_here = dec_width // HEAD_DIM
    tok_dev = hidden.shape[0]
    groups_here = tok_dev // GROUP_LEN
    span = quarter * n_mp
    slot_cap = max(1, neigh_dev // n_dp)
    scale = HEAD_DIM ** (-0.5)
    width = HEADS * HEAD_DIM
    flat_ids = group_neighbours.reshape(-1)
    total = flat_ids.shape[0]
    counter = jnp.arange(neigh_dev, dtype=jnp.int32)
    full_rows = gather_hidden(hidden)
    columns = full_rows
    queries = jnp.dot(
        columns, gather_weight(wq), preferred_element_type=jnp.float32
    ).astype(jnp.bfloat16)
    owned = me_dp * neigh_dev + counter
    matches = flat_ids[None, :] == owned[:, None]
    slot_of = jnp.sum(jnp.where(matches, jnp.arange(total, dtype=jnp.int32)[None, :], 0), axis=1)
    target = slot_of // neigh_dev
    send_rank = jnp.sum(
        (target[:, None] == target[None, :]) & (counter[None, :] < counter[:, None]), axis=1
    )
    send_pos = target * slot_cap + send_rank
    send_rows, send_used = lookup(send_pos, n_dp * slot_cap, neigh_dev)
    packed = jnp.where(
        send_used[:, None, None, None],
        jnp.take(kv_enc, send_rows, axis=0),
        jnp.zeros((), jnp.bfloat16),
    )
    packed = packed.reshape(n_dp, slot_cap, 2, quarter, n_mp, dec_width).transpose(0, 4, 1, 2, 3, 5)
    arrived = relayout(packed)
    arrived = arrived.transpose(0, 2, 3, 1, 4, 5).reshape(n_dp * slot_cap, 2, span, dec_width)
    mine = lax.dynamic_slice_in_dim(flat_ids, me_dp * neigh_dev, neigh_dev)
    source = mine // neigh_dev
    recv_rank = jnp.sum(
        (source[:, None] == source[None, :]) & (mine[None, :] < mine[:, None]), axis=1
    )
    recv_pos = source * slot_cap + recv_rank
    near = jnp.take(arrived, recv_pos, axis=0)
    keys = near[:, 0].reshape(groups_here, NEIGHBOURS * span, heads_here, HEAD_DIM)
    values = near[:, 1].reshape(groups_here, NEIGHBOURS * span, heads_here, HEAD_DIM)
    query_heads = queries.reshape(groups_here, GROUP_LEN, heads_here, HEAD_DIM)
    scores = (
        jnp.einsum("cihd,cthd->chit", query_heads, keys, preferred_element_type=jnp.float32) * scale
    )
    top = jnp.max(scores, axis=-1, keepdims=True)
    expo = jnp.exp(scores - top)
    probs = expo / jnp.sum(expo, axis=-1, keepdims=True)
    weights = probs.astype(jnp.bfloat16)
    heads_out = jnp.einsum("chit,cthd->cihd", weights, values, preferred_element_type=jnp.float32)
    attended = heads_out.reshape(tok_dev, dec_width)
    grad_in = d_mixed.astype(jnp.float32) * gain
    square_sum, grad_dot = total_over_heads(
        (jnp.sum(attended * attended, axis=-1), jnp.sum(grad_in * attended, axis=-1))
    )
    inverse = lax.rsqrt(square_sum / width + 1e-06)
    mixed = (attended * inverse[:, None] * gain).astype(jnp.bfloat16)
    grad_att = inverse[:, None] * (
        grad_in - attended * (grad_dot * inverse * inverse / width)[:, None]
    )
    grad_b = grad_att.astype(jnp.bfloat16).reshape(groups_here, GROUP_LEN, heads_here, HEAD_DIM)
    grad_probs = jnp.einsum("cihd,cthd->chit", grad_b, values, preferred_element_type=jnp.float32)
    delta = jnp.swapaxes(jnp.sum(grad_b.astype(jnp.float32) * heads_out, axis=-1), 1, 2)
    grad_scores = (probs * (grad_probs - delta[..., None])).astype(jnp.bfloat16)
    grad_q = (
        jnp.einsum("chit,cthd->cihd", grad_scores, keys, preferred_element_type=jnp.float32) * scale
    )
    grad_q = grad_q.astype(jnp.bfloat16).reshape(tok_dev, dec_width)
    grad_k = (
        jnp.einsum("chit,cihd->cthd", grad_scores, query_heads, preferred_element_type=jnp.float32)
        * scale
    ).astype(jnp.bfloat16)
    grad_v = jnp.einsum(
        "chit,cihd->cthd", weights, grad_b, preferred_element_type=jnp.float32
    ).astype(jnp.bfloat16)
    back = jnp.stack(
        [grad_k.reshape(neigh_dev, span, dec_width), grad_v.reshape(neigh_dev, span, dec_width)],
        axis=1,
    )
    back_rows, back_used = lookup(recv_pos, n_dp * slot_cap, neigh_dev)
    outgoing = jnp.where(
        back_used[:, None, None, None],
        jnp.take(back, back_rows, axis=0),
        jnp.zeros((), jnp.bfloat16),
    )
    outgoing = outgoing.reshape(n_dp, slot_cap, 2, n_mp, quarter, dec_width).transpose(
        0, 3, 1, 2, 4, 5
    )
    returned = relayout(outgoing)
    returned = returned.transpose(0, 2, 3, 4, 1, 5).reshape(
        n_dp * slot_cap, 2, quarter, n_mp * dec_width
    )
    grad_kv = jnp.take(returned, send_pos, axis=0)
    columns = full_rows
    grad_wq = scatter_weight(
        lax.dot_general(
            columns, grad_q, (((0,), (0,)), ((), ())), preferred_element_type=jnp.float32
        ).astype(jnp.bfloat16)
    )
    return (mixed, grad_q, grad_kv, grad_wq)


def solution(mesh):
    cut = Mesh(mesh.devices.reshape(2, 2, 8, 4, 4), GRP + DP + ("mp",))
    heads = GRP + ("mp",)
    placed = (P(DP, heads), P(DP, heads), P(DP, None, "mp", GRP), P(), P(heads), P(DP, heads))
    return jax.shard_map(
        shards,
        mesh=cut,
        in_specs=placed,
        out_specs=(P(DP, heads), P(DP, heads), P(DP, None, "mp", GRP), P(DP, heads)),
        check_vma=False,
    )
```

```python
import functools

import jax
import jax.numpy as jnp
from jax import lax
from jax.experimental import pallas as pl
from jax.experimental.pallas import tpu as pltpu
from jax.sharding import Mesh
from jax.sharding import PartitionSpec as P

GROUP_LEN = 64
NEIGHBOURS = 2
HEAD_DIM = 128
EXTRA = 16
EPS = 1e-06
SCALE = HEAD_DIM ** (-0.5)
DP = ("dz", "dx")
GRP = ("yl", "co")
LINE = ("yl", "mp")
BF = jnp.bfloat16
F32 = jnp.float32
SMEM = pl.BlockSpec(memory_space=pltpu.SMEM)
VMEM = pl.BlockSpec(memory_space=pltpu.VMEM)
PARAMS = pltpu.CompilerParams(vmem_limit_bytes=40 << 20)
LAST = (((1,), (1,)), ((), ()))
FIRST = (((0,), (0,)), ((), ()))
PLAIN = (((1,), (0,)), ((), ()))


def call(kernel, scalars, arrays, outs):
    return pl.pallas_call(
        kernel,
        in_specs=[SMEM] * len(scalars) + [VMEM] * len(arrays),
        out_specs=[VMEM] * len(outs),
        out_shape=[jax.ShapeDtypeStruct(shape, kind) for shape, kind in outs],
        compiler_params=PARAMS,
    )(*scalars, *arrays)


def exchange(array, axes):
    return lax.all_to_all(array, axes, split_axis=0, concat_axis=0, tiled=True)


def copies(array, count):
    return jnp.broadcast_to(array[None], (count,) + array.shape)


def shift(array, axis, step):
    size = lax.axis_size(axis)
    return lax.ppermute(array, axis, [(i, (i + step) % size) for i in range(size)])


def dot(a, b, dims):
    return lax.dot_general(a, b, dims, preferred_element_type=F32)


def eye(size):
    rows = lax.broadcasted_iota(jnp.int32, (size, size), 0)
    return rows == lax.broadcasted_iota(jnp.int32, (size, size), 1)


def as_column(row):
    return jnp.sum(jnp.where(eye(row.shape[1]), row, 0.0), axis=1, keepdims=True)


def as_row(column):
    return jnp.sum(jnp.where(eye(column.shape[0]), column, 0.0), axis=0, keepdims=True)


def by_head(block):
    blank = jnp.zeros((block.shape[0], HEAD_DIM), block.dtype)
    upper = jnp.concatenate([block[:, :HEAD_DIM], blank], axis=1)
    lower = jnp.concatenate([blank, block[:, HEAD_DIM:]], axis=1)
    return jnp.concatenate([upper, lower], axis=0)


def own_head(both):
    half = both.shape[0] // 2
    return jnp.concatenate([both[:half, :HEAD_DIM], both[half:, HEAD_DIM:]], axis=1)


def pieces(row, count, width):
    index = lax.broadcasted_iota(jnp.int32, (EXTRA, row.shape[1]), 0)
    tile = jnp.zeros((EXTRA, row.shape[1]), F32)
    rest = row
    for i in range(count):
        part = rest.astype(BF).astype(F32)
        tile = jnp.where(index == i, part, tile)
        rest = rest - part
    blank = jnp.zeros((EXTRA, width - row.shape[1]), F32)
    return jnp.concatenate([tile, blank], axis=1).astype(BF)


def joined(tile, count, width):
    tile = tile.astype(F32)[:, :width]
    index = lax.broadcasted_iota(jnp.int32, tile.shape, 0)
    return jnp.sum(jnp.where(index < count, tile, 0.0), axis=0, keepdims=True)


def split_kernel(place, *refs):
    for block, out in zip(refs[:4], refs[4:]):
        out[...] = block[...]


def weight_rows(line, co, n_co, n_mp):
    return (line // n_mp * n_co + co) * n_mp + line % n_mp


def query_kernel(sizes, place, source, mine, other, weight, slots, total):
    n_co, n_mp, n_x = sizes
    rows = weight.shape[2]
    per = mine.shape[2] // rows
    for part, block in enumerate((mine, other)):
        co = lax.rem(place[1] + part, n_co)
        for line in range(mine.shape[0]):
            first = weight_rows(line, co, n_co, n_mp) * per
            w = jnp.concatenate(
                [weight[lax.rem(first + i, n_x), lax.div(first + i, n_x)] for i in range(per)], axis=0
            )
            product = dot(block[line], w, PLAIN)
            if part == 0 and line == 0:
                total[...] = product
            else:
                total[...] += product
    for k in range(source.shape[0]):
        c = k // NEIGHBOURS
        slots[source[k]] = total[c * GROUP_LEN : (c + 1) * GROUP_LEN].astype(BF)


def owner_forward_kernel(target, arrived, kv0, kv1, kv2, kv3, slots, probs):
    for n in range(target.shape[0]):
        t = target[n]
        keys = jnp.concatenate([kv[n, 0] for kv in (kv0, kv1, kv2, kv3)], axis=0)
        values = jnp.concatenate([kv[n, 1] for kv in (kv0, kv1, kv2, kv3)], axis=0)
        scores = dot(keys, by_head(arrived[t]), LAST) * SCALE
        top = jnp.max(scores, axis=0, keepdims=True)
        expo = jnp.exp(scores - top)
        total = jnp.sum(expo, axis=0, keepdims=True)
        prob = expo / total
        probs[n] = prob
        out = own_head(dot(prob.astype(BF), values, FIRST))
        slots[t, :GROUP_LEN, :] = out.astype(BF)
        slots[t, GROUP_LEN:, :] = pieces(top + jnp.log(total), 3, out.shape[1])


def combine_kernel(source, arrived, d_mixed, gain, attended, shares, stats):
    stats[...] = jnp.zeros_like(stats)
    shares[...] = jnp.zeros_like(shares)
    lanes = NEIGHBOURS * GROUP_LEN
    for c in range(source.shape[0] // NEIGHBOURS):
        here = slice(c * GROUP_LEN, (c + 1) * GROUP_LEN)
        tiles = [arrived[source[NEIGHBOURS * c + k]] for k in range(NEIGHBOURS)]
        logs = [joined(tile[GROUP_LEN:], 3, lanes) for tile in tiles]
        top = jnp.maximum(logs[0], logs[1])
        expos = [jnp.exp(log - top) for log in logs]
        rest = 1.0 / (expos[0] + expos[1])
        out = jnp.zeros((GROUP_LEN, 2 * HEAD_DIM), F32)
        for k in range(NEIGHBOURS):
            share = expos[k] * rest
            shares[NEIGHBOURS * c + k : NEIGHBOURS * c + k + 1, :] = share
            column = as_column(share)
            value = tiles[k][:GROUP_LEN].astype(F32)
            out = out + jnp.concatenate(
                [
                    value[:, :HEAD_DIM] * column[:GROUP_LEN],
                    value[:, HEAD_DIM:] * column[GROUP_LEN:],
                ],
                axis=1,
            )
        attended[here, :] = out
        grad_in = d_mixed[here, :].astype(F32) * gain[...]
        column = jnp.concatenate(
            [
                jnp.sum(out * out, axis=1, keepdims=True),
                jnp.sum(grad_in * out, axis=1, keepdims=True),
            ],
            axis=0,
        )
        stats[c : c + 1, :] = as_row(column)


def grad_kernel(width, source, moved, attended, shares, d_mixed, gain, mixed, slots):
    total = jnp.sum(moved[...], axis=0)
    for c in range(source.shape[0] // NEIGHBOURS):
        here = slice(c * GROUP_LEN, (c + 1) * GROUP_LEN)
        column = as_column(total[c : c + 1, :])
        inverse = lax.rsqrt(column[:GROUP_LEN] / width + EPS)
        out = attended[here, :]
        grad_in = d_mixed[here, :].astype(F32) * gain[...]
        mixed[here, :] = (out * inverse * gain[...]).astype(BF)
        factor = column[GROUP_LEN:] * inverse * inverse / width
        grad = (inverse * (grad_in - out * factor)).astype(BF).astype(F32)
        inner = grad * out
        delta = jnp.concatenate(
            [
                jnp.sum(inner[:, :HEAD_DIM], axis=1, keepdims=True),
                jnp.sum(inner[:, HEAD_DIM:], axis=1, keepdims=True),
            ],
            axis=0,
        )
        for k in range(NEIGHBOURS):
            slot = source[NEIGHBOURS * c + k]
            share = as_column(shares[NEIGHBOURS * c + k : NEIGHBOURS * c + k + 1, :])
            scaled = jnp.concatenate(
                [grad[:, :HEAD_DIM] * share[:GROUP_LEN], grad[:, HEAD_DIM:] * share[GROUP_LEN:]],
                axis=1,
            )
            slots[slot, :GROUP_LEN, :] = scaled.astype(BF)
            slots[slot, GROUP_LEN:, :] = pieces(as_row(delta * share), 2, scaled.shape[1])


def owner_backward_kernel(target, arrived, queries, probs, *refs):
    kv_refs, slots, outs = refs[:4], refs[4], refs[5:]
    for n in range(target.shape[0]):
        t = target[n]
        keys = jnp.concatenate([kv[n, 0] for kv in kv_refs], axis=0)
        values = jnp.concatenate([kv[n, 1] for kv in kv_refs], axis=0)
        grad = by_head(arrived[t, :GROUP_LEN, :])
        query = by_head(queries[t])
        prob = probs[n]
        delta = joined(arrived[t, GROUP_LEN:, :], 2, prob.shape[1])
        grad_scores = (prob * (dot(values, grad, LAST) - delta)).astype(BF)
        slots[t] = (own_head(dot(grad_scores, keys, FIRST)) * SCALE).astype(BF)
        grad_keys = (dot(grad_scores, query, PLAIN) * SCALE).astype(BF)
        grad_values = dot(prob.astype(BF), grad, PLAIN).astype(BF)
        rows = grad_keys.shape[0] // 4
        for d in range(4):
            outs[d][n, 0] = grad_keys[d * rows : (d + 1) * rows]
            outs[d][n, 1] = grad_values[d * rows : (d + 1) * rows]


def weight_kernel(sizes, place, source, arrived, mine, other, grad_q, partial):
    n_co, n_mp, n_x = sizes
    for c in range(source.shape[0] // NEIGHBOURS):
        both = sum(arrived[source[NEIGHBOURS * c + k]].astype(F32) for k in range(NEIGHBOURS))
        grad_q[c * GROUP_LEN : (c + 1) * GROUP_LEN, :] = both.astype(BF)
    rows = partial.shape[2]
    per = mine.shape[2] // rows
    for part, block in enumerate((mine, other)):
        co = lax.rem(place[1] + part, n_co)
        for line in range(mine.shape[0]):
            first = weight_rows(line, co, n_co, n_mp) * per
            product = dot(block[line], grad_q[...], FIRST).astype(BF)
            for i in range(per):
                partial[lax.rem(first + i, n_x), lax.div(first + i, n_x)] = product[
                    i * rows : (i + 1) * rows
                ]


def merge_kernel(place, *refs):
    pieces_in, out = refs[:-1], refs[-1]
    for d in range(4):

        @pl.when(pl.program_id(0) == d)
        def _():
            out[...] = pieces_in[d][...]


def split_by_quarter(place, kv):
    n, _, quarter, width = kv.shape
    part = width // 4
    take = [
        pl.BlockSpec((n, 2, quarter, part), functools.partial(block_at, d)) for d in range(4)
    ]
    whole = pl.BlockSpec((n, 2, quarter, part), lambda i, place: (0, 0, 0, 0))
    return pl.pallas_call(
        split_kernel,
        grid_spec=pltpu.PrefetchScalarGridSpec(
            num_scalar_prefetch=1, grid=(1,), in_specs=take, out_specs=[whole] * 4
        ),
        out_shape=[jax.ShapeDtypeStruct((n, 2, quarter, part), kv.dtype)] * 4,
        compiler_params=PARAMS,
    )(place, kv, kv, kv, kv)


def block_at(d, i, place):
    return (0, 0, 0, lax.rem(place[0] + d, 4))


def merge_quarters(place, parts):
    n, _, quarter, part = parts[0].shape
    whole = pl.BlockSpec((n, 2, quarter, part), lambda i, place: (0, 0, 0, 0))
    return pl.pallas_call(
        merge_kernel,
        grid_spec=pltpu.PrefetchScalarGridSpec(
            num_scalar_prefetch=1,
            grid=(4,),
            in_specs=[whole] * 4,
            out_specs=pl.BlockSpec(
                (n, 2, quarter, part), lambda i, place: (0, 0, 0, lax.rem(place[0] + i, 4))
            ),
        ),
        out_shape=jax.ShapeDtypeStruct((n, 2, quarter, 4 * part), parts[0].dtype),
        compiler_params=PARAMS,
    )(place, *parts)


def shards(hidden, wq, kv_enc, group_neighbours, gain, d_mixed):
    n_z, n_x = lax.axis_size("dz"), lax.axis_size("dx")
    n_co, n_mp = lax.axis_size("co"), lax.axis_size("mp")
    n_dp = n_z * n_x
    heads = GRP + ("mp",)
    n_heads = lax.axis_size(heads)
    sizes = (n_co, n_mp, n_x)
    me_dp = lax.axis_index(DP)
    neigh_dev = kv_enc.shape[0]
    tok_dev, dec_width = hidden.shape[0], wq.shape[1]
    model = wq.shape[0] * n_dp
    gain = gain.reshape(1, dec_width)
    place = jnp.stack([lax.axis_index("mp"), lax.axis_index("co")]).astype(jnp.int32)
    flat_ids = group_neighbours.reshape(-1)
    slot_block = jnp.arange(flat_ids.shape[0], dtype=jnp.int32) // neigh_dev
    owned = me_dp * neigh_dev + jnp.arange(neigh_dev, dtype=jnp.int32)
    matches = flat_ids[None, :] == owned[:, None]
    target = jnp.sum(jnp.where(matches, slot_block[None, :], 0), axis=1)
    source = lax.dynamic_slice_in_dim(flat_ids, me_dp * neigh_dev, neigh_dev) // neigh_dev

    line = lax.all_gather(hidden, LINE, axis=0)
    near = exchange(copies(wq, n_z), "dz").reshape(n_z, -1, dec_width)
    weight = exchange(copies(near, n_x).reshape(n_x * n_z, -1, dec_width), "dx")
    weight = weight.reshape(n_x, n_z, -1, dec_width)
    other = shift(line, "co", 1)

    split = split_by_quarter(place, kv_enc)
    kv = [shift(part, "mp", d) if d else part for d, part in enumerate(split)]

    (slots,) = pl.pallas_call(
        functools.partial(query_kernel, sizes),
        in_specs=[SMEM, SMEM, VMEM, VMEM, VMEM],
        out_specs=[VMEM],
        out_shape=[jax.ShapeDtypeStruct((n_dp, GROUP_LEN, dec_width), BF)],
        scratch_shapes=[pltpu.VMEM((tok_dev, dec_width), F32)],
        compiler_params=PARAMS,
    )(place, source, line, other, weight)
    queries = exchange(slots, DP)

    wide = (n_dp, GROUP_LEN + EXTRA, dec_width)
    span = kv_enc.shape[2] * n_mp
    slots, probs = call(
        owner_forward_kernel,
        (target,),
        (queries, *kv),
        [(wide, BF), ((neigh_dev, span, 2 * GROUP_LEN), F32)],
    )
    arrived = exchange(slots, DP)
    attended, shares, stats = call(
        combine_kernel,
        (source,),
        (arrived, d_mixed, gain),
        [((tok_dev, dec_width), F32), ((16, 128), F32), ((8, 128), F32)],
    )
    moved = exchange(copies(stats, n_heads), heads)
    mixed, slots = call(
        functools.partial(grad_kernel, model),
        (source,),
        (moved, attended, shares, d_mixed, gain),
        [((tok_dev, dec_width), BF), (wide, BF)],
    )
    arrived = exchange(slots, DP)
    slots, *parts = call(
        owner_backward_kernel,
        (target,),
        (arrived, queries, probs, *kv),
        [((n_dp, GROUP_LEN, dec_width), BF)] + [(kv[0].shape, BF)] * 4,
    )
    arrived = exchange(slots, DP)
    grad_q, partial = call(
        functools.partial(weight_kernel, sizes),
        (place, source),
        (arrived, line, other),
        [((tok_dev, dec_width), BF), (weight.shape, BF)],
    )
    parts = [shift(part, "mp", -d) if d else part for d, part in enumerate(parts)]
    column = exchange(partial.reshape(n_x * n_z, -1, dec_width), "dx").reshape(weight.shape)
    column = jnp.sum(column, axis=0, dtype=F32).astype(BF)
    grad_wq = jnp.sum(exchange(column, "dz"), axis=0, dtype=F32).astype(BF)
    grad_kv = merge_quarters(place, parts)
    return (mixed, grad_q, grad_kv, grad_wq)


def solution(mesh):
    cut = Mesh(mesh.devices.reshape(2, 2, 8, 4, 4), GRP + DP + ("mp",))
    heads = GRP + ("mp",)
    placed = (P(DP, heads), P(DP, heads), P(DP, None, "mp", GRP), P(), P(heads), P(DP, heads))
    return jax.shard_map(
        shards,
        mesh=cut,
        in_specs=placed,
        out_specs=(P(DP, heads), P(DP, heads), P(DP, None, "mp", GRP), P(DP, heads)),
        check_vma=False,
    )
```

```python
import functools

import jax
import jax.numpy as jnp
from jax import lax
from jax.experimental import pallas as pl
from jax.experimental.pallas import tpu as pltpu
from jax.sharding import Mesh
from jax.sharding import PartitionSpec as P

GROUP_LEN = 64
NEIGHBOURS = 2
HEAD_DIM = 128
EXTRA = 16
EPS = 1e-06
SCALE = HEAD_DIM ** (-0.5)
DP = ("dz", "dx")
GRP = ("yl", "co")
LINE = ("yl", "mp")
BF = jnp.bfloat16
F32 = jnp.float32
SMEM = pl.BlockSpec(memory_space=pltpu.SMEM)
VMEM = pl.BlockSpec(memory_space=pltpu.VMEM)
PARAMS = pltpu.CompilerParams(vmem_limit_bytes=40 << 20)
LAST = (((1,), (1,)), ((), ()))
FIRST = (((0,), (0,)), ((), ()))
PLAIN = (((1,), (0,)), ((), ()))


def call(kernel, scalars, arrays, outs):
    return pl.pallas_call(
        kernel,
        in_specs=[SMEM] * len(scalars) + [VMEM] * len(arrays),
        out_specs=[VMEM] * len(outs),
        out_shape=[jax.ShapeDtypeStruct(shape, kind) for shape, kind in outs],
        compiler_params=PARAMS,
    )(*scalars, *arrays)


def exchange(array, axes):
    return lax.all_to_all(array, axes, split_axis=0, concat_axis=0, tiled=True)


def copies(array, count):
    return jnp.broadcast_to(array[None], (count,) + array.shape)


def shift(array, axis, step):
    size = lax.axis_size(axis)
    return lax.ppermute(array, axis, [(i, (i + step) % size) for i in range(size)])


def dot(a, b, dims):
    return lax.dot_general(a, b, dims, preferred_element_type=F32)


def eye(size):
    rows = lax.broadcasted_iota(jnp.int32, (size, size), 0)
    return rows == lax.broadcasted_iota(jnp.int32, (size, size), 1)


def as_column(row):
    return jnp.sum(jnp.where(eye(row.shape[1]), row, 0.0), axis=1, keepdims=True)


def as_row(column):
    return jnp.sum(jnp.where(eye(column.shape[0]), column, 0.0), axis=0, keepdims=True)


def by_head(block):
    blank = jnp.zeros((block.shape[0], HEAD_DIM), block.dtype)
    upper = jnp.concatenate([block[:, :HEAD_DIM], blank], axis=1)
    lower = jnp.concatenate([blank, block[:, HEAD_DIM:]], axis=1)
    return jnp.concatenate([upper, lower], axis=0)


def own_head(both):
    half = both.shape[0] // 2
    return jnp.concatenate([both[:half, :HEAD_DIM], both[half:, HEAD_DIM:]], axis=1)


def pieces(row, count):
    index = lax.broadcasted_iota(jnp.int32, (EXTRA, row.shape[1]), 0)
    tile = jnp.zeros((EXTRA, row.shape[1]), F32)
    rest = row
    for i in range(count):
        part = rest.astype(BF).astype(F32)
        tile = jnp.where(index == i, part, tile)
        rest = rest - part
    return tile.astype(BF)


def write_slot(slots, slot, block, row, count):
    width = block.shape[1]
    for i in range(GROUP_LEN // EXTRA):
        slots[slot, :, i * width : (i + 1) * width] = block[i * EXTRA : (i + 1) * EXTRA]
    slots[slot, :, GROUP_LEN // EXTRA * width :] = pieces(row, count)


def read_slot(slots, slot, width, count):
    folds = GROUP_LEN // EXTRA
    tile = slots[slot]
    block = jnp.concatenate([tile[:, i * width : (i + 1) * width] for i in range(folds)], axis=0)
    return block, joined(tile[:, folds * width :], count)


def joined(tile, count):
    tile = tile.astype(F32)
    index = lax.broadcasted_iota(jnp.int32, tile.shape, 0)
    return jnp.sum(jnp.where(index < count, tile, 0.0), axis=0, keepdims=True)


def split_kernel(place, block0, block1, block2, block3, own, up, down):
    own[...] = block0[...]
    up[:, :2] = block1[...]
    up[:, 2] = block2[:, 0]
    down[:, :2] = block3[...]
    down[:, 2] = block2[:, 1]


def whole_rows(n, own, first, far_keys, far_values, last):
    return [
        jnp.concatenate([own[n, i], first[n, i], far[n], last[n, i]], axis=0)
        for i, far in enumerate((far_keys, far_values))
    ]


def weight_rows(line, co, n_co, n_mp):
    return (line // n_mp * n_co + co) * n_mp + line % n_mp


def query_kernel(sizes, place, source, mine, other, weight, slots, total):
    n_co, n_mp, n_x = sizes
    rows = weight.shape[2]
    per = mine.shape[2] // rows
    for part, block in enumerate((mine, other)):
        co = lax.rem(place[1] + part, n_co)
        for line in range(mine.shape[0]):
            first = weight_rows(line, co, n_co, n_mp) * per
            w = jnp.concatenate(
                [weight[lax.rem(first + i, n_x), lax.div(first + i, n_x)] for i in range(per)], axis=0
            )
            product = dot(block[line], w, PLAIN)
            if part == 0 and line == 0:
                total[...] = product
            else:
                total[...] += product
    for k in range(source.shape[0]):
        c = k // NEIGHBOURS
        slots[source[k]] = total[c * GROUP_LEN : (c + 1) * GROUP_LEN].astype(BF)


def owner_forward_kernel(target, arrived, own, first, far_keys, far_values, last, slots, probs):
    for n in range(target.shape[0]):
        t = target[n]
        keys, values = whole_rows(n, own, first, far_keys, far_values, last)
        scores = dot(keys, by_head(arrived[t]), LAST) * SCALE
        top = jnp.max(scores, axis=0, keepdims=True)
        expo = jnp.exp(scores - top)
        total = jnp.sum(expo, axis=0, keepdims=True)
        prob = expo / total
        probs[n] = prob
        out = own_head(dot(prob.astype(BF), values, FIRST))
        write_slot(slots, t, out.astype(BF), top + jnp.log(total), 3)


def combine_kernel(source, arrived, d_mixed, gain, attended, shares, stats):
    stats[...] = jnp.zeros_like(stats)
    shares[...] = jnp.zeros_like(shares)
    width = attended.shape[1]
    for c in range(source.shape[0] // NEIGHBOURS):
        here = slice(c * GROUP_LEN, (c + 1) * GROUP_LEN)
        values, logs = zip(
            *[read_slot(arrived, source[NEIGHBOURS * c + k], width, 3) for k in range(NEIGHBOURS)]
        )
        top = jnp.maximum(logs[0], logs[1])
        expos = [jnp.exp(log - top) for log in logs]
        rest = 1.0 / (expos[0] + expos[1])
        out = jnp.zeros((GROUP_LEN, 2 * HEAD_DIM), F32)
        for k in range(NEIGHBOURS):
            share = expos[k] * rest
            shares[NEIGHBOURS * c + k : NEIGHBOURS * c + k + 1, :] = share
            column = as_column(share)
            value = values[k].astype(F32)
            out = out + jnp.concatenate(
                [
                    value[:, :HEAD_DIM] * column[:GROUP_LEN],
                    value[:, HEAD_DIM:] * column[GROUP_LEN:],
                ],
                axis=1,
            )
        attended[here, :] = out
        grad_in = d_mixed[here, :].astype(F32) * gain[...]
        column = jnp.concatenate(
            [
                jnp.sum(out * out, axis=1, keepdims=True),
                jnp.sum(grad_in * out, axis=1, keepdims=True),
            ],
            axis=0,
        )
        stats[c : c + 1, :] = as_row(column)


def grad_kernel(width, source, moved, attended, shares, d_mixed, gain, mixed, slots):
    total = jnp.sum(moved[...], axis=0)
    for c in range(source.shape[0] // NEIGHBOURS):
        here = slice(c * GROUP_LEN, (c + 1) * GROUP_LEN)
        column = as_column(total[c : c + 1, :])
        inverse = lax.rsqrt(column[:GROUP_LEN] / width + EPS)
        out = attended[here, :]
        grad_in = d_mixed[here, :].astype(F32) * gain[...]
        mixed[here, :] = (out * inverse * gain[...]).astype(BF)
        factor = column[GROUP_LEN:] * inverse * inverse / width
        grad = (inverse * (grad_in - out * factor)).astype(BF).astype(F32)
        inner = grad * out
        delta = jnp.concatenate(
            [
                jnp.sum(inner[:, :HEAD_DIM], axis=1, keepdims=True),
                jnp.sum(inner[:, HEAD_DIM:], axis=1, keepdims=True),
            ],
            axis=0,
        )
        for k in range(NEIGHBOURS):
            slot = source[NEIGHBOURS * c + k]
            share = as_column(shares[NEIGHBOURS * c + k : NEIGHBOURS * c + k + 1, :])
            scaled = jnp.concatenate(
                [grad[:, :HEAD_DIM] * share[:GROUP_LEN], grad[:, HEAD_DIM:] * share[GROUP_LEN:]],
                axis=1,
            )
            write_slot(slots, slot, scaled.astype(BF), as_row(delta * share), 2)


def owner_backward_kernel(target, arrived, queries, probs, *refs):
    kv_refs, (slots, own, down, up) = refs[:5], refs[5:]
    for n in range(target.shape[0]):
        t = target[n]
        keys, values = whole_rows(n, *kv_refs)
        block, delta = read_slot(arrived, t, keys.shape[1], 2)
        grad = by_head(block)
        query = by_head(queries[t])
        prob = probs[n]
        grad_scores = (prob * (dot(values, grad, LAST) - delta)).astype(BF)
        slots[t] = (own_head(dot(grad_scores, keys, FIRST)) * SCALE).astype(BF)
        grad_keys = (dot(grad_scores, query, PLAIN) * SCALE).astype(BF)
        grad_values = dot(prob.astype(BF), grad, PLAIN).astype(BF)
        rows = grad_keys.shape[0] // 4
        for i, grads in enumerate((grad_keys, grad_values)):
            own[n, i] = grads[:rows]
            down[n, i] = grads[rows : 2 * rows]
            (down, up)[i][n, 2] = grads[2 * rows : 3 * rows]
            up[n, i] = grads[3 * rows :]


def weight_kernel(sizes, place, source, arrived, mine, other, grad_q, partial):
    n_co, n_mp, n_x = sizes
    for c in range(source.shape[0] // NEIGHBOURS):
        both = sum(arrived[source[NEIGHBOURS * c + k]].astype(F32) for k in range(NEIGHBOURS))
        grad_q[c * GROUP_LEN : (c + 1) * GROUP_LEN, :] = both.astype(BF)
    rows = partial.shape[2]
    per = mine.shape[2] // rows
    for part, block in enumerate((mine, other)):
        co = lax.rem(place[1] + part, n_co)
        for line in range(mine.shape[0]):
            first = weight_rows(line, co, n_co, n_mp) * per
            product = dot(block[line], grad_q[...], FIRST).astype(BF)
            for i in range(per):
                partial[lax.rem(first + i, n_x), lax.div(first + i, n_x)] = product[
                    i * rows : (i + 1) * rows
                ]


def merge_kernel(place, own, first, far_keys, far_values, last, out):
    step = pl.program_id(0)

    @pl.when(step == 0)
    def _():
        out[...] = own[...]

    @pl.when(step == 1)
    def _():
        out[...] = first[:, :2]

    @pl.when(step == 2)
    def _():
        out[:, 0] = far_keys[...]
        out[:, 1] = far_values[...]

    @pl.when(step == 3)
    def _():
        out[...] = last[:, :2]


def split_by_quarter(place, kv):
    n, _, quarter, width = kv.shape
    part = width // 4
    take = [
        pl.BlockSpec((n, 2, quarter, part), functools.partial(block_at, d)) for d in range(4)
    ]
    shapes = [(n, 2, quarter, part), (n, 3, quarter, part), (n, 3, quarter, part)]
    return pl.pallas_call(
        split_kernel,
        grid_spec=pltpu.PrefetchScalarGridSpec(
            num_scalar_prefetch=1,
            grid=(1,),
            in_specs=take,
            out_specs=[pl.BlockSpec(shape, lambda i, place: (0, 0, 0, 0)) for shape in shapes],
        ),
        out_shape=[jax.ShapeDtypeStruct(shape, kv.dtype) for shape in shapes],
        compiler_params=PARAMS,
    )(place, kv, kv, kv, kv)


def block_at(d, i, place):
    return (0, 0, 0, lax.rem(place[0] + d, 4))


def merge_quarters(place, parts):
    n, _, quarter, part = parts[0].shape
    return pl.pallas_call(
        merge_kernel,
        grid_spec=pltpu.PrefetchScalarGridSpec(
            num_scalar_prefetch=1,
            grid=(4,),
            in_specs=[
                pl.BlockSpec(x.shape, functools.partial(origin, x.ndim)) for x in parts
            ],
            out_specs=pl.BlockSpec(
                (n, 2, quarter, part), lambda i, place: (0, 0, 0, lax.rem(place[0] + i, 4))
            ),
        ),
        out_shape=jax.ShapeDtypeStruct((n, 2, quarter, 4 * part), parts[0].dtype),
        compiler_params=PARAMS,
    )(place, *parts)


def origin(ndim, i, place):
    return (0,) * ndim


def shards(hidden, wq, kv_enc, group_neighbours, gain, d_mixed):
    n_z, n_x = lax.axis_size("dz"), lax.axis_size("dx")
    n_co, n_mp = lax.axis_size("co"), lax.axis_size("mp")
    n_dp = n_z * n_x
    heads = GRP + ("mp",)
    n_heads = lax.axis_size(heads)
    sizes = (n_co, n_mp, n_x)
    me_dp = lax.axis_index(DP)
    neigh_dev = kv_enc.shape[0]
    tok_dev, dec_width = hidden.shape[0], wq.shape[1]
    model = wq.shape[0] * n_dp
    gain = gain.reshape(1, dec_width)
    place = jnp.stack([lax.axis_index("mp"), lax.axis_index("co")]).astype(jnp.int32)
    flat_ids = group_neighbours.reshape(-1)
    slot_block = jnp.arange(flat_ids.shape[0], dtype=jnp.int32) // neigh_dev
    owned = me_dp * neigh_dev + jnp.arange(neigh_dev, dtype=jnp.int32)
    matches = flat_ids[None, :] == owned[:, None]
    target = jnp.sum(jnp.where(matches, slot_block[None, :], 0), axis=1)
    source = lax.dynamic_slice_in_dim(flat_ids, me_dp * neigh_dev, neigh_dev) // neigh_dev

    line = lax.all_gather(hidden, LINE, axis=0)
    own, up, down = split_by_quarter(place, kv_enc)
    first, last = shift(up, "mp", 1), shift(down, "mp", -1)
    near = exchange(copies(wq, n_z), "dz").reshape(n_z, -1, dec_width)
    near, first, last = lax.optimization_barrier((near, first, last))
    far_keys, far_values = shift(first[:, 2], "mp", 1), shift(last[:, 2], "mp", -1)
    weight = exchange(copies(near, n_x).reshape(n_x * n_z, -1, dec_width), "dx")
    weight = weight.reshape(n_x, n_z, -1, dec_width)
    line, weight, far_keys, far_values = lax.optimization_barrier(
        (line, weight, far_keys, far_values)
    )
    other = shift(line, "co", 1)
    kv = (own, first, far_keys, far_values, last)

    (slots,) = pl.pallas_call(
        functools.partial(query_kernel, sizes),
        in_specs=[SMEM, SMEM, VMEM, VMEM, VMEM],
        out_specs=[VMEM],
        out_shape=[jax.ShapeDtypeStruct((n_dp, GROUP_LEN, dec_width), BF)],
        scratch_shapes=[pltpu.VMEM((tok_dev, dec_width), F32)],
        compiler_params=PARAMS,
    )(place, source, line, other, weight)
    queries = exchange(slots, DP)

    wide = (n_dp, EXTRA, GROUP_LEN // EXTRA * dec_width + NEIGHBOURS * GROUP_LEN)
    span = kv_enc.shape[2] * n_mp
    slots, probs = call(
        owner_forward_kernel,
        (target,),
        (queries, *kv),
        [(wide, BF), ((neigh_dev, span, 2 * GROUP_LEN), F32)],
    )
    arrived = exchange(slots, DP)
    attended, shares, stats = call(
        combine_kernel,
        (source,),
        (arrived, d_mixed, gain),
        [((tok_dev, dec_width), F32), ((16, 128), F32), ((8, 128), F32)],
    )
    moved = exchange(copies(stats, n_heads), heads)
    mixed, slots = call(
        functools.partial(grad_kernel, model),
        (source,),
        (moved, attended, shares, d_mixed, gain),
        [((tok_dev, dec_width), BF), (wide, BF)],
    )
    arrived = exchange(slots, DP)
    slots, own, down, up = call(
        owner_backward_kernel,
        (target,),
        (arrived, queries, probs, *kv),
        [((n_dp, GROUP_LEN, dec_width), BF)] + [(x.shape, BF) for x in (own, first, last)],
    )
    first, last = shift(down, "mp", -1), shift(up, "mp", 1)
    arrived = exchange(slots, DP)
    arrived, first, last = lax.optimization_barrier((arrived, first, last))
    far_keys, far_values = shift(first[:, 2], "mp", -1), shift(last[:, 2], "mp", 1)
    grad_q, partial = call(
        functools.partial(weight_kernel, sizes),
        (place, source),
        (arrived, line, other),
        [((tok_dev, dec_width), BF), (weight.shape, BF)],
    )
    column = exchange(partial.reshape(n_x * n_z, -1, dec_width), "dx").reshape(weight.shape)
    column, far_keys, far_values = lax.optimization_barrier((column, far_keys, far_values))
    grad_kv = merge_quarters(place, (own, first, far_keys, far_values, last))
    column = jnp.sum(column, axis=0, dtype=F32).astype(BF)
    grad_wq = jnp.sum(exchange(column, "dz"), axis=0, dtype=F32).astype(BF)
    return (mixed, grad_q, grad_kv, grad_wq)


def solution(mesh):
    cut = Mesh(mesh.devices.reshape(2, 2, 8, 4, 4), GRP + DP + ("mp",))
    heads = GRP + ("mp",)
    placed = (P(DP, heads), P(DP, heads), P(DP, None, "mp", GRP), P(), P(heads), P(DP, heads))
    return jax.shard_map(
        shards,
        mesh=cut,
        in_specs=placed,
        out_specs=(P(DP, heads), P(DP, heads), P(DP, None, "mp", GRP), P(DP, heads)),
        check_vma=False,
    )
```

```python
import functools

import jax
import jax.numpy as jnp
from jax import lax
from jax.experimental import pallas as pl
from jax.experimental.pallas import tpu as pltpu
from jax.sharding import Mesh
from jax.sharding import PartitionSpec as P

GROUP_LEN = 64
NEIGHBOURS = 2
HEAD_DIM = 128
EXTRA = 16
EPS = 1e-06
SCALE = HEAD_DIM ** (-0.5)
DP = ("dz", "dx")
GRP = ("yl", "co")
LINE = ("mp", "yl")
BF = jnp.bfloat16
F32 = jnp.float32
SMEM = pl.BlockSpec(memory_space=pltpu.SMEM)
VMEM = pl.BlockSpec(memory_space=pltpu.VMEM)
PARAMS = pltpu.CompilerParams(vmem_limit_bytes=24 << 20)
LAST = (((1,), (1,)), ((), ()))
FIRST = (((0,), (0,)), ((), ()))
PLAIN = (((1,), (0,)), ((), ()))


def call(kernel, scalars, arrays, outs):
    return pl.pallas_call(
        kernel,
        in_specs=[SMEM] * len(scalars) + [VMEM] * len(arrays),
        out_specs=[VMEM] * len(outs),
        out_shape=[jax.ShapeDtypeStruct(shape, kind) for shape, kind in outs],
        compiler_params=PARAMS,
    )(*scalars, *arrays)


def exchange(array, axes):
    return lax.all_to_all(array, axes, split_axis=0, concat_axis=0, tiled=True)


def copies(array, count):
    return jnp.broadcast_to(array[None], (count,) + array.shape)


def shift(array, axis, step):
    size = lax.axis_size(axis)
    return lax.ppermute(array, axis, [(i, (i + step) % size) for i in range(size)])


def dot(a, b, dims):
    return lax.dot_general(a, b, dims, preferred_element_type=F32)


def eye(size):
    rows = lax.broadcasted_iota(jnp.int32, (size, size), 0)
    return rows == lax.broadcasted_iota(jnp.int32, (size, size), 1)


def as_column(row):
    return jnp.sum(jnp.where(eye(row.shape[1]), row, 0.0), axis=1, keepdims=True)


def as_row(column):
    return jnp.sum(jnp.where(eye(column.shape[0]), column, 0.0), axis=0, keepdims=True)


def by_head(block):
    blank = jnp.zeros((block.shape[0], HEAD_DIM), block.dtype)
    upper = jnp.concatenate([block[:, :HEAD_DIM], blank], axis=1)
    lower = jnp.concatenate([blank, block[:, HEAD_DIM:]], axis=1)
    return jnp.concatenate([upper, lower], axis=0)


def own_head(both):
    half = both.shape[0] // 2
    return jnp.concatenate([both[:half, :HEAD_DIM], both[half:, HEAD_DIM:]], axis=1)


def pieces(row, count):
    index = lax.broadcasted_iota(jnp.int32, (EXTRA, row.shape[1]), 0)
    tile = jnp.zeros((EXTRA, row.shape[1]), F32)
    rest = row
    for i in range(count):
        part = rest.astype(BF).astype(F32)
        tile = jnp.where(index == i, part, tile)
        rest = rest - part
    return tile.astype(BF)


def write_slot(slots, slot, block, row, count):
    width = block.shape[1]
    for i in range(GROUP_LEN // EXTRA):
        slots[slot, :, i * width : (i + 1) * width] = block[i * EXTRA : (i + 1) * EXTRA]
    slots[slot, :, GROUP_LEN // EXTRA * width :] = pieces(row, count)


def read_slot(slots, slot, width, count):
    folds = GROUP_LEN // EXTRA
    tile = slots[slot]
    block = jnp.concatenate([tile[:, i * width : (i + 1) * width] for i in range(folds)], axis=0)
    return block, joined(tile[:, folds * width :], count)


def joined(tile, count):
    tile = tile.astype(F32)
    index = lax.broadcasted_iota(jnp.int32, tile.shape, 0)
    return jnp.sum(jnp.where(index < count, tile, 0.0), axis=0, keepdims=True)


def split_kernel(place, block0, block1, block2, block3, own, up, down):
    own[...] = block0[...]
    up[:, :2] = block1[...]
    up[:, 2] = block2[:, 0]
    down[:, :2] = block3[...]
    down[:, 2] = block2[:, 1]


def whole_rows(n, own, first, far_keys, far_values, last):
    return [
        jnp.concatenate([own[n, i], first[n, i], far[n], last[n, i]], axis=0)
        for i, far in enumerate((far_keys, far_values))
    ]


def weight_rows(line, co, n_yl, n_co, n_mp):
    return (line % n_yl * n_co + co) * n_mp + line // n_yl


def query_kernel(sizes, place, source, mine, other, weight, slots, total):
    n_yl, n_co, n_mp, n_x = sizes
    rows = weight.shape[2]
    per = mine.shape[2] // rows
    for part, block in enumerate((mine, other)):
        co = lax.rem(place[1] + part, n_co)
        for line in range(mine.shape[0]):
            first = weight_rows(line, co, n_yl, n_co, n_mp) * per
            w = jnp.concatenate(
                [weight[lax.rem(first + i, n_x), lax.div(first + i, n_x)] for i in range(per)], axis=0
            )
            product = dot(block[line], w, PLAIN)
            if part == 0 and line == 0:
                total[...] = product
            else:
                total[...] += product
    for k in range(source.shape[0]):
        c = k // NEIGHBOURS
        slots[source[k]] = total[c * GROUP_LEN : (c + 1) * GROUP_LEN].astype(BF)


def owner_forward_kernel(target, arrived, own, first, far_keys, far_values, last, slots, probs):
    for n in range(target.shape[0]):
        t = target[n]
        keys, values = whole_rows(n, own, first, far_keys, far_values, last)
        scores = dot(keys, by_head(arrived[t]), LAST) * SCALE
        top = jnp.max(scores, axis=0, keepdims=True)
        expo = jnp.exp(scores - top)
        total = jnp.sum(expo, axis=0, keepdims=True)
        prob = expo / total
        probs[n] = prob
        out = own_head(dot(prob.astype(BF), values, FIRST))
        write_slot(slots, t, out.astype(BF), top + jnp.log(total), 3)


def combine_kernel(source, arrived, d_mixed, gain, attended, shares, stats):
    stats[...] = jnp.zeros_like(stats)
    shares[...] = jnp.zeros_like(shares)
    width = attended.shape[1]
    for c in range(source.shape[0] // NEIGHBOURS):
        here = slice(c * GROUP_LEN, (c + 1) * GROUP_LEN)
        values, logs = zip(
            *[read_slot(arrived, source[NEIGHBOURS * c + k], width, 3) for k in range(NEIGHBOURS)]
        )
        top = jnp.maximum(logs[0], logs[1])
        expos = [jnp.exp(log - top) for log in logs]
        rest = 1.0 / (expos[0] + expos[1])
        out = jnp.zeros((GROUP_LEN, 2 * HEAD_DIM), F32)
        for k in range(NEIGHBOURS):
            share = expos[k] * rest
            shares[NEIGHBOURS * c + k : NEIGHBOURS * c + k + 1, :] = share
            column = as_column(share)
            value = values[k].astype(F32)
            out = out + jnp.concatenate(
                [
                    value[:, :HEAD_DIM] * column[:GROUP_LEN],
                    value[:, HEAD_DIM:] * column[GROUP_LEN:],
                ],
                axis=1,
            )
        attended[here, :] = out
        grad_in = d_mixed[here, :].astype(F32) * gain[...]
        column = jnp.concatenate(
            [
                jnp.sum(out * out, axis=1, keepdims=True),
                jnp.sum(grad_in * out, axis=1, keepdims=True),
            ],
            axis=0,
        )
        stats[c : c + 1, :] = as_row(column)


def grad_kernel(width, source, moved, attended, shares, d_mixed, gain, mixed, slots):
    total = jnp.sum(moved[...], axis=0)
    for c in range(source.shape[0] // NEIGHBOURS):
        here = slice(c * GROUP_LEN, (c + 1) * GROUP_LEN)
        column = as_column(total[c : c + 1, :])
        inverse = lax.rsqrt(column[:GROUP_LEN] / width + EPS)
        out = attended[here, :]
        grad_in = d_mixed[here, :].astype(F32) * gain[...]
        mixed[here, :] = (out * inverse * gain[...]).astype(BF)
        factor = column[GROUP_LEN:] * inverse * inverse / width
        grad = (inverse * (grad_in - out * factor)).astype(BF).astype(F32)
        inner = grad * out
        delta = jnp.concatenate(
            [
                jnp.sum(inner[:, :HEAD_DIM], axis=1, keepdims=True),
                jnp.sum(inner[:, HEAD_DIM:], axis=1, keepdims=True),
            ],
            axis=0,
        )
        for k in range(NEIGHBOURS):
            slot = source[NEIGHBOURS * c + k]
            share = as_column(shares[NEIGHBOURS * c + k : NEIGHBOURS * c + k + 1, :])
            scaled = jnp.concatenate(
                [grad[:, :HEAD_DIM] * share[:GROUP_LEN], grad[:, HEAD_DIM:] * share[GROUP_LEN:]],
                axis=1,
            )
            write_slot(slots, slot, scaled.astype(BF), as_row(delta * share), 2)


def owner_backward_kernel(target, arrived, queries, probs, *refs):
    kv_refs, (slots, own, down, up) = refs[:5], refs[5:]
    for n in range(target.shape[0]):
        t = target[n]
        keys, values = whole_rows(n, *kv_refs)
        block, delta = read_slot(arrived, t, keys.shape[1], 2)
        grad = by_head(block)
        query = by_head(queries[t])
        prob = probs[n]
        grad_scores = (prob * (dot(values, grad, LAST) - delta)).astype(BF)
        slots[t] = (own_head(dot(grad_scores, keys, FIRST)) * SCALE).astype(BF)
        grad_keys = (dot(grad_scores, query, PLAIN) * SCALE).astype(BF)
        grad_values = dot(prob.astype(BF), grad, PLAIN).astype(BF)
        rows = grad_keys.shape[0] // 4
        for i, grads in enumerate((grad_keys, grad_values)):
            own[n, i] = grads[:rows]
            down[n, i] = grads[rows : 2 * rows]
            (down, up)[i][n, 2] = grads[2 * rows : 3 * rows]
            up[n, i] = grads[3 * rows :]


def weight_kernel(sizes, place, source, arrived, mine, other, grad_q, partial):
    n_yl, n_co, n_mp, n_x = sizes
    for c in range(source.shape[0] // NEIGHBOURS):
        both = sum(arrived[source[NEIGHBOURS * c + k]].astype(F32) for k in range(NEIGHBOURS))
        grad_q[c * GROUP_LEN : (c + 1) * GROUP_LEN, :] = both.astype(BF)
    rows = partial.shape[2]
    per = mine.shape[2] // rows
    for part, block in enumerate((mine, other)):
        co = lax.rem(place[1] + part, n_co)
        for line in range(mine.shape[0]):
            first = weight_rows(line, co, n_yl, n_co, n_mp) * per
            product = dot(block[line], grad_q[...], FIRST).astype(BF)
            for i in range(per):
                partial[lax.rem(first + i, n_x), lax.div(first + i, n_x)] = product[
                    i * rows : (i + 1) * rows
                ]


def merge_kernel(place, own, first, far_keys, far_values, last, out):
    step = pl.program_id(0)

    @pl.when(step == 0)
    def _():
        out[...] = own[...]

    @pl.when(step == 1)
    def _():
        out[...] = first[:, :2]

    @pl.when(step == 2)
    def _():
        out[:, 0] = far_keys[...]
        out[:, 1] = far_values[...]

    @pl.when(step == 3)
    def _():
        out[...] = last[:, :2]


def split_by_quarter(place, kv):
    n, _, quarter, width = kv.shape
    part = width // 4
    take = [
        pl.BlockSpec((n, 2, quarter, part), functools.partial(block_at, d)) for d in range(4)
    ]
    shapes = [(n, 2, quarter, part), (n, 3, quarter, part), (n, 3, quarter, part)]
    return pl.pallas_call(
        split_kernel,
        grid_spec=pltpu.PrefetchScalarGridSpec(
            num_scalar_prefetch=1,
            grid=(1,),
            in_specs=take,
            out_specs=[pl.BlockSpec(shape, lambda i, place: (0, 0, 0, 0)) for shape in shapes],
        ),
        out_shape=[jax.ShapeDtypeStruct(shape, kv.dtype) for shape in shapes],
        compiler_params=PARAMS,
    )(place, kv, kv, kv, kv)


def block_at(d, i, place):
    return (0, 0, 0, lax.rem(place[0] + d, 4))


def merge_quarters(place, parts):
    n, _, quarter, part = parts[0].shape
    return pl.pallas_call(
        merge_kernel,
        grid_spec=pltpu.PrefetchScalarGridSpec(
            num_scalar_prefetch=1,
            grid=(4,),
            in_specs=[
                pl.BlockSpec(x.shape, functools.partial(origin, x.ndim)) for x in parts
            ],
            out_specs=pl.BlockSpec(
                (n, 2, quarter, part), lambda i, place: (0, 0, 0, lax.rem(place[0] + i, 4))
            ),
        ),
        out_shape=jax.ShapeDtypeStruct((n, 2, quarter, 4 * part), parts[0].dtype),
        compiler_params=PARAMS,
    )(place, *parts)


def origin(ndim, i, place):
    return (0,) * ndim


def shards(hidden, wq, kv_enc, group_neighbours, gain, d_mixed):
    n_z, n_x = lax.axis_size("dz"), lax.axis_size("dx")
    n_co, n_mp = lax.axis_size("co"), lax.axis_size("mp")
    n_dp = n_z * n_x
    heads = GRP + ("mp",)
    n_heads = lax.axis_size(heads)
    sizes = (lax.axis_size("yl"), n_co, n_mp, n_x)
    me_dp = lax.axis_index(DP)
    neigh_dev = kv_enc.shape[0]
    tok_dev, dec_width = hidden.shape[0], wq.shape[1]
    model = wq.shape[0] * n_dp
    gain = gain.reshape(1, dec_width)
    place = jnp.stack([lax.axis_index("mp"), lax.axis_index("co")]).astype(jnp.int32)
    flat_ids = group_neighbours.reshape(-1)
    slot_block = jnp.arange(flat_ids.shape[0], dtype=jnp.int32) // neigh_dev
    owned = me_dp * neigh_dev + jnp.arange(neigh_dev, dtype=jnp.int32)
    matches = flat_ids[None, :] == owned[:, None]
    target = jnp.sum(jnp.where(matches, slot_block[None, :], 0), axis=1)
    source = lax.dynamic_slice_in_dim(flat_ids, me_dp * neigh_dev, neigh_dev) // neigh_dev

    line = lax.all_gather(hidden, LINE, axis=0)
    own, up, down = split_by_quarter(place, kv_enc)
    near = exchange(copies(wq, n_z), "dz").reshape(n_z, -1, dec_width)
    near, up, down = lax.optimization_barrier((near, up, down))
    first, last = shift(up, "mp", 1), shift(down, "mp", -1)
    weight = exchange(copies(near, n_x).reshape(n_x * n_z, -1, dec_width), "dx")
    weight = weight.reshape(n_x, n_z, -1, dec_width)
    line, weight, first, last = lax.optimization_barrier((line, weight, first, last))
    far_keys, far_values = shift(first[:, 2], "mp", 1), shift(last[:, 2], "mp", -1)
    other = shift(line, "co", 1)
    kv = (own, first, far_keys, far_values, last)

    (slots,) = pl.pallas_call(
        functools.partial(query_kernel, sizes),
        in_specs=[SMEM, SMEM, VMEM, VMEM, VMEM],
        out_specs=[VMEM],
        out_shape=[jax.ShapeDtypeStruct((n_dp, GROUP_LEN, dec_width), BF)],
        scratch_shapes=[pltpu.VMEM((tok_dev, dec_width), F32)],
        compiler_params=PARAMS,
    )(place, source, line, other, weight)
    queries = exchange(slots, DP)

    wide = (n_dp, EXTRA, GROUP_LEN // EXTRA * dec_width + NEIGHBOURS * GROUP_LEN)
    span = kv_enc.shape[2] * n_mp
    slots, probs = call(
        owner_forward_kernel,
        (target,),
        (queries, *kv),
        [(wide, BF), ((neigh_dev, span, 2 * GROUP_LEN), F32)],
    )
    arrived = exchange(slots, DP)
    attended, shares, stats = call(
        combine_kernel,
        (source,),
        (arrived, d_mixed, gain),
        [((tok_dev, dec_width), F32), ((16, 128), F32), ((8, 128), F32)],
    )
    moved = exchange(copies(stats, n_heads), heads)
    mixed, slots = call(
        functools.partial(grad_kernel, model),
        (source,),
        (moved, attended, shares, d_mixed, gain),
        [((tok_dev, dec_width), BF), (wide, BF)],
    )
    arrived = exchange(slots, DP)
    slots, own, down, up = call(
        owner_backward_kernel,
        (target,),
        (arrived, queries, probs, *kv),
        [((n_dp, GROUP_LEN, dec_width), BF)] + [(x.shape, BF) for x in (own, first, last)],
    )
    first, last = shift(down, "mp", -1), shift(up, "mp", 1)
    arrived = exchange(slots, DP)
    grad_q, partial = call(
        functools.partial(weight_kernel, sizes),
        (place, source),
        (arrived, line, other),
        [((tok_dev, dec_width), BF), (weight.shape, BF)],
    )
    partial, first, last = lax.optimization_barrier((partial, first, last))
    far_keys, far_values = shift(first[:, 2], "mp", -1), shift(last[:, 2], "mp", 1)
    column = exchange(partial.reshape(n_x * n_z, -1, dec_width), "dx").reshape(weight.shape)
    column, far_keys, far_values = lax.optimization_barrier((column, far_keys, far_values))
    grad_kv = merge_quarters(place, (own, first, far_keys, far_values, last))
    column = jnp.sum(column, axis=0, dtype=F32).astype(BF)
    grad_wq = jnp.sum(exchange(column, "dz"), axis=0, dtype=F32).astype(BF)
    return (mixed, grad_q, grad_kv, grad_wq)


def solution(mesh):
    cut = Mesh(mesh.devices.reshape(2, 2, 8, 4, 4), GRP + DP + ("mp",))
    heads = GRP + ("mp",)
    placed = (P(DP, heads), P(DP, heads), P(DP, None, "mp", GRP), P(), P(heads), P(DP, heads))
    return jax.shard_map(
        shards,
        mesh=cut,
        in_specs=placed,
        out_specs=(P(DP, heads), P(DP, heads), P(DP, None, "mp", GRP), P(DP, heads)),
        check_vma=False,
    )
```

```python
import functools

import jax
import jax.numpy as jnp
from jax import lax
from jax.experimental import pallas as pl
from jax.experimental.pallas import tpu as pltpu
from jax.sharding import Mesh
from jax.sharding import PartitionSpec as P

GROUP_LEN = 64
NEIGHBOURS = 2
HEAD_DIM = 128
EXTRA = 16
EPS = 1e-06
SCALE = HEAD_DIM ** (-0.5)
DP = ("dz", "dx")
GRP = ("yl", "co")
LINE = ("mp", "yl")
BF = jnp.bfloat16
F32 = jnp.float32
SMEM = pl.BlockSpec(memory_space=pltpu.SMEM)
VMEM = pl.BlockSpec(memory_space=pltpu.VMEM)
PARAMS = pltpu.CompilerParams(vmem_limit_bytes=24 << 20)
LAST = (((1,), (1,)), ((), ()))
FIRST = (((0,), (0,)), ((), ()))
PLAIN = (((1,), (0,)), ((), ()))


def call(kernel, scalars, arrays, outs):
    return pl.pallas_call(
        kernel,
        in_specs=[SMEM] * len(scalars) + [VMEM] * len(arrays),
        out_specs=[VMEM] * len(outs),
        out_shape=[jax.ShapeDtypeStruct(shape, kind) for shape, kind in outs],
        compiler_params=PARAMS,
    )(*scalars, *arrays)


def exchange(array, axes):
    return lax.all_to_all(array, axes, split_axis=0, concat_axis=0, tiled=True)


def copies(array, count):
    return jnp.broadcast_to(array[None], (count,) + array.shape)


def shift(array, axis, step):
    size = lax.axis_size(axis)
    return lax.ppermute(array, axis, [(i, (i + step) % size) for i in range(size)])


def dot(a, b, dims):
    return lax.dot_general(a, b, dims, preferred_element_type=F32)


def eye(size):
    rows = lax.broadcasted_iota(jnp.int32, (size, size), 0)
    return rows == lax.broadcasted_iota(jnp.int32, (size, size), 1)


def as_column(row):
    return jnp.sum(jnp.where(eye(row.shape[1]), row, 0.0), axis=1, keepdims=True)


def as_row(column):
    return jnp.sum(jnp.where(eye(column.shape[0]), column, 0.0), axis=0, keepdims=True)


def by_head(block):
    blank = jnp.zeros((block.shape[0], HEAD_DIM), block.dtype)
    upper = jnp.concatenate([block[:, :HEAD_DIM], blank], axis=1)
    lower = jnp.concatenate([blank, block[:, HEAD_DIM:]], axis=1)
    return jnp.concatenate([upper, lower], axis=0)


def own_head(both):
    half = both.shape[0] // 2
    return jnp.concatenate([both[:half, :HEAD_DIM], both[half:, HEAD_DIM:]], axis=1)


def pieces(row, count):
    index = lax.broadcasted_iota(jnp.int32, (EXTRA, row.shape[1]), 0)
    tile = jnp.zeros((EXTRA, row.shape[1]), F32)
    rest = row
    for i in range(count):
        part = rest.astype(BF).astype(F32)
        tile = jnp.where(index == i, part, tile)
        rest = rest - part
    return tile.astype(BF)


def write_slot(slots, slot, block, row, count):
    width = block.shape[1]
    for i in range(GROUP_LEN // EXTRA):
        slots[slot, :, i * width : (i + 1) * width] = block[i * EXTRA : (i + 1) * EXTRA]
    slots[slot, :, GROUP_LEN // EXTRA * width :] = pieces(row, count)


def read_slot(slots, slot, width, count):
    folds = GROUP_LEN // EXTRA
    tile = slots[slot]
    block = jnp.concatenate([tile[:, i * width : (i + 1) * width] for i in range(folds)], axis=0)
    return block, joined(tile[:, folds * width :], count)


def joined(tile, count):
    tile = tile.astype(F32)
    index = lax.broadcasted_iota(jnp.int32, tile.shape, 0)
    return jnp.sum(jnp.where(index < count, tile, 0.0), axis=0, keepdims=True)


def split_kernel(place, block0, block1, block2, block3, own, first, far_keys, far_values, last):
    own[...] = block0[...]
    first[...] = block1[...]
    far_keys[...] = block2[:, 0]
    far_values[...] = block2[:, 1]
    last[...] = block3[...]


def whole_rows(n, own, first, far_keys, far_values, last):
    return [
        jnp.concatenate([own[n, i], first[n, i], far[n], last[n, i]], axis=0)
        for i, far in enumerate((far_keys, far_values))
    ]


def weight_rows(line, co, n_yl, n_co, n_mp):
    return (line % n_yl * n_co + co) * n_mp + line // n_yl


def query_kernel(sizes, place, source, mine, other, weight, slots, total):
    n_yl, n_co, n_mp, n_x = sizes
    rows = weight.shape[2]
    per = mine.shape[2] // rows
    for part, block in enumerate((mine, other)):
        co = lax.rem(place[1] + part, n_co)
        for line in range(mine.shape[0]):
            first = weight_rows(line, co, n_yl, n_co, n_mp) * per
            w = jnp.concatenate(
                [weight[lax.rem(first + i, n_x), lax.div(first + i, n_x)] for i in range(per)], axis=0
            )
            product = dot(block[line], w, PLAIN)
            if part == 0 and line == 0:
                total[...] = product
            else:
                total[...] += product
    for k in range(source.shape[0]):
        c = k // NEIGHBOURS
        slots[source[k]] = total[c * GROUP_LEN : (c + 1) * GROUP_LEN].astype(BF)


def owner_forward_kernel(target, arrived, own, first, far_keys, far_values, last, slots, probs):
    for n in range(target.shape[0]):
        t = target[n]
        keys, values = whole_rows(n, own, first, far_keys, far_values, last)
        scores = dot(keys, by_head(arrived[t]), LAST) * SCALE
        top = jnp.max(scores, axis=0, keepdims=True)
        expo = jnp.exp(scores - top)
        total = jnp.sum(expo, axis=0, keepdims=True)
        prob = expo / total
        probs[n] = prob
        out = own_head(dot(prob.astype(BF), values, FIRST))
        write_slot(slots, t, out.astype(BF), top + jnp.log(total), 3)


def combine_kernel(source, arrived, d_mixed, gain, attended, shares, stats):
    stats[...] = jnp.zeros_like(stats)
    shares[...] = jnp.zeros_like(shares)
    width = attended.shape[1]
    for c in range(source.shape[0] // NEIGHBOURS):
        here = slice(c * GROUP_LEN, (c + 1) * GROUP_LEN)
        values, logs = zip(
            *[read_slot(arrived, source[NEIGHBOURS * c + k], width, 3) for k in range(NEIGHBOURS)]
        )
        top = jnp.maximum(logs[0], logs[1])
        expos = [jnp.exp(log - top) for log in logs]
        rest = 1.0 / (expos[0] + expos[1])
        out = jnp.zeros((GROUP_LEN, 2 * HEAD_DIM), F32)
        for k in range(NEIGHBOURS):
            share = expos[k] * rest
            shares[NEIGHBOURS * c + k : NEIGHBOURS * c + k + 1, :] = share
            column = as_column(share)
            value = values[k].astype(F32)
            out = out + jnp.concatenate(
                [
                    value[:, :HEAD_DIM] * column[:GROUP_LEN],
                    value[:, HEAD_DIM:] * column[GROUP_LEN:],
                ],
                axis=1,
            )
        attended[here, :] = out
        grad_in = d_mixed[here, :].astype(F32) * gain[...]
        column = jnp.concatenate(
            [
                jnp.sum(out * out, axis=1, keepdims=True),
                jnp.sum(grad_in * out, axis=1, keepdims=True),
            ],
            axis=0,
        )
        stats[c : c + 1, :] = as_row(column)


def grad_kernel(width, source, moved, attended, shares, d_mixed, gain, mixed, slots):
    total = jnp.sum(moved[...], axis=0)
    for c in range(source.shape[0] // NEIGHBOURS):
        here = slice(c * GROUP_LEN, (c + 1) * GROUP_LEN)
        column = as_column(total[c : c + 1, :])
        inverse = lax.rsqrt(column[:GROUP_LEN] / width + EPS)
        out = attended[here, :]
        grad_in = d_mixed[here, :].astype(F32) * gain[...]
        mixed[here, :] = (out * inverse * gain[...]).astype(BF)
        factor = column[GROUP_LEN:] * inverse * inverse / width
        grad = (inverse * (grad_in - out * factor)).astype(BF).astype(F32)
        inner = grad * out
        delta = jnp.concatenate(
            [
                jnp.sum(inner[:, :HEAD_DIM], axis=1, keepdims=True),
                jnp.sum(inner[:, HEAD_DIM:], axis=1, keepdims=True),
            ],
            axis=0,
        )
        for k in range(NEIGHBOURS):
            slot = source[NEIGHBOURS * c + k]
            share = as_column(shares[NEIGHBOURS * c + k : NEIGHBOURS * c + k + 1, :])
            scaled = jnp.concatenate(
                [grad[:, :HEAD_DIM] * share[:GROUP_LEN], grad[:, HEAD_DIM:] * share[GROUP_LEN:]],
                axis=1,
            )
            write_slot(slots, slot, scaled.astype(BF), as_row(delta * share), 2)


def owner_backward_kernel(target, arrived, queries, probs, *refs):
    kv_refs, (slots, own, first, far_keys, far_values, last) = refs[:5], refs[5:]
    for n in range(target.shape[0]):
        t = target[n]
        keys, values = whole_rows(n, *kv_refs)
        block, delta = read_slot(arrived, t, keys.shape[1], 2)
        grad = by_head(block)
        query = by_head(queries[t])
        prob = probs[n]
        grad_scores = (prob * (dot(values, grad, LAST) - delta)).astype(BF)
        slots[t] = (own_head(dot(grad_scores, keys, FIRST)) * SCALE).astype(BF)
        grad_keys = (dot(grad_scores, query, PLAIN) * SCALE).astype(BF)
        grad_values = dot(prob.astype(BF), grad, PLAIN).astype(BF)
        rows = grad_keys.shape[0] // 4
        for i, grads in enumerate((grad_keys, grad_values)):
            own[n, i] = grads[:rows]
            first[n, i] = grads[rows : 2 * rows]
            (far_keys, far_values)[i][n] = grads[2 * rows : 3 * rows]
            last[n, i] = grads[3 * rows :]


def weight_kernel(sizes, place, source, arrived, mine, other, grad_q, partial):
    n_yl, n_co, n_mp, n_x = sizes
    for c in range(source.shape[0] // NEIGHBOURS):
        both = sum(arrived[source[NEIGHBOURS * c + k]].astype(F32) for k in range(NEIGHBOURS))
        grad_q[c * GROUP_LEN : (c + 1) * GROUP_LEN, :] = both.astype(BF)
    rows = partial.shape[2]
    per = mine.shape[2] // rows
    for part, block in enumerate((mine, other)):
        co = lax.rem(place[1] + part, n_co)
        for line in range(mine.shape[0]):
            first = weight_rows(line, co, n_yl, n_co, n_mp) * per
            product = dot(block[line], grad_q[...], FIRST).astype(BF)
            for i in range(per):
                partial[lax.rem(first + i, n_x), lax.div(first + i, n_x)] = product[
                    i * rows : (i + 1) * rows
                ]


def merge_kernel(place, own, first, far_keys, far_values, last, out):
    step = pl.program_id(0)

    @pl.when(step == 0)
    def _():
        out[...] = own[...]

    @pl.when(step == 1)
    def _():
        out[...] = first[...]

    @pl.when(step == 2)
    def _():
        out[:, 0] = far_keys[...]
        out[:, 1] = far_values[...]

    @pl.when(step == 3)
    def _():
        out[...] = last[...]


def split_by_quarter(place, kv):
    n, _, quarter, width = kv.shape
    part = width // 4
    take = [
        pl.BlockSpec((n, 2, quarter, part), functools.partial(block_at, d)) for d in range(4)
    ]
    pair, single = (n, 2, quarter, part), (n, quarter, part)
    shapes = [pair, pair, single, single, pair]
    return pl.pallas_call(
        split_kernel,
        grid_spec=pltpu.PrefetchScalarGridSpec(
            num_scalar_prefetch=1,
            grid=(1,),
            in_specs=take,
            out_specs=[
                pl.BlockSpec(shape, functools.partial(origin, len(shape))) for shape in shapes
            ],
        ),
        out_shape=[jax.ShapeDtypeStruct(shape, kv.dtype) for shape in shapes],
        compiler_params=PARAMS,
    )(place, kv, kv, kv, kv)


def block_at(d, i, place):
    return (0, 0, 0, lax.rem(place[0] + d, 4))


def merge_quarters(place, parts):
    n, _, quarter, part = parts[0].shape
    return pl.pallas_call(
        merge_kernel,
        grid_spec=pltpu.PrefetchScalarGridSpec(
            num_scalar_prefetch=1,
            grid=(4,),
            in_specs=[
                pl.BlockSpec(x.shape, functools.partial(origin, x.ndim)) for x in parts
            ],
            out_specs=pl.BlockSpec(
                (n, 2, quarter, part), lambda i, place: (0, 0, 0, lax.rem(place[0] + i, 4))
            ),
        ),
        out_shape=jax.ShapeDtypeStruct((n, 2, quarter, 4 * part), parts[0].dtype),
        compiler_params=PARAMS,
    )(place, *parts)


def origin(ndim, i, place):
    return (0,) * ndim


def shards(hidden, wq, kv_enc, group_neighbours, gain, d_mixed):
    n_z, n_x = lax.axis_size("dz"), lax.axis_size("dx")
    n_co, n_mp = lax.axis_size("co"), lax.axis_size("mp")
    n_dp = n_z * n_x
    heads = GRP + ("mp",)
    n_heads = lax.axis_size(heads)
    sizes = (lax.axis_size("yl"), n_co, n_mp, n_x)
    me_dp = lax.axis_index(DP)
    neigh_dev = kv_enc.shape[0]
    tok_dev, dec_width = hidden.shape[0], wq.shape[1]
    model = wq.shape[0] * n_dp
    gain = gain.reshape(1, dec_width)
    place = jnp.stack([lax.axis_index("mp"), lax.axis_index("co")]).astype(jnp.int32)
    flat_ids = group_neighbours.reshape(-1)
    slot_block = jnp.arange(flat_ids.shape[0], dtype=jnp.int32) // neigh_dev
    owned = me_dp * neigh_dev + jnp.arange(neigh_dev, dtype=jnp.int32)
    matches = flat_ids[None, :] == owned[:, None]
    target = jnp.sum(jnp.where(matches, slot_block[None, :], 0), axis=1)
    source = lax.dynamic_slice_in_dim(flat_ids, me_dp * neigh_dev, neigh_dev) // neigh_dev

    line = lax.all_gather(hidden, LINE, axis=0)
    own, first, far_keys, far_values, last = split_by_quarter(place, kv_enc)
    near = exchange(copies(wq, n_z), "dz").reshape(n_z, -1, dec_width)
    near, far_keys, far_values = lax.optimization_barrier((near, far_keys, far_values))
    far_keys, far_values = shift(far_keys, "mp", 1), shift(far_values, "mp", -1)
    weight = exchange(copies(near, n_x).reshape(n_x * n_z, -1, dec_width), "dx")
    weight = weight.reshape(n_x, n_z, -1, dec_width)
    line, weight, far_keys, far_values, first, last = lax.optimization_barrier(
        (line, weight, far_keys, far_values, first, last)
    )
    other = shift(line, "co", 1)
    first, last = shift(first, "mp", 1), shift(last, "mp", -1)
    far_keys, far_values = shift(far_keys, "mp", 1), shift(far_values, "mp", -1)
    kv = (own, first, far_keys, far_values, last)

    (slots,) = pl.pallas_call(
        functools.partial(query_kernel, sizes),
        in_specs=[SMEM, SMEM, VMEM, VMEM, VMEM],
        out_specs=[VMEM],
        out_shape=[jax.ShapeDtypeStruct((n_dp, GROUP_LEN, dec_width), BF)],
        scratch_shapes=[pltpu.VMEM((tok_dev, dec_width), F32)],
        compiler_params=PARAMS,
    )(place, source, line, other, weight)
    queries = exchange(slots, DP)

    wide = (n_dp, EXTRA, GROUP_LEN // EXTRA * dec_width + NEIGHBOURS * GROUP_LEN)
    span = kv_enc.shape[2] * n_mp
    slots, probs = call(
        owner_forward_kernel,
        (target,),
        (queries, *kv),
        [(wide, BF), ((neigh_dev, span, 2 * GROUP_LEN), F32)],
    )
    arrived = exchange(slots, DP)
    attended, shares, stats = call(
        combine_kernel,
        (source,),
        (arrived, d_mixed, gain),
        [((tok_dev, dec_width), F32), ((16, 128), F32), ((8, 128), F32)],
    )
    moved = exchange(copies(stats, n_heads), heads)
    mixed, slots = call(
        functools.partial(grad_kernel, model),
        (source,),
        (moved, attended, shares, d_mixed, gain),
        [((tok_dev, dec_width), BF), (wide, BF)],
    )
    arrived = exchange(slots, DP)
    slots, own, first, far_keys, far_values, last = call(
        owner_backward_kernel,
        (target,),
        (arrived, queries, probs, *kv),
        [((n_dp, GROUP_LEN, dec_width), BF)] + [(x.shape, BF) for x in kv],
    )
    far_keys, far_values = shift(far_keys, "mp", -1), shift(far_values, "mp", 1)
    first, last = shift(first, "mp", -1), shift(last, "mp", 1)
    arrived = exchange(slots, DP)
    grad_q, partial = call(
        functools.partial(weight_kernel, sizes),
        (place, source),
        (arrived, line, other),
        [((tok_dev, dec_width), BF), (weight.shape, BF)],
    )
    partial, first, far_keys, far_values, last = lax.optimization_barrier(
        (partial, first, far_keys, far_values, last)
    )
    far_keys, far_values = shift(far_keys, "mp", -1), shift(far_values, "mp", 1)
    column = exchange(partial.reshape(n_x * n_z, -1, dec_width), "dx").reshape(weight.shape)
    column, far_keys, far_values = lax.optimization_barrier((column, far_keys, far_values))
    grad_kv = merge_quarters(place, (own, first, far_keys, far_values, last))
    column = jnp.sum(column, axis=0, dtype=F32).astype(BF)
    grad_wq = jnp.sum(exchange(column, "dz"), axis=0, dtype=F32).astype(BF)
    return (mixed, grad_q, grad_kv, grad_wq)


def solution(mesh):
    cut = Mesh(mesh.devices.reshape(2, 2, 8, 4, 4), GRP + DP + ("mp",))
    heads = GRP + ("mp",)
    placed = (P(DP, heads), P(DP, heads), P(DP, None, "mp", GRP), P(), P(heads), P(DP, heads))
    return jax.shard_map(
        shards,
        mesh=cut,
        in_specs=placed,
        out_specs=(P(DP, heads), P(DP, heads), P(DP, None, "mp", GRP), P(DP, heads)),
        check_vma=False,
    )
```

```python
import functools

import jax
import jax.numpy as jnp
from jax import lax
from jax.experimental import pallas as pl
from jax.experimental.pallas import tpu as pltpu
from jax.sharding import Mesh
from jax.sharding import PartitionSpec as P

GROUP_LEN = 64
NEIGHBOURS = 2
HEAD_DIM = 128
EXTRA = 16
EPS = 1e-06
SCALE = HEAD_DIM ** (-0.5)
DP = ("dz", "dx")
GRP = ("yl", "co")
LINE = ("mp", "yl")
BF = jnp.bfloat16
F32 = jnp.float32
SMEM = pl.BlockSpec(memory_space=pltpu.SMEM)
VMEM = pl.BlockSpec(memory_space=pltpu.VMEM)
PARAMS = pltpu.CompilerParams(vmem_limit_bytes=24 << 20)
LAST = (((1,), (1,)), ((), ()))
FIRST = (((0,), (0,)), ((), ()))
PLAIN = (((1,), (0,)), ((), ()))


def call(kernel, scalars, arrays, outs):
    return pl.pallas_call(
        kernel,
        in_specs=[SMEM] * len(scalars) + [VMEM] * len(arrays),
        out_specs=[VMEM] * len(outs),
        out_shape=[jax.ShapeDtypeStruct(shape, kind) for shape, kind in outs],
        compiler_params=PARAMS,
    )(*scalars, *arrays)


def exchange(array, axes):
    return lax.all_to_all(array, axes, split_axis=0, concat_axis=0, tiled=True)


def copies(array, count):
    return jnp.broadcast_to(array[None], (count,) + array.shape)


def shift(array, axis, step):
    size = lax.axis_size(axis)
    return lax.ppermute(array, axis, [(i, (i + step) % size) for i in range(size)])


def dot(a, b, dims):
    return lax.dot_general(a, b, dims, preferred_element_type=F32)


def eye(size):
    rows = lax.broadcasted_iota(jnp.int32, (size, size), 0)
    return rows == lax.broadcasted_iota(jnp.int32, (size, size), 1)


def as_column(row):
    return jnp.sum(jnp.where(eye(row.shape[1]), row, 0.0), axis=1, keepdims=True)


def as_row(column):
    return jnp.sum(jnp.where(eye(column.shape[0]), column, 0.0), axis=0, keepdims=True)


def by_head(block):
    blank = jnp.zeros((block.shape[0], HEAD_DIM), block.dtype)
    upper = jnp.concatenate([block[:, :HEAD_DIM], blank], axis=1)
    lower = jnp.concatenate([blank, block[:, HEAD_DIM:]], axis=1)
    return jnp.concatenate([upper, lower], axis=0)


def own_head(both):
    half = both.shape[0] // 2
    return jnp.concatenate([both[:half, :HEAD_DIM], both[half:, HEAD_DIM:]], axis=1)


def pieces(row, count):
    index = lax.broadcasted_iota(jnp.int32, (EXTRA, row.shape[1]), 0)
    tile = jnp.zeros((EXTRA, row.shape[1]), F32)
    rest = row
    for i in range(count):
        part = rest.astype(BF).astype(F32)
        tile = jnp.where(index == i, part, tile)
        rest = rest - part
    return tile.astype(BF)


def write_slot(slots, slot, block, row, count):
    width = block.shape[1]
    for i in range(GROUP_LEN // EXTRA):
        slots[slot, :, i * width : (i + 1) * width] = block[i * EXTRA : (i + 1) * EXTRA]
    slots[slot, :, GROUP_LEN // EXTRA * width :] = pieces(row, count)


def read_slot(slots, slot, width, count):
    folds = GROUP_LEN // EXTRA
    tile = slots[slot]
    block = jnp.concatenate([tile[:, i * width : (i + 1) * width] for i in range(folds)], axis=0)
    return block, joined(tile[:, folds * width :], count)


def joined(tile, count):
    tile = tile.astype(F32)
    index = lax.broadcasted_iota(jnp.int32, tile.shape, 0)
    return jnp.sum(jnp.where(index < count, tile, 0.0), axis=0, keepdims=True)


def split_kernel(place, block0, block1, block2, block3, own, up, down, first, last):
    own[...] = block0[...]
    up[:, 0] = block1[:, 0]
    up[:, 1] = block2[:, 0]
    down[:, 0] = block3[:, 0]
    down[:, 1] = block2[:, 1]
    first[...] = block1[:, 1]
    last[...] = block3[:, 1]


def whole_rows(n, own, up, down, far_up, far_down):
    return [
        jnp.concatenate([own[n, 0], up[n, 0], far_up[n, 1], down[n, 0]], axis=0),
        jnp.concatenate([own[n, 1], far_up[n, 0], far_down[n, 1], far_down[n, 0]], axis=0),
    ]


def second_step(first, arrived):
    return jnp.stack([first, arrived[:, 1]], axis=1)


def weight_rows(line, co, n_yl, n_co, n_mp):
    return (line % n_yl * n_co + co) * n_mp + line // n_yl


def query_kernel(sizes, place, source, mine, other, weight, slots, total):
    n_yl, n_co, n_mp, n_x = sizes
    span = mine.shape[2]
    for part, block in enumerate((mine, other)):
        co = lax.rem(place[1] + part, n_co)
        for line in range(mine.shape[0]):
            first = pl.multiple_of(weight_rows(line, co, n_yl, n_co, n_mp) * span, span)
            product = dot(block[line], weight[pl.ds(first, span), :], PLAIN)
            if part == 0 and line == 0:
                total[...] = product
            else:
                total[...] += product
    for k in range(source.shape[0]):
        c = k // NEIGHBOURS
        slots[source[k]] = total[c * GROUP_LEN : (c + 1) * GROUP_LEN].astype(BF)


def owner_forward_kernel(target, arrived, own, up, down, far_up, far_down, slots, probs):
    for n in range(target.shape[0]):
        t = target[n]
        keys, values = whole_rows(n, own, up, down, far_up, far_down)
        scores = dot(keys, by_head(arrived[t]), LAST) * SCALE
        top = jnp.max(scores, axis=0, keepdims=True)
        expo = jnp.exp(scores - top)
        total = jnp.sum(expo, axis=0, keepdims=True)
        prob = expo / total
        probs[n] = prob
        out = own_head(dot(prob.astype(BF), values, FIRST))
        write_slot(slots, t, out.astype(BF), top + jnp.log(total), 3)


def combine_kernel(source, arrived, d_mixed, gain, attended, shares, stats):
    stats[...] = jnp.zeros_like(stats)
    shares[...] = jnp.zeros_like(shares)
    width = attended.shape[1]
    for c in range(source.shape[0] // NEIGHBOURS):
        here = slice(c * GROUP_LEN, (c + 1) * GROUP_LEN)
        values, logs = zip(
            *[read_slot(arrived, source[NEIGHBOURS * c + k], width, 3) for k in range(NEIGHBOURS)]
        )
        top = jnp.maximum(logs[0], logs[1])
        expos = [jnp.exp(log - top) for log in logs]
        rest = 1.0 / (expos[0] + expos[1])
        out = jnp.zeros((GROUP_LEN, 2 * HEAD_DIM), F32)
        for k in range(NEIGHBOURS):
            share = expos[k] * rest
            shares[NEIGHBOURS * c + k : NEIGHBOURS * c + k + 1, :] = share
            column = as_column(share)
            value = values[k].astype(F32)
            out = out + jnp.concatenate(
                [
                    value[:, :HEAD_DIM] * column[:GROUP_LEN],
                    value[:, HEAD_DIM:] * column[GROUP_LEN:],
                ],
                axis=1,
            )
        attended[here, :] = out
        grad_in = d_mixed[here, :].astype(F32) * gain[...]
        column = jnp.concatenate(
            [
                jnp.sum(out * out, axis=1, keepdims=True),
                jnp.sum(grad_in * out, axis=1, keepdims=True),
            ],
            axis=0,
        )
        stats[c : c + 1, :] = as_row(column)


def grad_kernel(width, source, moved, attended, shares, d_mixed, gain, mixed, slots):
    total = jnp.sum(moved[...], axis=0)
    for c in range(source.shape[0] // NEIGHBOURS):
        here = slice(c * GROUP_LEN, (c + 1) * GROUP_LEN)
        column = as_column(total[c : c + 1, :])
        inverse = lax.rsqrt(column[:GROUP_LEN] / width + EPS)
        out = attended[here, :]
        grad_in = d_mixed[here, :].astype(F32) * gain[...]
        mixed[here, :] = (out * inverse * gain[...]).astype(BF)
        factor = column[GROUP_LEN:] * inverse * inverse / width
        grad = (inverse * (grad_in - out * factor)).astype(BF).astype(F32)
        inner = grad * out
        delta = jnp.concatenate(
            [
                jnp.sum(inner[:, :HEAD_DIM], axis=1, keepdims=True),
                jnp.sum(inner[:, HEAD_DIM:], axis=1, keepdims=True),
            ],
            axis=0,
        )
        for k in range(NEIGHBOURS):
            slot = source[NEIGHBOURS * c + k]
            share = as_column(shares[NEIGHBOURS * c + k : NEIGHBOURS * c + k + 1, :])
            scaled = jnp.concatenate(
                [grad[:, :HEAD_DIM] * share[:GROUP_LEN], grad[:, HEAD_DIM:] * share[GROUP_LEN:]],
                axis=1,
            )
            write_slot(slots, slot, scaled.astype(BF), as_row(delta * share), 2)


def owner_backward_kernel(target, arrived, queries, probs, *refs):
    kv_refs, (slots, own, up, down, first, last) = refs[:5], refs[5:]
    for n in range(target.shape[0]):
        t = target[n]
        keys, values = whole_rows(n, *kv_refs)
        block, delta = read_slot(arrived, t, keys.shape[1], 2)
        grad = by_head(block)
        query = by_head(queries[t])
        prob = probs[n]
        grad_scores = (prob * (dot(values, grad, LAST) - delta)).astype(BF)
        slots[t] = (own_head(dot(grad_scores, keys, FIRST)) * SCALE).astype(BF)
        grad_keys = (dot(grad_scores, query, PLAIN) * SCALE).astype(BF)
        grad_values = dot(prob.astype(BF), grad, PLAIN).astype(BF)
        rows = grad_keys.shape[0] // 4
        own[n, 0], own[n, 1] = grad_keys[:rows], grad_values[:rows]
        up[n, 0], first[n] = grad_keys[rows : 2 * rows], grad_values[rows : 2 * rows]
        up[n, 1], down[n, 1] = grad_keys[2 * rows : 3 * rows], grad_values[2 * rows : 3 * rows]
        down[n, 0], last[n] = grad_keys[3 * rows :], grad_values[3 * rows :]


def weight_kernel(sizes, place, source, arrived, mine, other, grad_q, partial):
    n_yl, n_co, n_mp, n_x = sizes
    for c in range(source.shape[0] // NEIGHBOURS):
        both = sum(arrived[source[NEIGHBOURS * c + k]].astype(F32) for k in range(NEIGHBOURS))
        grad_q[c * GROUP_LEN : (c + 1) * GROUP_LEN, :] = both.astype(BF)
    rows = partial.shape[2]
    per = mine.shape[2] // rows
    for part, block in enumerate((mine, other)):
        co = lax.rem(place[1] + part, n_co)
        for line in range(mine.shape[0]):
            first = weight_rows(line, co, n_yl, n_co, n_mp) * per
            product = dot(block[line], grad_q[...], FIRST).astype(BF)
            for i in range(per):
                partial[lax.rem(first + i, n_x), lax.div(first + i, n_x)] = product[
                    i * rows : (i + 1) * rows
                ]


def merge_kernel(place, own, up, down, far_up, far_down, out):
    step = pl.program_id(0)

    @pl.when(step == 0)
    def _():
        out[...] = own[...]

    @pl.when(step == 1)
    def _():
        out[:, 0] = up[:, 0]
        out[:, 1] = far_up[:, 0]

    @pl.when(step == 2)
    def _():
        out[:, 0] = far_up[:, 1]
        out[:, 1] = far_down[:, 1]

    @pl.when(step == 3)
    def _():
        out[:, 0] = down[:, 0]
        out[:, 1] = far_down[:, 0]


def split_by_quarter(place, kv):
    n, _, quarter, width = kv.shape
    part = width // 4
    take = [
        pl.BlockSpec((n, 2, quarter, part), functools.partial(block_at, d)) for d in range(4)
    ]
    pair, single = (n, 2, quarter, part), (n, quarter, part)
    shapes = [pair, pair, pair, single, single]
    return pl.pallas_call(
        split_kernel,
        grid_spec=pltpu.PrefetchScalarGridSpec(
            num_scalar_prefetch=1,
            grid=(1,),
            in_specs=take,
            out_specs=[
                pl.BlockSpec(shape, functools.partial(origin, len(shape))) for shape in shapes
            ],
        ),
        out_shape=[jax.ShapeDtypeStruct(shape, kv.dtype) for shape in shapes],
        compiler_params=PARAMS,
    )(place, kv, kv, kv, kv)


def block_at(d, i, place):
    return (0, 0, 0, lax.rem(place[0] + d, 4))


def merge_quarters(place, parts):
    n, _, quarter, part = parts[0].shape
    return pl.pallas_call(
        merge_kernel,
        grid_spec=pltpu.PrefetchScalarGridSpec(
            num_scalar_prefetch=1,
            grid=(4,),
            in_specs=[
                pl.BlockSpec(x.shape, functools.partial(origin, x.ndim)) for x in parts
            ],
            out_specs=pl.BlockSpec(
                (n, 2, quarter, part), lambda i, place: (0, 0, 0, lax.rem(place[0] + i, 4))
            ),
        ),
        out_shape=jax.ShapeDtypeStruct((n, 2, quarter, 4 * part), parts[0].dtype),
        compiler_params=PARAMS,
    )(place, *parts)


def origin(ndim, i, place):
    return (0,) * ndim


def shards(hidden, wq, kv_enc, group_neighbours, gain, d_mixed):
    n_z, n_x = lax.axis_size("dz"), lax.axis_size("dx")
    n_co, n_mp = lax.axis_size("co"), lax.axis_size("mp")
    n_dp = n_z * n_x
    heads = GRP + ("mp",)
    n_heads = lax.axis_size(heads)
    sizes = (lax.axis_size("yl"), n_co, n_mp, n_x)
    me_dp = lax.axis_index(DP)
    neigh_dev = kv_enc.shape[0]
    tok_dev, dec_width = hidden.shape[0], wq.shape[1]
    model = wq.shape[0] * n_dp
    gain = gain.reshape(1, dec_width)
    place = jnp.stack([lax.axis_index("mp"), lax.axis_index("co")]).astype(jnp.int32)
    flat_ids = group_neighbours.reshape(-1)
    slot_block = jnp.arange(flat_ids.shape[0], dtype=jnp.int32) // neigh_dev
    owned = me_dp * neigh_dev + jnp.arange(neigh_dev, dtype=jnp.int32)
    matches = flat_ids[None, :] == owned[:, None]
    target = jnp.sum(jnp.where(matches, slot_block[None, :], 0), axis=1)
    source = lax.dynamic_slice_in_dim(flat_ids, me_dp * neigh_dev, neigh_dev) // neigh_dev

    line = lax.all_gather(hidden, LINE, axis=0)
    own, up, down, first, last = split_by_quarter(place, kv_enc)
    weight = exchange(copies(wq, n_dp), DP).reshape(-1, dec_width)
    up, down = shift(up, "mp", 1), shift(down, "mp", -1)
    line, up, down = lax.optimization_barrier((line, up, down))
    other = shift(line, "co", 1)
    far_up = shift(second_step(first, up), "mp", 1)
    far_down = shift(second_step(last, down), "mp", -1)
    kv = (own, up, down, far_up, far_down)

    (slots,) = pl.pallas_call(
        functools.partial(query_kernel, sizes),
        in_specs=[SMEM, SMEM, VMEM, VMEM, VMEM],
        out_specs=[VMEM],
        out_shape=[jax.ShapeDtypeStruct((n_dp, GROUP_LEN, dec_width), BF)],
        scratch_shapes=[pltpu.VMEM((tok_dev, dec_width), F32)],
        compiler_params=PARAMS,
    )(place, source, line, other, weight)
    queries = exchange(slots, DP)

    wide = (n_dp, EXTRA, GROUP_LEN // EXTRA * dec_width + NEIGHBOURS * GROUP_LEN)
    span = kv_enc.shape[2] * n_mp
    slots, probs = call(
        owner_forward_kernel,
        (target,),
        (queries, *kv),
        [(wide, BF), ((neigh_dev, span, 2 * GROUP_LEN), F32)],
    )
    arrived = exchange(slots, DP)
    attended, shares, stats = call(
        combine_kernel,
        (source,),
        (arrived, d_mixed, gain),
        [((tok_dev, dec_width), F32), ((16, 128), F32), ((8, 128), F32)],
    )
    moved = exchange(copies(stats, n_heads), heads)
    mixed, slots = call(
        functools.partial(grad_kernel, model),
        (source,),
        (moved, attended, shares, d_mixed, gain),
        [((tok_dev, dec_width), BF), (wide, BF)],
    )
    arrived = exchange(slots, DP)
    slots, own, up, down, first, last = call(
        owner_backward_kernel,
        (target,),
        (arrived, queries, probs, *kv),
        [((n_dp, GROUP_LEN, dec_width), BF)]
        + [(x.shape, BF) for x in (own, up, down, first, last)],
    )
    up, down = shift(up, "mp", -1), shift(down, "mp", 1)
    arrived = exchange(slots, DP)
    blocks = (n_x, n_z, wq.shape[0], dec_width)
    grad_q, partial = call(
        functools.partial(weight_kernel, sizes),
        (place, source),
        (arrived, line, other),
        [((tok_dev, dec_width), BF), (blocks, BF)],
    )
    partial, up, down = lax.optimization_barrier((partial, up, down))
    far_up = shift(second_step(first, up), "mp", -1)
    far_down = shift(second_step(last, down), "mp", 1)
    column = exchange(partial.reshape(n_x * n_z, -1, dec_width), "dx").reshape(blocks)
    column, far_up, far_down = lax.optimization_barrier((column, far_up, far_down))
    grad_kv = merge_quarters(place, (own, up, down, far_up, far_down))
    column = jnp.sum(column, axis=0, dtype=F32).astype(BF)
    grad_wq = jnp.sum(exchange(column, "dz"), axis=0, dtype=F32).astype(BF)
    return (mixed, grad_q, grad_kv, grad_wq)


def solution(mesh):
    cut = Mesh(mesh.devices.reshape(2, 2, 8, 4, 4), GRP + DP + ("mp",))
    heads = GRP + ("mp",)
    placed = (P(DP, heads), P(DP, heads), P(DP, None, "mp", GRP), P(), P(heads), P(DP, heads))
    return jax.shard_map(
        shards,
        mesh=cut,
        in_specs=placed,
        out_specs=(P(DP, heads), P(DP, heads), P(DP, None, "mp", GRP), P(DP, heads)),
        check_vma=False,
    )
```

```python
import functools

import jax
import jax.numpy as jnp
from jax import lax
from jax.experimental import pallas as pl
from jax.experimental.pallas import tpu as pltpu
from jax.sharding import Mesh
from jax.sharding import PartitionSpec as P

GROUP_LEN = 64
NEIGHBOURS = 2
HEAD_DIM = 128
EXTRA = 16
EPS = 1e-06
SCALE = HEAD_DIM ** (-0.5)
DP = ("dz", "dx")
GRP = ("yl", "co")
LINE = ("mp", "yl")
BF = jnp.bfloat16
F32 = jnp.float32
SMEM = pl.BlockSpec(memory_space=pltpu.SMEM)
VMEM = pl.BlockSpec(memory_space=pltpu.VMEM)
PARAMS = pltpu.CompilerParams(vmem_limit_bytes=24 << 20)
LAST = (((1,), (1,)), ((), ()))
FIRST = (((0,), (0,)), ((), ()))
PLAIN = (((1,), (0,)), ((), ()))


def call(kernel, scalars, arrays, outs, params=PARAMS):
    return pl.pallas_call(
        kernel,
        in_specs=[SMEM] * len(scalars) + [VMEM] * len(arrays),
        out_specs=[VMEM] * len(outs),
        out_shape=[jax.ShapeDtypeStruct(shape, kind) for shape, kind in outs],
        compiler_params=params,
    )(*scalars, *arrays)


def exchange(array, axes):
    return lax.all_to_all(array, axes, split_axis=0, concat_axis=0, tiled=True)


def copies(array, count):
    return jnp.broadcast_to(array[None], (count,) + array.shape)


def shift(array, axis, step):
    size = lax.axis_size(axis)
    return lax.ppermute(array, axis, [(i, (i + step) % size) for i in range(size)])


def dot(a, b, dims):
    return lax.dot_general(a, b, dims, preferred_element_type=F32)


def eye(size):
    rows = lax.broadcasted_iota(jnp.int32, (size, size), 0)
    return rows == lax.broadcasted_iota(jnp.int32, (size, size), 1)


def as_column(row):
    return jnp.sum(jnp.where(eye(row.shape[1]), row, 0.0), axis=1, keepdims=True)


def as_row(column):
    return jnp.sum(jnp.where(eye(column.shape[0]), column, 0.0), axis=0, keepdims=True)


def by_head(block):
    blank = jnp.zeros((block.shape[0], HEAD_DIM), block.dtype)
    upper = jnp.concatenate([block[:, :HEAD_DIM], blank], axis=1)
    lower = jnp.concatenate([blank, block[:, HEAD_DIM:]], axis=1)
    return jnp.concatenate([upper, lower], axis=0)


def own_head(both):
    half = both.shape[0] // 2
    return jnp.concatenate([both[:half, :HEAD_DIM], both[half:, HEAD_DIM:]], axis=1)


def pieces(row, count):
    index = lax.broadcasted_iota(jnp.int32, (EXTRA, row.shape[1]), 0)
    tile = jnp.zeros((EXTRA, row.shape[1]), F32)
    rest = row
    for i in range(count):
        part = rest.astype(BF).astype(F32)
        tile = jnp.where(index == i, part, tile)
        rest = rest - part
    return tile.astype(BF)


def write_slot(slots, slot, block, row, count):
    width = block.shape[1]
    for i in range(GROUP_LEN // EXTRA):
        slots[slot, :, i * width : (i + 1) * width] = block[i * EXTRA : (i + 1) * EXTRA]
    slots[slot, :, GROUP_LEN // EXTRA * width :] = pieces(row, count)


def read_slot(slots, slot, width, count):
    folds = GROUP_LEN // EXTRA
    tile = slots[slot]
    block = jnp.concatenate([tile[:, i * width : (i + 1) * width] for i in range(folds)], axis=0)
    return block, joined(tile[:, folds * width :], count)


def joined(tile, count):
    tile = tile.astype(F32)
    index = lax.broadcasted_iota(jnp.int32, tile.shape, 0)
    return jnp.sum(jnp.where(index < count, tile, 0.0), axis=0, keepdims=True)


def split_kernel(place, block0, block1, block2, block3, own, first, last, far_keys, far_values):
    own[...] = block0[...]
    first[...] = block1[...]
    last[...] = block3[...]
    far_keys[...] = block2[:, 0]
    far_values[...] = block2[:, 1]


def whole_rows(n, own, up, down):
    return [
        jnp.concatenate([own[n, 0], up[n, 0], up[n, 2], down[n, 0]], axis=0),
        jnp.concatenate([own[n, 1], up[n, 1], down[n, 2], down[n, 1]], axis=0),
    ]


def second_step(first, arrived):
    return jnp.stack([first, arrived[:, 1]], axis=1)


def weight_rows(line, co, n_yl, n_co, n_mp):
    return (line % n_yl * n_co + co) * n_mp + line // n_yl


def query_kernel(sizes, place, source, mine, other, weight, slots, total):
    n_yl, n_co, n_mp, n_x = sizes
    span = mine.shape[2]
    for part, block in enumerate((mine, other)):
        co = lax.rem(place[1] + part, n_co)
        for line in range(mine.shape[0]):
            first = pl.multiple_of(weight_rows(line, co, n_yl, n_co, n_mp) * span, span)
            product = dot(block[line], weight[pl.ds(first, span), :], PLAIN)
            if part == 0 and line == 0:
                total[...] = product
            else:
                total[...] += product
    for k in range(source.shape[0]):
        c = k // NEIGHBOURS
        slots[source[k]] = total[c * GROUP_LEN : (c + 1) * GROUP_LEN].astype(BF)


def owner_forward_kernel(target, arrived, own, up, down, slots, probs):
    for n in range(target.shape[0]):
        t = target[n]
        keys, values = whole_rows(n, own, up, down)
        scores = dot(keys, by_head(arrived[t]), LAST) * SCALE
        top = jnp.max(scores, axis=0, keepdims=True)
        expo = jnp.exp(scores - top)
        total = jnp.sum(expo, axis=0, keepdims=True)
        prob = expo / total
        probs[n] = prob
        out = own_head(dot(prob.astype(BF), values, FIRST))
        write_slot(slots, t, out.astype(BF), top + jnp.log(total), 3)


def combine_kernel(source, arrived, d_mixed, gain, attended, shares, stats):
    stats[...] = jnp.zeros_like(stats)
    shares[...] = jnp.zeros_like(shares)
    width = attended.shape[1]
    for c in range(source.shape[0] // NEIGHBOURS):
        here = slice(c * GROUP_LEN, (c + 1) * GROUP_LEN)
        values, logs = zip(
            *[read_slot(arrived, source[NEIGHBOURS * c + k], width, 3) for k in range(NEIGHBOURS)]
        )
        top = jnp.maximum(logs[0], logs[1])
        expos = [jnp.exp(log - top) for log in logs]
        rest = 1.0 / (expos[0] + expos[1])
        out = jnp.zeros((GROUP_LEN, 2 * HEAD_DIM), F32)
        for k in range(NEIGHBOURS):
            share = expos[k] * rest
            shares[NEIGHBOURS * c + k : NEIGHBOURS * c + k + 1, :] = share
            column = as_column(share)
            value = values[k].astype(F32)
            out = out + jnp.concatenate(
                [
                    value[:, :HEAD_DIM] * column[:GROUP_LEN],
                    value[:, HEAD_DIM:] * column[GROUP_LEN:],
                ],
                axis=1,
            )
        attended[here, :] = out
        grad_in = d_mixed[here, :].astype(F32) * gain[...]
        column = jnp.concatenate(
            [
                jnp.sum(out * out, axis=1, keepdims=True),
                jnp.sum(grad_in * out, axis=1, keepdims=True),
            ],
            axis=0,
        )
        stats[c : c + 1, :] = as_row(column)


def grad_kernel(width, source, moved, attended, shares, d_mixed, gain, mixed, slots):
    total = jnp.sum(moved[...], axis=0)
    for c in range(source.shape[0] // NEIGHBOURS):
        here = slice(c * GROUP_LEN, (c + 1) * GROUP_LEN)
        column = as_column(total[c : c + 1, :])
        inverse = lax.rsqrt(column[:GROUP_LEN] / width + EPS)
        out = attended[here, :]
        grad_in = d_mixed[here, :].astype(F32) * gain[...]
        mixed[here, :] = (out * inverse * gain[...]).astype(BF)
        factor = column[GROUP_LEN:] * inverse * inverse / width
        grad = (inverse * (grad_in - out * factor)).astype(BF).astype(F32)
        inner = grad * out
        delta = jnp.concatenate(
            [
                jnp.sum(inner[:, :HEAD_DIM], axis=1, keepdims=True),
                jnp.sum(inner[:, HEAD_DIM:], axis=1, keepdims=True),
            ],
            axis=0,
        )
        for k in range(NEIGHBOURS):
            slot = source[NEIGHBOURS * c + k]
            share = as_column(shares[NEIGHBOURS * c + k : NEIGHBOURS * c + k + 1, :])
            scaled = jnp.concatenate(
                [grad[:, :HEAD_DIM] * share[:GROUP_LEN], grad[:, HEAD_DIM:] * share[GROUP_LEN:]],
                axis=1,
            )
            write_slot(slots, slot, scaled.astype(BF), as_row(delta * share), 2)


def owner_backward_kernel(target, arrived, queries, probs, *refs):
    kv_refs, (slots, own, up, down, first, last) = refs[:3], refs[3:]
    for n in range(target.shape[0]):
        t = target[n]
        keys, values = whole_rows(n, *kv_refs)
        block, delta = read_slot(arrived, t, keys.shape[1], 2)
        grad = by_head(block)
        query = by_head(queries[t])
        prob = probs[n]
        grad_scores = (prob * (dot(values, grad, LAST) - delta)).astype(BF)
        slots[t] = (own_head(dot(grad_scores, keys, FIRST)) * SCALE).astype(BF)
        grad_keys = (dot(grad_scores, query, PLAIN) * SCALE).astype(BF)
        grad_values = dot(prob.astype(BF), grad, PLAIN).astype(BF)
        rows = grad_keys.shape[0] // 4
        own[n, 0], own[n, 1] = grad_keys[:rows], grad_values[:rows]
        up[n, 0], first[n] = grad_keys[rows : 2 * rows], grad_values[rows : 2 * rows]
        up[n, 1], down[n, 1] = grad_keys[2 * rows : 3 * rows], grad_values[2 * rows : 3 * rows]
        down[n, 0], last[n] = grad_keys[3 * rows :], grad_values[3 * rows :]


def weight_kernel(sizes, place, source, arrived, mine, other, grad_q, partial):
    n_yl, n_co, n_mp, n_x = sizes
    for c in range(source.shape[0] // NEIGHBOURS):
        both = sum(arrived[source[NEIGHBOURS * c + k]].astype(F32) for k in range(NEIGHBOURS))
        grad_q[c * GROUP_LEN : (c + 1) * GROUP_LEN, :] = both.astype(BF)
    rows = partial.shape[2]
    per = mine.shape[2] // rows
    for part, block in enumerate((mine, other)):
        co = lax.rem(place[1] + part, n_co)
        for line in range(mine.shape[0]):
            first = weight_rows(line, co, n_yl, n_co, n_mp) * per
            product = dot(block[line], grad_q[...], FIRST).astype(BF)
            for i in range(per):
                partial[lax.rem(first + i, n_x), lax.div(first + i, n_x)] = product[
                    i * rows : (i + 1) * rows
                ]


def merge_kernel(place, own, up, down, far_up, far_down, out):
    step = pl.program_id(0)

    @pl.when(step == 0)
    def _():
        out[...] = own[...]

    @pl.when(step == 1)
    def _():
        out[:, 0] = up[:, 0]
        out[:, 1] = far_up[:, 0]

    @pl.when(step == 2)
    def _():
        out[:, 0] = far_up[:, 1]
        out[:, 1] = far_down[:, 1]

    @pl.when(step == 3)
    def _():
        out[:, 0] = down[:, 0]
        out[:, 1] = far_down[:, 0]


def split_by_quarter(place, kv):
    n, _, quarter, width = kv.shape
    part = width // 4
    take = [
        pl.BlockSpec((n, 2, quarter, part), functools.partial(block_at, d)) for d in range(4)
    ]
    pair, single = (n, 2, quarter, part), (n, quarter, part)
    shapes = [pair, pair, pair, single, single]
    return pl.pallas_call(
        split_kernel,
        grid_spec=pltpu.PrefetchScalarGridSpec(
            num_scalar_prefetch=1,
            grid=(1,),
            in_specs=take,
            out_specs=[
                pl.BlockSpec(shape, functools.partial(origin, len(shape))) for shape in shapes
            ],
        ),
        out_shape=[jax.ShapeDtypeStruct(shape, kv.dtype) for shape in shapes],
        compiler_params=PARAMS,
    )(place, kv, kv, kv, kv)


def block_at(d, i, place):
    return (0, 0, 0, lax.rem(place[0] + d, 4))


def merge_quarters(place, parts):
    n, _, quarter, part = parts[0].shape
    return pl.pallas_call(
        merge_kernel,
        grid_spec=pltpu.PrefetchScalarGridSpec(
            num_scalar_prefetch=1,
            grid=(4,),
            in_specs=[
                pl.BlockSpec(x.shape, functools.partial(origin, x.ndim)) for x in parts
            ],
            out_specs=pl.BlockSpec(
                (n, 2, quarter, part), lambda i, place: (0, 0, 0, lax.rem(place[0] + i, 4))
            ),
        ),
        out_shape=jax.ShapeDtypeStruct((n, 2, quarter, 4 * part), parts[0].dtype),
        compiler_params=PARAMS,
    )(place, *parts)


def origin(ndim, i, place):
    return (0,) * ndim


def shards(hidden, wq, kv_enc, group_neighbours, gain, d_mixed):
    n_z, n_x = lax.axis_size("dz"), lax.axis_size("dx")
    n_co, n_mp = lax.axis_size("co"), lax.axis_size("mp")
    n_dp = n_z * n_x
    heads = GRP + ("mp",)
    n_heads = lax.axis_size(heads)
    sizes = (lax.axis_size("yl"), n_co, n_mp, n_x)
    me_dp = lax.axis_index(DP)
    neigh_dev = kv_enc.shape[0]
    tok_dev, dec_width = hidden.shape[0], wq.shape[1]
    model = wq.shape[0] * n_dp
    gain = gain.reshape(1, dec_width)
    place = jnp.stack([lax.axis_index("mp"), lax.axis_index("co")]).astype(jnp.int32)
    flat_ids = group_neighbours.reshape(-1)
    slot_block = jnp.arange(flat_ids.shape[0], dtype=jnp.int32) // neigh_dev
    owned = me_dp * neigh_dev + jnp.arange(neigh_dev, dtype=jnp.int32)
    matches = flat_ids[None, :] == owned[:, None]
    target = jnp.sum(jnp.where(matches, slot_block[None, :], 0), axis=1)
    source = lax.dynamic_slice_in_dim(flat_ids, me_dp * neigh_dev, neigh_dev) // neigh_dev

    line = lax.all_gather(hidden, LINE, axis=0)
    own, first, last, far_keys, far_values = split_by_quarter(place, kv_enc)
    weight = exchange(copies(wq, n_dp), DP).reshape(-1, dec_width)
    up = jnp.concatenate([first, shift(far_keys, "mp", 1)[:, None]], axis=1)
    down = jnp.concatenate([last, shift(far_values, "mp", -1)[:, None]], axis=1)
    line, up, down = lax.optimization_barrier((line, up, down))
    other = shift(line, "co", 1)
    kv = (own, shift(up, "mp", 1), shift(down, "mp", -1))

    (slots,) = pl.pallas_call(
        functools.partial(query_kernel, sizes),
        in_specs=[SMEM, SMEM, VMEM, VMEM, VMEM],
        out_specs=[VMEM],
        out_shape=[jax.ShapeDtypeStruct((n_dp, GROUP_LEN, dec_width), BF)],
        scratch_shapes=[pltpu.VMEM((tok_dev, dec_width), F32)],
        compiler_params=PARAMS,
    )(place, source, line, other, weight)
    queries = exchange(slots, DP)

    wide = (n_dp, EXTRA, GROUP_LEN // EXTRA * dec_width + NEIGHBOURS * GROUP_LEN)
    span = kv_enc.shape[2] * n_mp
    slots, probs = call(
        owner_forward_kernel,
        (target,),
        (queries, *kv),
        [(wide, BF), ((neigh_dev, span, 2 * GROUP_LEN), F32)],
    )
    arrived = exchange(slots, DP)
    attended, shares, stats = call(
        combine_kernel,
        (source,),
        (arrived, d_mixed, gain),
        [((tok_dev, dec_width), F32), ((16, 128), F32), ((8, 128), F32)],
    )
    moved = exchange(copies(stats, n_heads), heads)
    mixed, slots = call(
        functools.partial(grad_kernel, model),
        (source,),
        (moved, attended, shares, d_mixed, gain),
        [((tok_dev, dec_width), BF), (wide, BF)],
    )
    arrived = exchange(slots, DP)
    slots, own, up, down, first, last = call(
        owner_backward_kernel,
        (target,),
        (arrived, queries, probs, *kv),
        [((n_dp, GROUP_LEN, dec_width), BF)]
        + [(own.shape, BF)] * 3
        + [(far_keys.shape, BF)] * 2,
        pltpu.CompilerParams(vmem_limit_bytes=60 << 20),
    )
    up, down = shift(up, "mp", -1), shift(down, "mp", 1)
    arrived = exchange(slots, DP)
    blocks = (n_x, n_z, wq.shape[0], dec_width)
    grad_q, partial = call(
        functools.partial(weight_kernel, sizes),
        (place, source),
        (arrived, line, other),
        [((tok_dev, dec_width), BF), (blocks, BF)],
    )
    partial, up, down = lax.optimization_barrier((partial, up, down))
    far_up = shift(second_step(first, up), "mp", -1)
    far_down = shift(second_step(last, down), "mp", 1)
    column = exchange(partial.reshape(n_x * n_z, -1, dec_width), "dx").reshape(blocks)
    column, far_up, far_down = lax.optimization_barrier((column, far_up, far_down))
    grad_kv = merge_quarters(place, (own, up, down, far_up, far_down))
    column = jnp.sum(column, axis=0, dtype=F32).astype(BF)
    grad_wq = jnp.sum(exchange(column, "dz"), axis=0, dtype=F32).astype(BF)
    return (mixed, grad_q, grad_kv, grad_wq)


def solution(mesh):
    cut = Mesh(mesh.devices.reshape(2, 2, 8, 4, 4), GRP + DP + ("mp",))
    heads = GRP + ("mp",)
    placed = (P(DP, heads), P(DP, heads), P(DP, None, "mp", GRP), P(), P(heads), P(DP, heads))
    return jax.shard_map(
        shards,
        mesh=cut,
        in_specs=placed,
        out_specs=(P(DP, heads), P(DP, heads), P(DP, None, "mp", GRP), P(DP, heads)),
        check_vma=False,
    )
```

```python
import functools

import jax
import jax.numpy as jnp
from jax import lax
from jax.experimental import pallas as pl
from jax.experimental.pallas import tpu as pltpu
from jax.sharding import Mesh
from jax.sharding import PartitionSpec as P

GROUP_LEN = 64
NEIGHBOURS = 2
HEAD_DIM = 128
EXTRA = 16
EPS = 1e-06
SCALE = HEAD_DIM ** (-0.5)
DP = ("dz", "dx")
GRP = ("yl", "co")
LINE = ("mp", "yl")
BF = jnp.bfloat16
F32 = jnp.float32
SMEM = pl.BlockSpec(memory_space=pltpu.SMEM)
VMEM = pl.BlockSpec(memory_space=pltpu.VMEM)
PARAMS = pltpu.CompilerParams(vmem_limit_bytes=24 << 20)
LAST = (((1,), (1,)), ((), ()))
FIRST = (((0,), (0,)), ((), ()))
PLAIN = (((1,), (0,)), ((), ()))


def call(kernel, scalars, arrays, outs, params=PARAMS):
    return pl.pallas_call(
        kernel,
        in_specs=[SMEM] * len(scalars) + [VMEM] * len(arrays),
        out_specs=[VMEM] * len(outs),
        out_shape=[jax.ShapeDtypeStruct(shape, kind) for shape, kind in outs],
        compiler_params=params,
    )(*scalars, *arrays)


def exchange(array, axes):
    return lax.all_to_all(array, axes, split_axis=0, concat_axis=0, tiled=True)


def copies(array, count):
    return jnp.broadcast_to(array[None], (count,) + array.shape)


def shift(array, axis, step):
    size = lax.axis_size(axis)
    return lax.ppermute(array, axis, [(i, (i + step) % size) for i in range(size)])


def dot(a, b, dims):
    return lax.dot_general(a, b, dims, preferred_element_type=F32)


def eye(size):
    rows = lax.broadcasted_iota(jnp.int32, (size, size), 0)
    return rows == lax.broadcasted_iota(jnp.int32, (size, size), 1)


def as_column(row):
    return jnp.sum(jnp.where(eye(row.shape[1]), row, 0.0), axis=1, keepdims=True)


def as_row(column):
    return jnp.sum(jnp.where(eye(column.shape[0]), column, 0.0), axis=0, keepdims=True)


def by_head(block):
    blank = jnp.zeros((block.shape[0], HEAD_DIM), block.dtype)
    upper = jnp.concatenate([block[:, :HEAD_DIM], blank], axis=1)
    lower = jnp.concatenate([blank, block[:, HEAD_DIM:]], axis=1)
    return jnp.concatenate([upper, lower], axis=0)


def own_head(both):
    half = both.shape[0] // 2
    return jnp.concatenate([both[:half, :HEAD_DIM], both[half:, HEAD_DIM:]], axis=1)


def pieces(row, count):
    index = lax.broadcasted_iota(jnp.int32, (EXTRA, row.shape[1]), 0)
    tile = jnp.zeros((EXTRA, row.shape[1]), F32)
    rest = row
    for i in range(count):
        part = rest.astype(BF).astype(F32)
        tile = jnp.where(index == i, part, tile)
        rest = rest - part
    return tile.astype(BF)


def write_slot(slots, slot, block, row, count):
    width = block.shape[1]
    for i in range(GROUP_LEN // EXTRA):
        slots[slot, :, i * width : (i + 1) * width] = block[i * EXTRA : (i + 1) * EXTRA]
    slots[slot, :, GROUP_LEN // EXTRA * width :] = pieces(row, count)


def read_slot(slots, slot, width, count):
    folds = GROUP_LEN // EXTRA
    tile = slots[slot]
    block = jnp.concatenate([tile[:, i * width : (i + 1) * width] for i in range(folds)], axis=0)
    return block, joined(tile[:, folds * width :], count)


def joined(tile, count):
    tile = tile.astype(F32)
    index = lax.broadcasted_iota(jnp.int32, tile.shape, 0)
    return jnp.sum(jnp.where(index < count, tile, 0.0), axis=0, keepdims=True)


def split_kernel(place, block0, block1, block2, block3, own, first, last, far_keys, far_values):
    own[...] = block0[...]
    first[...] = block1[...]
    last[...] = block3[...]
    far_keys[...] = block2[:, 0]
    far_values[...] = block2[:, 1]


def whole_rows(n, own, first, last, far_keys, far_values):
    return [
        jnp.concatenate([own[n, i], first[n, i], far[n], last[n, i]], axis=0)
        for i, far in enumerate((far_keys, far_values))
    ]


def second_step(first, arrived):
    return jnp.stack([first, arrived[:, 1]], axis=1)


def weight_rows(line, co, n_yl, n_co, n_mp):
    return (line % n_yl * n_co + co) * n_mp + line // n_yl


def query_kernel(sizes, place, source, mine, other, weight, slots, total):
    n_yl, n_co, n_mp, n_x = sizes
    span = mine.shape[2]
    for part, block in enumerate((mine, other)):
        co = lax.rem(place[1] + part, n_co)
        for line in range(mine.shape[0]):
            first = pl.multiple_of(weight_rows(line, co, n_yl, n_co, n_mp) * span, span)
            product = dot(block[line], weight[pl.ds(first, span), :], PLAIN)
            if part == 0 and line == 0:
                total[...] = product
            else:
                total[...] += product
    for k in range(source.shape[0]):
        c = k // NEIGHBOURS
        slots[source[k]] = total[c * GROUP_LEN : (c + 1) * GROUP_LEN].astype(BF)


def owner_forward_kernel(target, arrived, own, first, last, far_keys, far_values, slots, probs):
    for n in range(target.shape[0]):
        t = target[n]
        keys, values = whole_rows(n, own, first, last, far_keys, far_values)
        scores = dot(keys, by_head(arrived[t]), LAST) * SCALE
        top = jnp.max(scores, axis=0, keepdims=True)
        expo = jnp.exp(scores - top)
        total = jnp.sum(expo, axis=0, keepdims=True)
        prob = expo / total
        probs[n] = prob
        out = own_head(dot(prob.astype(BF), values, FIRST))
        write_slot(slots, t, out.astype(BF), top + jnp.log(total), 3)


def combine_kernel(source, arrived, d_mixed, gain, attended, shares, stats):
    stats[...] = jnp.zeros_like(stats)
    shares[...] = jnp.zeros_like(shares)
    width = attended.shape[1]
    for c in range(source.shape[0] // NEIGHBOURS):
        here = slice(c * GROUP_LEN, (c + 1) * GROUP_LEN)
        values, logs = zip(
            *[read_slot(arrived, source[NEIGHBOURS * c + k], width, 3) for k in range(NEIGHBOURS)]
        )
        top = jnp.maximum(logs[0], logs[1])
        expos = [jnp.exp(log - top) for log in logs]
        rest = 1.0 / (expos[0] + expos[1])
        out = jnp.zeros((GROUP_LEN, 2 * HEAD_DIM), F32)
        for k in range(NEIGHBOURS):
            share = expos[k] * rest
            shares[NEIGHBOURS * c + k : NEIGHBOURS * c + k + 1, :] = share
            column = as_column(share)
            value = values[k].astype(F32)
            out = out + jnp.concatenate(
                [
                    value[:, :HEAD_DIM] * column[:GROUP_LEN],
                    value[:, HEAD_DIM:] * column[GROUP_LEN:],
                ],
                axis=1,
            )
        attended[here, :] = out
        grad_in = d_mixed[here, :].astype(F32) * gain[...]
        column = jnp.concatenate(
            [
                jnp.sum(out * out, axis=1, keepdims=True),
                jnp.sum(grad_in * out, axis=1, keepdims=True),
            ],
            axis=0,
        )
        stats[c : c + 1, :] = as_row(column)


def grad_kernel(width, source, moved, attended, shares, d_mixed, gain, mixed, slots):
    total = jnp.sum(moved[...], axis=0)
    for c in range(source.shape[0] // NEIGHBOURS):
        here = slice(c * GROUP_LEN, (c + 1) * GROUP_LEN)
        column = as_column(total[c : c + 1, :])
        inverse = lax.rsqrt(column[:GROUP_LEN] / width + EPS)
        out = attended[here, :]
        grad_in = d_mixed[here, :].astype(F32) * gain[...]
        mixed[here, :] = (out * inverse * gain[...]).astype(BF)
        factor = column[GROUP_LEN:] * inverse * inverse / width
        grad = (inverse * (grad_in - out * factor)).astype(BF).astype(F32)
        inner = grad * out
        delta = jnp.concatenate(
            [
                jnp.sum(inner[:, :HEAD_DIM], axis=1, keepdims=True),
                jnp.sum(inner[:, HEAD_DIM:], axis=1, keepdims=True),
            ],
            axis=0,
        )
        for k in range(NEIGHBOURS):
            slot = source[NEIGHBOURS * c + k]
            share = as_column(shares[NEIGHBOURS * c + k : NEIGHBOURS * c + k + 1, :])
            scaled = jnp.concatenate(
                [grad[:, :HEAD_DIM] * share[:GROUP_LEN], grad[:, HEAD_DIM:] * share[GROUP_LEN:]],
                axis=1,
            )
            write_slot(slots, slot, scaled.astype(BF), as_row(delta * share), 2)


def owner_backward_kernel(target, arrived, queries, probs, *refs):
    kv_refs, (slots, own, up, down, first, last) = refs[:5], refs[5:]
    for n in range(target.shape[0]):
        t = target[n]
        keys, values = whole_rows(n, *kv_refs)
        block, delta = read_slot(arrived, t, keys.shape[1], 2)
        grad = by_head(block)
        query = by_head(queries[t])
        prob = probs[n]
        grad_scores = (prob * (dot(values, grad, LAST) - delta)).astype(BF)
        slots[t] = (own_head(dot(grad_scores, keys, FIRST)) * SCALE).astype(BF)
        grad_keys = (dot(grad_scores, query, PLAIN) * SCALE).astype(BF)
        grad_values = dot(prob.astype(BF), grad, PLAIN).astype(BF)
        rows = grad_keys.shape[0] // 4
        own[n, 0], own[n, 1] = grad_keys[:rows], grad_values[:rows]
        up[n, 0], first[n] = grad_keys[rows : 2 * rows], grad_values[rows : 2 * rows]
        up[n, 1], down[n, 1] = grad_keys[2 * rows : 3 * rows], grad_values[2 * rows : 3 * rows]
        down[n, 0], last[n] = grad_keys[3 * rows :], grad_values[3 * rows :]


def weight_kernel(sizes, place, source, arrived, mine, other, grad_q, partial):
    n_yl, n_co, n_mp, n_x = sizes
    for c in range(source.shape[0] // NEIGHBOURS):
        both = sum(arrived[source[NEIGHBOURS * c + k]].astype(F32) for k in range(NEIGHBOURS))
        grad_q[c * GROUP_LEN : (c + 1) * GROUP_LEN, :] = both.astype(BF)
    rows = partial.shape[2]
    per = mine.shape[2] // rows
    for part, block in enumerate((mine, other)):
        co = lax.rem(place[1] + part, n_co)
        for line in range(mine.shape[0]):
            first = weight_rows(line, co, n_yl, n_co, n_mp) * per
            product = dot(block[line], grad_q[...], FIRST).astype(BF)
            for i in range(per):
                partial[lax.rem(first + i, n_x), lax.div(first + i, n_x)] = product[
                    i * rows : (i + 1) * rows
                ]


def add_kernel(parts, out):
    total = parts[0].astype(F32)
    for i in range(1, parts.shape[0]):
        total = total + parts[i].astype(F32)
    out[...] = total.astype(BF)


def merge_kernel(place, own, up, down, far_up, far_down, out):
    step = pl.program_id(0)

    @pl.when(step == 0)
    def _():
        out[...] = own[...]

    @pl.when(step == 1)
    def _():
        out[:, 0] = up[:, 0]
        out[:, 1] = far_up[:, 0]

    @pl.when(step == 2)
    def _():
        out[:, 0] = far_up[:, 1]
        out[:, 1] = far_down[:, 1]

    @pl.when(step == 3)
    def _():
        out[:, 0] = down[:, 0]
        out[:, 1] = far_down[:, 0]


def split_by_quarter(place, kv):
    n, _, quarter, width = kv.shape
    part = width // 4
    take = [
        pl.BlockSpec((n, 2, quarter, part), functools.partial(block_at, d)) for d in range(4)
    ]
    pair, single = (n, 2, quarter, part), (n, quarter, part)
    shapes = [pair, pair, pair, single, single]
    return pl.pallas_call(
        split_kernel,
        grid_spec=pltpu.PrefetchScalarGridSpec(
            num_scalar_prefetch=1,
            grid=(1,),
            in_specs=take,
            out_specs=[
                pl.BlockSpec(shape, functools.partial(origin, len(shape))) for shape in shapes
            ],
        ),
        out_shape=[jax.ShapeDtypeStruct(shape, kv.dtype) for shape in shapes],
        compiler_params=PARAMS,
    )(place, kv, kv, kv, kv)


def block_at(d, i, place):
    return (0, 0, 0, lax.rem(place[0] + d, 4))


def merge_quarters(place, parts):
    n, _, quarter, part = parts[0].shape
    return pl.pallas_call(
        merge_kernel,
        grid_spec=pltpu.PrefetchScalarGridSpec(
            num_scalar_prefetch=1,
            grid=(4,),
            in_specs=[
                pl.BlockSpec(x.shape, functools.partial(origin, x.ndim)) for x in parts
            ],
            out_specs=pl.BlockSpec(
                (n, 2, quarter, part), lambda i, place: (0, 0, 0, lax.rem(place[0] + i, 4))
            ),
        ),
        out_shape=jax.ShapeDtypeStruct((n, 2, quarter, 4 * part), parts[0].dtype),
        compiler_params=PARAMS,
    )(place, *parts)


def origin(ndim, i, place):
    return (0,) * ndim


def shards(hidden, wq, kv_enc, group_neighbours, gain, d_mixed):
    n_z, n_x = lax.axis_size("dz"), lax.axis_size("dx")
    n_co, n_mp = lax.axis_size("co"), lax.axis_size("mp")
    n_dp = n_z * n_x
    heads = GRP + ("mp",)
    n_heads = lax.axis_size(heads)
    sizes = (lax.axis_size("yl"), n_co, n_mp, n_x)
    me_dp = lax.axis_index(DP)
    neigh_dev = kv_enc.shape[0]
    tok_dev, dec_width = hidden.shape[0], wq.shape[1]
    model = wq.shape[0] * n_dp
    gain = gain.reshape(1, dec_width)
    place = jnp.stack([lax.axis_index("mp"), lax.axis_index("co")]).astype(jnp.int32)
    flat_ids = group_neighbours.reshape(-1)
    slot_block = jnp.arange(flat_ids.shape[0], dtype=jnp.int32) // neigh_dev
    owned = me_dp * neigh_dev + jnp.arange(neigh_dev, dtype=jnp.int32)
    matches = flat_ids[None, :] == owned[:, None]
    target = jnp.sum(jnp.where(matches, slot_block[None, :], 0), axis=1)
    source = lax.dynamic_slice_in_dim(flat_ids, me_dp * neigh_dev, neigh_dev) // neigh_dev

    line = lax.all_gather(hidden, LINE, axis=0)
    own, first, last, far_keys, far_values = split_by_quarter(place, kv_enc)
    weight = exchange(copies(wq, n_dp), DP).reshape(-1, dec_width)
    for _ in range(2):
        far_keys, far_values = shift(far_keys, "mp", 1), shift(far_values, "mp", -1)
    line, far_keys, far_values, first, last = lax.optimization_barrier(
        (line, far_keys, far_values, first, last)
    )
    other = shift(line, "co", 1)
    kv = (own, shift(first, "mp", 1), shift(last, "mp", -1), far_keys, far_values)

    (slots,) = pl.pallas_call(
        functools.partial(query_kernel, sizes),
        in_specs=[SMEM, SMEM, VMEM, VMEM, VMEM],
        out_specs=[VMEM],
        out_shape=[jax.ShapeDtypeStruct((n_dp, GROUP_LEN, dec_width), BF)],
        scratch_shapes=[pltpu.VMEM((tok_dev, dec_width), F32)],
        compiler_params=PARAMS,
    )(place, source, line, other, weight)
    queries = exchange(slots, DP)

    wide = (n_dp, EXTRA, GROUP_LEN // EXTRA * dec_width + NEIGHBOURS * GROUP_LEN)
    span = kv_enc.shape[2] * n_mp
    slots, probs = call(
        owner_forward_kernel,
        (target,),
        (queries, *kv),
        [(wide, BF), ((neigh_dev, span, 2 * GROUP_LEN), F32)],
    )
    arrived = exchange(slots, DP)
    attended, shares, stats = call(
        combine_kernel,
        (source,),
        (arrived, d_mixed, gain),
        [((tok_dev, dec_width), F32), ((16, 128), F32), ((8, 128), F32)],
    )
    moved = exchange(copies(stats, n_heads), heads)
    mixed, slots = call(
        functools.partial(grad_kernel, model),
        (source,),
        (moved, attended, shares, d_mixed, gain),
        [((tok_dev, dec_width), BF), (wide, BF)],
    )
    arrived = exchange(slots, DP)
    slots, own, up, down, first, last = call(
        owner_backward_kernel,
        (target,),
        (arrived, queries, probs, *kv),
        [((n_dp, GROUP_LEN, dec_width), BF)]
        + [(own.shape, BF)] * 3
        + [(far_keys.shape, BF)] * 2,
        pltpu.CompilerParams(vmem_limit_bytes=60 << 20),
    )
    up, down = shift(up, "mp", -1), shift(down, "mp", 1)
    arrived = exchange(slots, DP)
    blocks = (n_x, n_z, wq.shape[0], dec_width)
    grad_q, partial = call(
        functools.partial(weight_kernel, sizes),
        (place, source),
        (arrived, line, other),
        [((tok_dev, dec_width), BF), (blocks, BF)],
    )
    partial, up, down = lax.optimization_barrier((partial, up, down))
    far_up = shift(second_step(first, up), "mp", -1)
    far_down = shift(second_step(last, down), "mp", 1)
    column = exchange(partial.reshape(n_x * n_z, -1, dec_width), "dx").reshape(blocks)
    column, far_up, far_down = lax.optimization_barrier((column, far_up, far_down))
    grad_kv = merge_quarters(place, (own, up, down, far_up, far_down))
    (column,) = call(add_kernel, (), (column,), [(blocks[1:], BF)])
    grad_wq = jnp.sum(exchange(column, "dz"), axis=0, dtype=F32).astype(BF)
    return (mixed, grad_q, grad_kv, grad_wq)


def solution(mesh):
    cut = Mesh(mesh.devices.reshape(2, 2, 8, 4, 4), GRP + DP + ("mp",))
    heads = GRP + ("mp",)
    placed = (P(DP, heads), P(DP, heads), P(DP, None, "mp", GRP), P(), P(heads), P(DP, heads))
    return jax.shard_map(
        shards,
        mesh=cut,
        in_specs=placed,
        out_specs=(P(DP, heads), P(DP, heads), P(DP, None, "mp", GRP), P(DP, heads)),
        check_vma=False,
    )
```

```python
import functools

import jax
import jax.numpy as jnp
from jax import lax
from jax.experimental import pallas as pl
from jax.experimental.pallas import tpu as pltpu
from jax.sharding import Mesh
from jax.sharding import PartitionSpec as P

GROUP_LEN = 64
NEIGHBOURS = 2
HEAD_DIM = 128
EXTRA = 16
EPS = 1e-06
SCALE = HEAD_DIM ** (-0.5)
DP = ("dz", "dx")
GRP = ("yl", "co")
LINE = ("mp", "yl")
BF = jnp.bfloat16
F32 = jnp.float32
SMEM = pl.BlockSpec(memory_space=pltpu.SMEM)
VMEM = pl.BlockSpec(memory_space=pltpu.VMEM)
PARAMS = pltpu.CompilerParams(vmem_limit_bytes=24 << 20)
LAST = (((1,), (1,)), ((), ()))
FIRST = (((0,), (0,)), ((), ()))
PLAIN = (((1,), (0,)), ((), ()))


def call(kernel, scalars, arrays, outs, params=PARAMS):
    return pl.pallas_call(
        kernel,
        in_specs=[SMEM] * len(scalars) + [VMEM] * len(arrays),
        out_specs=[VMEM] * len(outs),
        out_shape=[jax.ShapeDtypeStruct(shape, kind) for shape, kind in outs],
        compiler_params=params,
    )(*scalars, *arrays)


def exchange(array, axes):
    return lax.all_to_all(array, axes, split_axis=0, concat_axis=0, tiled=True)


def copies(array, count):
    return jnp.broadcast_to(array[None], (count,) + array.shape)


def shift(array, axis, step):
    size = lax.axis_size(axis)
    return lax.ppermute(array, axis, [(i, (i + step) % size) for i in range(size)])


def dot(a, b, dims):
    return lax.dot_general(a, b, dims, preferred_element_type=F32)


def eye(size):
    rows = lax.broadcasted_iota(jnp.int32, (size, size), 0)
    return rows == lax.broadcasted_iota(jnp.int32, (size, size), 1)


def as_column(row):
    return jnp.sum(jnp.where(eye(row.shape[1]), row, 0.0), axis=1, keepdims=True)


def as_row(column):
    return jnp.sum(jnp.where(eye(column.shape[0]), column, 0.0), axis=0, keepdims=True)


def by_head(block):
    blank = jnp.zeros((block.shape[0], HEAD_DIM), block.dtype)
    upper = jnp.concatenate([block[:, :HEAD_DIM], blank], axis=1)
    lower = jnp.concatenate([blank, block[:, HEAD_DIM:]], axis=1)
    return jnp.concatenate([upper, lower], axis=0)


def own_head(both):
    half = both.shape[0] // 2
    return jnp.concatenate([both[:half, :HEAD_DIM], both[half:, HEAD_DIM:]], axis=1)


def pieces(rows):
    index = lax.broadcasted_iota(jnp.int32, (EXTRA, rows[0].shape[1]), 0)
    tile = jnp.zeros((EXTRA, rows[0].shape[1]), F32)
    for k, rest in enumerate(rows):
        for i in range(3):
            part = rest.astype(BF).astype(F32)
            tile = jnp.where(index == 3 * k + i, part, tile)
            rest = rest - part
    return tile.astype(BF)


def joined(tile, k):
    index = lax.broadcasted_iota(jnp.int32, tile.shape, 0)
    ours = (index >= 3 * k) & (index < 3 * k + 3)
    return jnp.sum(jnp.where(ours, tile, 0.0), axis=0, keepdims=True)


def write_slot(slots, slot, block, rows):
    width = block.shape[1]
    for i in range(GROUP_LEN // EXTRA):
        slots[slot, :, i * width : (i + 1) * width] = block[i * EXTRA : (i + 1) * EXTRA]
    slots[slot, :, GROUP_LEN // EXTRA * width :] = pieces(rows)


def read_slot(slots, slot, width):
    folds = GROUP_LEN // EXTRA
    tile = slots[slot]
    block = jnp.concatenate([tile[:, i * width : (i + 1) * width] for i in range(folds)], axis=0)
    extra = tile[:, folds * width :].astype(F32)
    return block, joined(extra, 0), joined(extra, 1)


def split_kernel(place, block0, block1, block2, block3, own, first, last, far_keys, far_values):
    own[...] = block0[...]
    first[...] = block1[...]
    last[...] = block3[...]
    far_keys[...] = block2[:, 0]
    far_values[...] = block2[:, 1]


def whole_rows(n, own, first, last, far_keys, far_values):
    return [
        jnp.concatenate([own[n, i], first[n, i], far[n], last[n, i]], axis=0)
        for i, far in enumerate((far_keys, far_values))
    ]


def second_step(first, arrived):
    return jnp.stack([first, arrived[:, 1]], axis=1)


def weight_rows(line, co, n_yl, n_co, n_mp):
    return (line % n_yl * n_co + co) * n_mp + line // n_yl


def query_kernel(sizes, place, source, mine, other, weight, slots, total):
    n_yl, n_co, n_mp, n_x = sizes
    span = mine.shape[2]
    for part, block in enumerate((mine, other)):
        co = lax.rem(place[1] + part, n_co)
        for line in range(mine.shape[0]):
            first = pl.multiple_of(weight_rows(line, co, n_yl, n_co, n_mp) * span, span)
            product = dot(block[line], weight[pl.ds(first, span), :], PLAIN)
            if part == 0 and line == 0:
                total[...] = product
            else:
                total[...] += product
    for k in range(source.shape[0]):
        c = k // NEIGHBOURS
        slots[source[k]] = total[c * GROUP_LEN : (c + 1) * GROUP_LEN].astype(BF)


def owner_forward_kernel(target, arrived, own, first, last, far_keys, far_values, slots, probs):
    for n in range(target.shape[0]):
        t = target[n]
        keys, values = whole_rows(n, own, first, last, far_keys, far_values)
        scores = dot(keys, by_head(arrived[t]), LAST) * SCALE
        top = jnp.max(scores, axis=0, keepdims=True)
        expo = jnp.exp(scores - top)
        total = jnp.sum(expo, axis=0, keepdims=True)
        prob = expo / total
        probs[n] = prob
        out = own_head(dot(prob.astype(BF), values, FIRST))
        write_slot(slots, t, out.astype(BF), [top, total])


def combine_kernel(source, arrived, d_mixed, gain, attended, shares, stats):
    stats[...] = jnp.zeros_like(stats)
    shares[...] = jnp.zeros_like(shares)
    width = attended.shape[1]
    for c in range(source.shape[0] // NEIGHBOURS):
        here = slice(c * GROUP_LEN, (c + 1) * GROUP_LEN)
        values, tops, totals = zip(
            *[read_slot(arrived, source[NEIGHBOURS * c + k], width) for k in range(NEIGHBOURS)]
        )
        top = jnp.maximum(tops[0], tops[1])
        expos = [total * jnp.exp(part - top) for part, total in zip(tops, totals)]
        rest = 1.0 / (expos[0] + expos[1])
        out = jnp.zeros((GROUP_LEN, 2 * HEAD_DIM), F32)
        for k in range(NEIGHBOURS):
            share = expos[k] * rest
            shares[NEIGHBOURS * c + k : NEIGHBOURS * c + k + 1, :] = share
            column = as_column(share)
            value = values[k].astype(F32)
            out = out + jnp.concatenate(
                [
                    value[:, :HEAD_DIM] * column[:GROUP_LEN],
                    value[:, HEAD_DIM:] * column[GROUP_LEN:],
                ],
                axis=1,
            )
        attended[here, :] = out
        grad_in = d_mixed[here, :].astype(F32) * gain[...]
        column = jnp.concatenate(
            [
                jnp.sum(out * out, axis=1, keepdims=True),
                jnp.sum(grad_in * out, axis=1, keepdims=True),
            ],
            axis=0,
        )
        stats[c : c + 1, :] = as_row(column)


def grad_kernel(width, source, moved, attended, shares, d_mixed, gain, mixed, slots):
    total = jnp.sum(moved[...], axis=0)
    for c in range(source.shape[0] // NEIGHBOURS):
        here = slice(c * GROUP_LEN, (c + 1) * GROUP_LEN)
        column = as_column(total[c : c + 1, :])
        inverse = lax.rsqrt(column[:GROUP_LEN] / width + EPS)
        out = attended[here, :]
        grad_in = d_mixed[here, :].astype(F32) * gain[...]
        mixed[here, :] = (out * inverse * gain[...]).astype(BF)
        factor = column[GROUP_LEN:] * inverse * inverse / width
        grad = (inverse * (grad_in - out * factor)).astype(BF).astype(F32)
        inner = grad * out
        delta = jnp.concatenate(
            [
                jnp.sum(inner[:, :HEAD_DIM], axis=1, keepdims=True),
                jnp.sum(inner[:, HEAD_DIM:], axis=1, keepdims=True),
            ],
            axis=0,
        )
        delta = as_row(delta)
        for k in range(NEIGHBOURS):
            share = shares[NEIGHBOURS * c + k : NEIGHBOURS * c + k + 1, :]
            write_slot(slots, source[NEIGHBOURS * c + k], grad.astype(BF), [share, delta])


def owner_backward_kernel(target, arrived, queries, probs, *refs):
    kv_refs, (slots, own, up, down, first, last) = refs[:5], refs[5:]
    for n in range(target.shape[0]):
        t = target[n]
        keys, values = whole_rows(n, *kv_refs)
        block, share, delta = read_slot(arrived, t, keys.shape[1])
        grad = by_head(block)
        query = by_head(queries[t])
        prob = probs[n] * share
        grad_scores = (prob * (dot(values, grad, LAST) - delta)).astype(BF)
        slots[t] = (own_head(dot(grad_scores, keys, FIRST)) * SCALE).astype(BF)
        grad_keys = (dot(grad_scores, query, PLAIN) * SCALE).astype(BF)
        grad_values = dot(prob.astype(BF), grad, PLAIN).astype(BF)
        rows = grad_keys.shape[0] // 4
        own[n, 0], own[n, 1] = grad_keys[:rows], grad_values[:rows]
        up[n, 0], first[n] = grad_keys[rows : 2 * rows], grad_values[rows : 2 * rows]
        up[n, 1], down[n, 1] = grad_keys[2 * rows : 3 * rows], grad_values[2 * rows : 3 * rows]
        down[n, 0], last[n] = grad_keys[3 * rows :], grad_values[3 * rows :]


def weight_kernel(sizes, place, source, arrived, mine, other, grad_q, partial):
    n_yl, n_co, n_mp, n_x = sizes
    for c in range(source.shape[0] // NEIGHBOURS):
        both = sum(arrived[source[NEIGHBOURS * c + k]].astype(F32) for k in range(NEIGHBOURS))
        grad_q[c * GROUP_LEN : (c + 1) * GROUP_LEN, :] = both.astype(BF)
    rows = partial.shape[2]
    per = mine.shape[2] // rows
    for part, block in enumerate((mine, other)):
        co = lax.rem(place[1] + part, n_co)
        for line in range(mine.shape[0]):
            first = weight_rows(line, co, n_yl, n_co, n_mp) * per
            product = dot(block[line], grad_q[...], FIRST).astype(BF)
            for i in range(per):
                partial[lax.rem(first + i, n_x), lax.div(first + i, n_x)] = product[
                    i * rows : (i + 1) * rows
                ]


def add_kernel(parts, out):
    total = parts[0].astype(F32)
    for i in range(1, parts.shape[0]):
        total = total + parts[i].astype(F32)
    out[...] = total.astype(BF)


def merge_kernel(place, own, up, down, far_up, far_down, out):
    step = pl.program_id(0)

    @pl.when(step == 0)
    def _():
        out[...] = own[...]

    @pl.when(step == 1)
    def _():
        out[:, 0] = up[:, 0]
        out[:, 1] = far_up[:, 0]

    @pl.when(step == 2)
    def _():
        out[:, 0] = far_up[:, 1]
        out[:, 1] = far_down[:, 1]

    @pl.when(step == 3)
    def _():
        out[:, 0] = down[:, 0]
        out[:, 1] = far_down[:, 0]


def split_by_quarter(place, kv):
    n, _, quarter, width = kv.shape
    part = width // 4
    take = [
        pl.BlockSpec((n, 2, quarter, part), functools.partial(block_at, d)) for d in range(4)
    ]
    pair, single = (n, 2, quarter, part), (n, quarter, part)
    shapes = [pair, pair, pair, single, single]
    return pl.pallas_call(
        split_kernel,
        grid_spec=pltpu.PrefetchScalarGridSpec(
            num_scalar_prefetch=1,
            grid=(1,),
            in_specs=take,
            out_specs=[
                pl.BlockSpec(shape, functools.partial(origin, len(shape))) for shape in shapes
            ],
        ),
        out_shape=[jax.ShapeDtypeStruct(shape, kv.dtype) for shape in shapes],
        compiler_params=PARAMS,
    )(place, kv, kv, kv, kv)


def block_at(d, i, place):
    return (0, 0, 0, lax.rem(place[0] + d, 4))


def merge_quarters(place, parts):
    n, _, quarter, part = parts[0].shape
    return pl.pallas_call(
        merge_kernel,
        grid_spec=pltpu.PrefetchScalarGridSpec(
            num_scalar_prefetch=1,
            grid=(4,),
            in_specs=[
                pl.BlockSpec(x.shape, functools.partial(origin, x.ndim)) for x in parts
            ],
            out_specs=pl.BlockSpec(
                (n, 2, quarter, part), lambda i, place: (0, 0, 0, lax.rem(place[0] + i, 4))
            ),
        ),
        out_shape=jax.ShapeDtypeStruct((n, 2, quarter, 4 * part), parts[0].dtype),
        compiler_params=PARAMS,
    )(place, *parts)


def origin(ndim, i, place):
    return (0,) * ndim


def shards(hidden, wq, kv_enc, group_neighbours, gain, d_mixed):
    n_z, n_x = lax.axis_size("dz"), lax.axis_size("dx")
    n_co, n_mp = lax.axis_size("co"), lax.axis_size("mp")
    n_dp = n_z * n_x
    heads = GRP + ("mp",)
    n_heads = lax.axis_size(heads)
    sizes = (lax.axis_size("yl"), n_co, n_mp, n_x)
    me_dp = lax.axis_index(DP)
    neigh_dev = kv_enc.shape[0]
    tok_dev, dec_width = hidden.shape[0], wq.shape[1]
    model = wq.shape[0] * n_dp
    gain = gain.reshape(1, dec_width)
    place = jnp.stack([lax.axis_index("mp"), lax.axis_index("co")]).astype(jnp.int32)
    flat_ids = group_neighbours.reshape(-1)
    slot_block = jnp.arange(flat_ids.shape[0], dtype=jnp.int32) // neigh_dev
    owned = me_dp * neigh_dev + jnp.arange(neigh_dev, dtype=jnp.int32)
    matches = flat_ids[None, :] == owned[:, None]
    target = jnp.sum(jnp.where(matches, slot_block[None, :], 0), axis=1)
    source = lax.dynamic_slice_in_dim(flat_ids, me_dp * neigh_dev, neigh_dev) // neigh_dev

    line = lax.all_gather(hidden, LINE, axis=0)
    own, first, last, far_keys, far_values = split_by_quarter(place, kv_enc)
    weight = exchange(copies(wq, n_dp), DP).reshape(-1, dec_width)
    for _ in range(2):
        far_keys, far_values = shift(far_keys, "mp", 1), shift(far_values, "mp", -1)
    line, far_keys, far_values, first, last = lax.optimization_barrier(
        (line, far_keys, far_values, first, last)
    )
    other = shift(line, "co", 1)
    kv = (own, shift(first, "mp", 1), shift(last, "mp", -1), far_keys, far_values)

    (slots,) = pl.pallas_call(
        functools.partial(query_kernel, sizes),
        in_specs=[SMEM, SMEM, VMEM, VMEM, VMEM],
        out_specs=[VMEM],
        out_shape=[jax.ShapeDtypeStruct((n_dp, GROUP_LEN, dec_width), BF)],
        scratch_shapes=[pltpu.VMEM((tok_dev, dec_width), F32)],
        compiler_params=PARAMS,
    )(place, source, line, other, weight)
    queries = exchange(slots, DP)

    wide = (n_dp, EXTRA, GROUP_LEN // EXTRA * dec_width + NEIGHBOURS * GROUP_LEN)
    span = kv_enc.shape[2] * n_mp
    slots, probs = call(
        owner_forward_kernel,
        (target,),
        (queries, *kv),
        [(wide, BF), ((neigh_dev, span, 2 * GROUP_LEN), F32)],
    )
    arrived = exchange(slots, DP)
    attended, shares, stats = call(
        combine_kernel,
        (source,),
        (arrived, d_mixed, gain),
        [((tok_dev, dec_width), F32), ((16, 128), F32), ((8, 128), F32)],
    )
    moved = exchange(copies(stats, n_heads), heads)
    mixed, slots = call(
        functools.partial(grad_kernel, model),
        (source,),
        (moved, attended, shares, d_mixed, gain),
        [((tok_dev, dec_width), BF), (wide, BF)],
    )
    arrived = exchange(slots, DP)
    slots, own, up, down, first, last = call(
        owner_backward_kernel,
        (target,),
        (arrived, queries, probs, *kv),
        [((n_dp, GROUP_LEN, dec_width), BF)]
        + [(own.shape, BF)] * 3
        + [(far_keys.shape, BF)] * 2,
        pltpu.CompilerParams(vmem_limit_bytes=60 << 20),
    )
    up, down = shift(up, "mp", -1), shift(down, "mp", 1)
    arrived = exchange(slots, DP)
    blocks = (n_x, n_z, wq.shape[0], dec_width)
    grad_q, partial = call(
        functools.partial(weight_kernel, sizes),
        (place, source),
        (arrived, line, other),
        [((tok_dev, dec_width), BF), (blocks, BF)],
    )
    partial, up, down = lax.optimization_barrier((partial, up, down))
    far_up = shift(second_step(first, up), "mp", -1)
    far_down = shift(second_step(last, down), "mp", 1)
    column = exchange(partial.reshape(n_x * n_z, -1, dec_width), "dx").reshape(blocks)
    column, far_up, far_down = lax.optimization_barrier((column, far_up, far_down))
    grad_kv = merge_quarters(place, (own, up, down, far_up, far_down))
    (column,) = call(add_kernel, (), (column,), [(blocks[1:], BF)])
    grad_wq = jnp.sum(exchange(column, "dz"), axis=0, dtype=F32).astype(BF)
    return (mixed, grad_q, grad_kv, grad_wq)


def solution(mesh):
    cut = Mesh(mesh.devices.reshape(2, 2, 8, 4, 4), GRP + DP + ("mp",))
    heads = GRP + ("mp",)
    placed = (P(DP, heads), P(DP, heads), P(DP, None, "mp", GRP), P(), P(heads), P(DP, heads))
    return jax.shard_map(
        shards,
        mesh=cut,
        in_specs=placed,
        out_specs=(P(DP, heads), P(DP, heads), P(DP, None, "mp", GRP), P(DP, heads)),
        check_vma=False,
    )
```

```python
import functools

import jax
import jax.numpy as jnp
from jax import lax
from jax.experimental import pallas as pl
from jax.experimental.pallas import tpu as pltpu
from jax.sharding import Mesh
from jax.sharding import PartitionSpec as P

GROUP_LEN = 64
NEIGHBOURS = 2
HEAD_DIM = 128
EXTRA = 16
EPS = 1e-06
SCALE = HEAD_DIM ** (-0.5)
DP = ("dz", "dx")
GRP = ("yl", "co")
LINE = ("mp", "yl")
BF = jnp.bfloat16
F32 = jnp.float32
SMEM = pl.BlockSpec(memory_space=pltpu.SMEM)
VMEM = pl.BlockSpec(memory_space=pltpu.VMEM)
PARAMS = pltpu.CompilerParams(vmem_limit_bytes=24 << 20)
LARGE = pltpu.CompilerParams(vmem_limit_bytes=60 << 20)
LAST = (((1,), (1,)), ((), ()))
FIRST = (((0,), (0,)), ((), ()))
PLAIN = (((1,), (0,)), ((), ()))


def call(kernel, scalars, arrays, outs, params=PARAMS):
    return pl.pallas_call(
        kernel,
        in_specs=[SMEM] * len(scalars) + [VMEM] * len(arrays),
        out_specs=[VMEM] * len(outs),
        out_shape=[jax.ShapeDtypeStruct(shape, kind) for shape, kind in outs],
        compiler_params=params,
    )(*scalars, *arrays)


def exchange(array, axes):
    return lax.all_to_all(array, axes, split_axis=0, concat_axis=0, tiled=True)


def copies(array, count):
    return jnp.broadcast_to(array[None], (count,) + array.shape)


def shift(array, axis, step):
    size = lax.axis_size(axis)
    return lax.ppermute(array, axis, [(i, (i + step) % size) for i in range(size)])


def dot(a, b, dims):
    return lax.dot_general(a, b, dims, preferred_element_type=F32)


def eye(size):
    rows = lax.broadcasted_iota(jnp.int32, (size, size), 0)
    return rows == lax.broadcasted_iota(jnp.int32, (size, size), 1)


def as_column(row):
    return jnp.sum(jnp.where(eye(row.shape[1]), row, 0.0), axis=1, keepdims=True)


def as_row(column):
    return jnp.sum(jnp.where(eye(column.shape[0]), column, 0.0), axis=0, keepdims=True)


def by_head(block):
    blank = jnp.zeros((block.shape[0], HEAD_DIM), block.dtype)
    upper = jnp.concatenate([block[:, :HEAD_DIM], blank], axis=1)
    lower = jnp.concatenate([blank, block[:, HEAD_DIM:]], axis=1)
    return jnp.concatenate([upper, lower], axis=0)


def own_head(both):
    half = both.shape[0] // 2
    return jnp.concatenate([both[:half, :HEAD_DIM], both[half:, HEAD_DIM:]], axis=1)


def pieces(rows):
    index = lax.broadcasted_iota(jnp.int32, (EXTRA, rows[0].shape[1]), 0)
    tile = jnp.zeros((EXTRA, rows[0].shape[1]), F32)
    for k, rest in enumerate(rows):
        for i in range(3):
            part = rest.astype(BF).astype(F32)
            tile = jnp.where(index == 3 * k + i, part, tile)
            rest = rest - part
    return tile.astype(BF)


def joined(tile, k):
    index = lax.broadcasted_iota(jnp.int32, tile.shape, 0)
    ours = (index >= 3 * k) & (index < 3 * k + 3)
    return jnp.sum(jnp.where(ours, tile, 0.0), axis=0, keepdims=True)


def write_slot(slots, slot, block, rows):
    width = block.shape[1]
    for i in range(GROUP_LEN // EXTRA):
        slots[slot, :, i * width : (i + 1) * width] = block[i * EXTRA : (i + 1) * EXTRA]
    slots[slot, :, GROUP_LEN // EXTRA * width :] = pieces(rows)


def read_slot(slots, slot, width):
    folds = GROUP_LEN // EXTRA
    tile = slots[slot]
    block = jnp.concatenate([tile[:, i * width : (i + 1) * width] for i in range(folds)], axis=0)
    extra = tile[:, folds * width :].astype(F32)
    return block, joined(extra, 0), joined(extra, 1)


def split_kernel(place, block0, block1, block2, block3, own, first, last, far_keys, far_values):
    own[...] = block0[...]
    first[...] = block1[...]
    last[...] = block3[...]
    far_keys[...] = block2[:, 0]
    far_values[...] = block2[:, 1]


def whole_rows(n, own, first, last, far_keys, far_values):
    return [
        jnp.concatenate([own[n, i], first[n, i], far[n], last[n, i]], axis=0)
        for i, far in enumerate((far_keys, far_values))
    ]


def second_step(first, arrived):
    return jnp.stack([first, arrived[:, 1]], axis=1)


def weight_rows(line, co, n_yl, n_co, n_mp):
    return (line % n_yl * n_co + co) * n_mp + line // n_yl


def query_kernel(sizes, place, source, mine, other, weight, slots, total):
    n_yl, n_co, n_mp, n_x = sizes
    span = mine.shape[2]
    for part, block in enumerate((mine, other)):
        co = lax.rem(place[1] + part, n_co)
        for line in range(mine.shape[0]):
            first = pl.multiple_of(weight_rows(line, co, n_yl, n_co, n_mp) * span, span)
            product = dot(block[line], weight[pl.ds(first, span), :], PLAIN)
            if part == 0 and line == 0:
                total[...] = product
            else:
                total[...] += product
    for k in range(source.shape[0]):
        c = k // NEIGHBOURS
        slots[source[k]] = total[c * GROUP_LEN : (c + 1) * GROUP_LEN].astype(BF)


def owner_forward_kernel(target, arrived, own, first, last, far_keys, far_values, slots, probs):
    for n in range(target.shape[0]):
        t = target[n]
        keys, values = whole_rows(n, own, first, last, far_keys, far_values)
        scores = dot(keys, by_head(arrived[t]), LAST) * SCALE
        top = jnp.max(scores, axis=0, keepdims=True)
        expo = jnp.exp(scores - top)
        total = jnp.sum(expo, axis=0, keepdims=True)
        prob = expo / total
        probs[n] = prob
        out = own_head(dot(prob.astype(BF), values, FIRST))
        write_slot(slots, t, out.astype(BF), [top, total])


def combine_kernel(source, arrived, d_mixed, gain, attended, shares, stats):
    stats[...] = jnp.zeros_like(stats)
    shares[...] = jnp.zeros_like(shares)
    width = attended.shape[1]
    for c in range(source.shape[0] // NEIGHBOURS):
        here = slice(c * GROUP_LEN, (c + 1) * GROUP_LEN)
        values, tops, totals = zip(
            *[read_slot(arrived, source[NEIGHBOURS * c + k], width) for k in range(NEIGHBOURS)]
        )
        top = jnp.maximum(tops[0], tops[1])
        expos = [total * jnp.exp(part - top) for part, total in zip(tops, totals)]
        rest = 1.0 / (expos[0] + expos[1])
        out = jnp.zeros((GROUP_LEN, 2 * HEAD_DIM), F32)
        for k in range(NEIGHBOURS):
            share = expos[k] * rest
            shares[NEIGHBOURS * c + k : NEIGHBOURS * c + k + 1, :] = share
            column = as_column(share)
            value = values[k].astype(F32)
            out = out + jnp.concatenate(
                [
                    value[:, :HEAD_DIM] * column[:GROUP_LEN],
                    value[:, HEAD_DIM:] * column[GROUP_LEN:],
                ],
                axis=1,
            )
        attended[here, :] = out
        grad_in = d_mixed[here, :].astype(F32) * gain[...]
        column = jnp.concatenate(
            [
                jnp.sum(out * out, axis=1, keepdims=True),
                jnp.sum(grad_in * out, axis=1, keepdims=True),
            ],
            axis=0,
        )
        stats[c : c + 1, :] = as_row(column)


def grad_kernel(width, source, moved, attended, shares, d_mixed, gain, mixed, slots):
    total = jnp.sum(moved[...], axis=0)
    for c in range(source.shape[0] // NEIGHBOURS):
        here = slice(c * GROUP_LEN, (c + 1) * GROUP_LEN)
        column = as_column(total[c : c + 1, :])
        inverse = lax.rsqrt(column[:GROUP_LEN] / width + EPS)
        out = attended[here, :]
        grad_in = d_mixed[here, :].astype(F32) * gain[...]
        mixed[here, :] = (out * inverse * gain[...]).astype(BF)
        factor = column[GROUP_LEN:] * inverse * inverse / width
        grad = (inverse * (grad_in - out * factor)).astype(BF).astype(F32)
        inner = grad * out
        delta = jnp.concatenate(
            [
                jnp.sum(inner[:, :HEAD_DIM], axis=1, keepdims=True),
                jnp.sum(inner[:, HEAD_DIM:], axis=1, keepdims=True),
            ],
            axis=0,
        )
        delta = as_row(delta)
        for k in range(NEIGHBOURS):
            share = shares[NEIGHBOURS * c + k : NEIGHBOURS * c + k + 1, :]
            write_slot(slots, source[NEIGHBOURS * c + k], grad.astype(BF), [share, delta])


def owner_backward_kernel(target, arrived, queries, probs, *refs):
    kv_refs, (slots, own, up, down, first, last) = refs[:5], refs[5:]
    for n in range(target.shape[0]):
        t = target[n]
        keys, values = whole_rows(n, *kv_refs)
        block, share, delta = read_slot(arrived, t, keys.shape[1])
        grad = by_head(block)
        query = by_head(queries[t])
        prob = probs[n] * share
        grad_scores = (prob * (dot(values, grad, LAST) - delta)).astype(BF)
        slots[t] = (own_head(dot(grad_scores, keys, FIRST)) * SCALE).astype(BF)
        grad_keys = (dot(grad_scores, query, PLAIN) * SCALE).astype(BF)
        grad_values = dot(prob.astype(BF), grad, PLAIN).astype(BF)
        rows = grad_keys.shape[0] // 4
        own[n, 0], own[n, 1] = grad_keys[:rows], grad_values[:rows]
        up[n, 0], first[n] = grad_keys[rows : 2 * rows], grad_values[rows : 2 * rows]
        up[n, 1], down[n, 1] = grad_keys[2 * rows : 3 * rows], grad_values[2 * rows : 3 * rows]
        down[n, 0], last[n] = grad_keys[3 * rows :], grad_values[3 * rows :]


def weight_kernel(sizes, place, source, arrived, mine, other, grad_q, partial):
    n_yl, n_co, n_mp, n_x = sizes
    for c in range(source.shape[0] // NEIGHBOURS):
        both = sum(arrived[source[NEIGHBOURS * c + k]].astype(F32) for k in range(NEIGHBOURS))
        grad_q[c * GROUP_LEN : (c + 1) * GROUP_LEN, :] = both.astype(BF)
    rows = partial.shape[2]
    per = mine.shape[2] // rows
    for part, block in enumerate((mine, other)):
        co = lax.rem(place[1] + part, n_co)
        for line in range(mine.shape[0]):
            first = weight_rows(line, co, n_yl, n_co, n_mp) * per
            product = dot(block[line], grad_q[...], FIRST).astype(BF)
            for i in range(per):
                partial[lax.rem(first + i, n_x), lax.div(first + i, n_x)] = product[
                    i * rows : (i + 1) * rows
                ]


def add_kernel(parts, out):
    total = parts[0].astype(F32)
    for i in range(1, parts.shape[0]):
        total = total + parts[i].astype(F32)
    out[...] = total.astype(BF)


def merge_kernel(place, own, up, down, far_up, far_down, out):
    step = pl.program_id(0)

    @pl.when(step == 0)
    def _():
        out[...] = own[...]

    @pl.when(step == 1)
    def _():
        out[:, 0] = up[:, 0]
        out[:, 1] = far_up[:, 0]

    @pl.when(step == 2)
    def _():
        out[:, 0] = far_up[:, 1]
        out[:, 1] = far_down[:, 1]

    @pl.when(step == 3)
    def _():
        out[:, 0] = down[:, 0]
        out[:, 1] = far_down[:, 0]


def split_by_quarter(place, kv):
    n, _, quarter, width = kv.shape
    part = width // 4
    take = [
        pl.BlockSpec((n, 2, quarter, part), functools.partial(block_at, d)) for d in range(4)
    ]
    pair, single = (n, 2, quarter, part), (n, quarter, part)
    shapes = [pair, pair, pair, single, single]
    return pl.pallas_call(
        split_kernel,
        grid_spec=pltpu.PrefetchScalarGridSpec(
            num_scalar_prefetch=1,
            grid=(1,),
            in_specs=take,
            out_specs=[
                pl.BlockSpec(shape, functools.partial(origin, len(shape))) for shape in shapes
            ],
        ),
        out_shape=[jax.ShapeDtypeStruct(shape, kv.dtype) for shape in shapes],
        compiler_params=PARAMS,
    )(place, kv, kv, kv, kv)


def block_at(d, i, place):
    return (0, 0, 0, lax.rem(place[0] + d, 4))


def merge_quarters(place, parts):
    n, _, quarter, part = parts[0].shape
    return pl.pallas_call(
        merge_kernel,
        grid_spec=pltpu.PrefetchScalarGridSpec(
            num_scalar_prefetch=1,
            grid=(4,),
            in_specs=[
                pl.BlockSpec(x.shape, functools.partial(origin, x.ndim)) for x in parts
            ],
            out_specs=pl.BlockSpec(
                (n, 2, quarter, part), lambda i, place: (0, 0, 0, lax.rem(place[0] + i, 4))
            ),
        ),
        out_shape=jax.ShapeDtypeStruct((n, 2, quarter, 4 * part), parts[0].dtype),
        compiler_params=LARGE,
    )(place, *parts)


def origin(ndim, i, place):
    return (0,) * ndim


def shards(hidden, wq, kv_enc, group_neighbours, gain, d_mixed):
    n_z, n_x = lax.axis_size("dz"), lax.axis_size("dx")
    n_co, n_mp = lax.axis_size("co"), lax.axis_size("mp")
    n_dp = n_z * n_x
    heads = GRP + ("mp",)
    n_heads = lax.axis_size(heads)
    sizes = (lax.axis_size("yl"), n_co, n_mp, n_x)
    me_dp = lax.axis_index(DP)
    neigh_dev = kv_enc.shape[0]
    tok_dev, dec_width = hidden.shape[0], wq.shape[1]
    model = wq.shape[0] * n_dp
    gain = gain.reshape(1, dec_width)
    place = jnp.stack([lax.axis_index("mp"), lax.axis_index("co")]).astype(jnp.int32)
    flat_ids = group_neighbours.reshape(-1)
    slot_block = jnp.arange(flat_ids.shape[0], dtype=jnp.int32) // neigh_dev
    owned = me_dp * neigh_dev + jnp.arange(neigh_dev, dtype=jnp.int32)
    matches = flat_ids[None, :] == owned[:, None]
    target = jnp.sum(jnp.where(matches, slot_block[None, :], 0), axis=1)
    source = lax.dynamic_slice_in_dim(flat_ids, me_dp * neigh_dev, neigh_dev) // neigh_dev

    line = lax.all_gather(hidden, LINE, axis=0)
    own, first, last, far_keys, far_values = split_by_quarter(place, kv_enc)
    weight = exchange(copies(wq, n_dp), DP).reshape(-1, dec_width)
    for _ in range(2):
        far_keys, far_values = shift(far_keys, "mp", 1), shift(far_values, "mp", -1)
    line, far_keys, far_values, first, last = lax.optimization_barrier(
        (line, far_keys, far_values, first, last)
    )
    other = shift(line, "co", 1)
    kv = (own, shift(first, "mp", 1), shift(last, "mp", -1), far_keys, far_values)

    (slots,) = pl.pallas_call(
        functools.partial(query_kernel, sizes),
        in_specs=[SMEM, SMEM, VMEM, VMEM, VMEM],
        out_specs=[VMEM],
        out_shape=[jax.ShapeDtypeStruct((n_dp, GROUP_LEN, dec_width), BF)],
        scratch_shapes=[pltpu.VMEM((tok_dev, dec_width), F32)],
        compiler_params=PARAMS,
    )(place, source, line, other, weight)
    queries = exchange(slots, DP)

    wide = (n_dp, EXTRA, GROUP_LEN // EXTRA * dec_width + NEIGHBOURS * GROUP_LEN)
    span = kv_enc.shape[2] * n_mp
    slots, probs = call(
        owner_forward_kernel,
        (target,),
        (queries, *kv),
        [(wide, BF), ((neigh_dev, span, 2 * GROUP_LEN), F32)],
    )
    arrived = exchange(slots, DP)
    attended, shares, stats = call(
        combine_kernel,
        (source,),
        (arrived, d_mixed, gain),
        [((tok_dev, dec_width), F32), ((16, 128), F32), ((8, 128), F32)],
    )
    moved = exchange(copies(stats, n_heads), heads)
    mixed, slots = call(
        functools.partial(grad_kernel, model),
        (source,),
        (moved, attended, shares, d_mixed, gain),
        [((tok_dev, dec_width), BF), (wide, BF)],
    )
    arrived = exchange(slots, DP)
    slots, own, up, down, first, last = call(
        owner_backward_kernel,
        (target,),
        (arrived, queries, probs, *kv),
        [((n_dp, GROUP_LEN, dec_width), BF)]
        + [(own.shape, BF)] * 3
        + [(far_keys.shape, BF)] * 2,
        LARGE,
    )
    up, down = shift(up, "mp", -1), shift(down, "mp", 1)
    arrived = exchange(slots, DP)
    blocks = (n_x, n_z, wq.shape[0], dec_width)
    grad_q, partial = call(
        functools.partial(weight_kernel, sizes),
        (place, source),
        (arrived, line, other),
        [((tok_dev, dec_width), BF), (blocks, BF)],
    )
    partial, up, down = lax.optimization_barrier((partial, up, down))
    far_up = shift(second_step(first, up), "mp", -1)
    far_down = shift(second_step(last, down), "mp", 1)
    column = exchange(partial.reshape(n_x * n_z, -1, dec_width), "dx").reshape(blocks)
    column, far_up, far_down = lax.optimization_barrier((column, far_up, far_down))
    grad_kv = merge_quarters(place, (own, up, down, far_up, far_down))
    (column,) = call(add_kernel, (), (column,), [(blocks[1:], BF)])
    grad_wq = jnp.sum(exchange(column, "dz"), axis=0, dtype=F32).astype(BF)
    return (mixed, grad_q, grad_kv, grad_wq)


def solution(mesh):
    cut = Mesh(mesh.devices.reshape(2, 2, 8, 4, 4), GRP + DP + ("mp",))
    heads = GRP + ("mp",)
    placed = (P(DP, heads), P(DP, heads), P(DP, None, "mp", GRP), P(), P(heads), P(DP, heads))
    return jax.shard_map(
        shards,
        mesh=cut,
        in_specs=placed,
        out_specs=(P(DP, heads), P(DP, heads), P(DP, None, "mp", GRP), P(DP, heads)),
        check_vma=False,
    )
```

```python
import functools

import jax
import jax.numpy as jnp
from jax import lax
from jax.experimental import pallas as pl
from jax.experimental.pallas import tpu as pltpu
from jax.sharding import Mesh
from jax.sharding import PartitionSpec as P

GROUP_LEN = 64
NEIGHBOURS = 2
HEAD_DIM = 128
EXTRA = 16
EPS = 1e-06
SCALE = HEAD_DIM ** (-0.5)
DP = ("dz", "dx")
GRP = ("yl", "co")
LINE = ("mp", "yl")
BF = jnp.bfloat16
F32 = jnp.float32
SMEM = pl.BlockSpec(memory_space=pltpu.SMEM)
VMEM = pl.BlockSpec(memory_space=pltpu.VMEM)
PARAMS = pltpu.CompilerParams(vmem_limit_bytes=24 << 20)
LARGE = pltpu.CompilerParams(vmem_limit_bytes=60 << 20)
LAST = (((1,), (1,)), ((), ()))
FIRST = (((0,), (0,)), ((), ()))
PLAIN = (((1,), (0,)), ((), ()))


def call(kernel, scalars, arrays, outs, params=PARAMS):
    return pl.pallas_call(
        kernel,
        in_specs=[SMEM] * len(scalars) + [VMEM] * len(arrays),
        out_specs=[VMEM] * len(outs),
        out_shape=[jax.ShapeDtypeStruct(shape, kind) for shape, kind in outs],
        compiler_params=params,
    )(*scalars, *arrays)


def exchange(array, axes):
    return lax.all_to_all(array, axes, split_axis=0, concat_axis=0, tiled=True)


def copies(array, count):
    return jnp.broadcast_to(array[None], (count,) + array.shape)


def shift(array, axis, step):
    size = lax.axis_size(axis)
    return lax.ppermute(array, axis, [(i, (i + step) % size) for i in range(size)])


def dot(a, b, dims):
    return lax.dot_general(a, b, dims, preferred_element_type=F32)


def eye(size):
    rows = lax.broadcasted_iota(jnp.int32, (size, size), 0)
    return rows == lax.broadcasted_iota(jnp.int32, (size, size), 1)


def as_column(row):
    return jnp.sum(jnp.where(eye(row.shape[1]), row, 0.0), axis=1, keepdims=True)


def as_row(column):
    return jnp.sum(jnp.where(eye(column.shape[0]), column, 0.0), axis=0, keepdims=True)


def by_head(block):
    blank = jnp.zeros((block.shape[0], HEAD_DIM), block.dtype)
    upper = jnp.concatenate([block[:, :HEAD_DIM], blank], axis=1)
    lower = jnp.concatenate([blank, block[:, HEAD_DIM:]], axis=1)
    return jnp.concatenate([upper, lower], axis=0)


def own_head(both):
    half = both.shape[0] // 2
    return jnp.concatenate([both[:half, :HEAD_DIM], both[half:, HEAD_DIM:]], axis=1)


def pieces(rows):
    index = lax.broadcasted_iota(jnp.int32, (EXTRA, rows[0].shape[1]), 0)
    tile = jnp.zeros((EXTRA, rows[0].shape[1]), F32)
    for k, rest in enumerate(rows):
        for i in range(3):
            part = rest.astype(BF).astype(F32)
            tile = jnp.where(index == 3 * k + i, part, tile)
            rest = rest - part
    return tile.astype(BF)


def joined(tile, k):
    index = lax.broadcasted_iota(jnp.int32, tile.shape, 0)
    ours = (index >= 3 * k) & (index < 3 * k + 3)
    return jnp.sum(jnp.where(ours, tile, 0.0), axis=0, keepdims=True)


def write_slot(slots, slot, block, rows):
    width = block.shape[1]
    for i in range(GROUP_LEN // EXTRA):
        slots[slot, :, i * width : (i + 1) * width] = block[i * EXTRA : (i + 1) * EXTRA]
    slots[slot, :, GROUP_LEN // EXTRA * width :] = pieces(rows)


def read_slot(slots, slot, width):
    folds = GROUP_LEN // EXTRA
    tile = slots[slot]
    block = jnp.concatenate([tile[:, i * width : (i + 1) * width] for i in range(folds)], axis=0)
    extra = tile[:, folds * width :].astype(F32)
    return block, joined(extra, 0), joined(extra, 1)


def split_kernel(place, block0, block1, block2, block3, own, first, last, far_keys, far_values):
    own[...] = block0[...]
    first[...] = block1[...]
    last[...] = block3[...]
    far_keys[...] = block2[:, 0]
    far_values[...] = block2[:, 1]


def whole_rows(n, own, first, last, far_keys, far_values):
    return [
        jnp.concatenate([own[n, i], first[n, i], far[n], last[n, i]], axis=0)
        for i, far in enumerate((far_keys, far_values))
    ]


def second_step(first, arrived):
    return jnp.stack([first, arrived[:, 1]], axis=1)


def weight_rows(line, co, n_yl, n_co, n_mp):
    return (line % n_yl * n_co + co) * n_mp + line // n_yl


def query_kernel(sizes, place, source, mine, other, weight, slots, total):
    n_yl, n_co, n_mp, n_x = sizes
    span = mine.shape[2]
    for part, block in enumerate((mine, other)):
        co = lax.rem(place[1] + part, n_co)
        for line in range(mine.shape[0]):
            first = pl.multiple_of(weight_rows(line, co, n_yl, n_co, n_mp) * span, span)
            product = dot(block[line], weight[pl.ds(first, span), :], PLAIN)
            if part == 0 and line == 0:
                total[...] = product
            else:
                total[...] += product
    for k in range(source.shape[0]):
        c = k // NEIGHBOURS
        slots[source[k]] = total[c * GROUP_LEN : (c + 1) * GROUP_LEN].astype(BF)


def owner_forward_kernel(target, arrived, own, first, last, far_keys, far_values, slots, probs):
    for n in range(target.shape[0]):
        t = target[n]
        keys, values = whole_rows(n, own, first, last, far_keys, far_values)
        scores = dot(keys, by_head(arrived[t]), LAST) * SCALE
        top = jnp.max(scores, axis=0, keepdims=True)
        expo = jnp.exp(scores - top)
        total = jnp.sum(expo, axis=0, keepdims=True)
        prob = expo / total
        probs[n] = prob
        out = own_head(dot(prob.astype(BF), values, FIRST))
        write_slot(slots, t, out.astype(BF), [top, total])


def combine_kernel(source, arrived, d_mixed, gain, attended, shares, stats):
    stats[...] = jnp.zeros_like(stats)
    shares[...] = jnp.zeros_like(shares)
    width = attended.shape[1]
    for c in range(source.shape[0] // NEIGHBOURS):
        here = slice(c * GROUP_LEN, (c + 1) * GROUP_LEN)
        values, tops, totals = zip(
            *[read_slot(arrived, source[NEIGHBOURS * c + k], width) for k in range(NEIGHBOURS)]
        )
        top = jnp.maximum(tops[0], tops[1])
        expos = [total * jnp.exp(part - top) for part, total in zip(tops, totals)]
        rest = 1.0 / (expos[0] + expos[1])
        out = jnp.zeros((GROUP_LEN, 2 * HEAD_DIM), F32)
        for k in range(NEIGHBOURS):
            share = expos[k] * rest
            shares[NEIGHBOURS * c + k : NEIGHBOURS * c + k + 1, :] = share
            column = as_column(share)
            value = values[k].astype(F32)
            out = out + jnp.concatenate(
                [
                    value[:, :HEAD_DIM] * column[:GROUP_LEN],
                    value[:, HEAD_DIM:] * column[GROUP_LEN:],
                ],
                axis=1,
            )
        attended[here, :] = out
        grad_in = d_mixed[here, :].astype(F32) * gain[...]
        column = jnp.concatenate(
            [
                jnp.sum(out * out, axis=1, keepdims=True),
                jnp.sum(grad_in * out, axis=1, keepdims=True),
            ],
            axis=0,
        )
        stats[c : c + 1, :] = as_row(column)


def grad_kernel(width, source, moved, attended, shares, d_mixed, gain, mixed, slots):
    total = jnp.sum(moved[...], axis=0)
    for c in range(source.shape[0] // NEIGHBOURS):
        here = slice(c * GROUP_LEN, (c + 1) * GROUP_LEN)
        column = as_column(total[c : c + 1, :])
        inverse = lax.rsqrt(column[:GROUP_LEN] / width + EPS)
        out = attended[here, :]
        grad_in = d_mixed[here, :].astype(F32) * gain[...]
        mixed[here, :] = (out * inverse * gain[...]).astype(BF)
        factor = column[GROUP_LEN:] * inverse * inverse / width
        grad = (inverse * (grad_in - out * factor)).astype(BF).astype(F32)
        inner = grad * out
        delta = jnp.concatenate(
            [
                jnp.sum(inner[:, :HEAD_DIM], axis=1, keepdims=True),
                jnp.sum(inner[:, HEAD_DIM:], axis=1, keepdims=True),
            ],
            axis=0,
        )
        delta = as_row(delta)
        for k in range(NEIGHBOURS):
            share = shares[NEIGHBOURS * c + k : NEIGHBOURS * c + k + 1, :]
            write_slot(slots, source[NEIGHBOURS * c + k], grad.astype(BF), [share, delta])


def owner_backward_kernel(target, arrived, queries, probs, *refs):
    kv_refs, (slots, own, up, down, first, last) = refs[:5], refs[5:]
    for n in range(target.shape[0]):
        t = target[n]
        keys, values = whole_rows(n, *kv_refs)
        block, share, delta = read_slot(arrived, t, keys.shape[1])
        grad = by_head(block)
        query = by_head(queries[t])
        prob = probs[n] * share
        grad_scores = (prob * (dot(values, grad, LAST) - delta)).astype(BF)
        slots[t] = (own_head(dot(grad_scores, keys, FIRST)) * SCALE).astype(BF)
        grad_keys = (dot(grad_scores, query, PLAIN) * SCALE).astype(BF)
        grad_values = dot(prob.astype(BF), grad, PLAIN).astype(BF)
        rows = grad_keys.shape[0] // 4
        own[n, 0], own[n, 1] = grad_keys[:rows], grad_values[:rows]
        up[n, 0], first[n] = grad_keys[rows : 2 * rows], grad_values[rows : 2 * rows]
        up[n, 1], down[n, 1] = grad_keys[2 * rows : 3 * rows], grad_values[2 * rows : 3 * rows]
        down[n, 0], last[n] = grad_keys[3 * rows :], grad_values[3 * rows :]


def weight_kernel(
    sizes, place, source, arrived, mine_far, other_far, grad_q, partial, mine, other, sems
):
    n_yl, n_co, n_mp, n_x = sizes
    fetches = [
        pltpu.make_async_copy(mine_far, mine, sems.at[0]),
        pltpu.make_async_copy(other_far, other, sems.at[1]),
    ]
    for fetch in fetches:
        fetch.start()
    for c in range(source.shape[0] // NEIGHBOURS):
        both = sum(arrived[source[NEIGHBOURS * c + k]].astype(F32) for k in range(NEIGHBOURS))
        grad_q[c * GROUP_LEN : (c + 1) * GROUP_LEN, :] = both.astype(BF)
    rows = partial.shape[2]
    per = mine.shape[2] // rows
    for part, block in enumerate((mine, other)):
        co = lax.rem(place[1] + part, n_co)
        fetches[part].wait()
        for line in range(mine.shape[0]):
            first = weight_rows(line, co, n_yl, n_co, n_mp) * per
            product = dot(block[line], grad_q[...], FIRST).astype(BF)
            for i in range(per):
                partial[lax.rem(first + i, n_x), lax.div(first + i, n_x)] = product[
                    i * rows : (i + 1) * rows
                ]


def add_kernel(parts, out):
    total = parts[0].astype(F32)
    for i in range(1, parts.shape[0]):
        total = total + parts[i].astype(F32)
    out[...] = total.astype(BF)


def merge_kernel(place, own, up, down, far_up, far_down, out):
    step = pl.program_id(0)

    @pl.when(step == 0)
    def _():
        out[...] = own[...]

    @pl.when(step == 1)
    def _():
        out[:, 0] = up[:, 0]
        out[:, 1] = far_up[:, 0]

    @pl.when(step == 2)
    def _():
        out[:, 0] = far_up[:, 1]
        out[:, 1] = far_down[:, 1]

    @pl.when(step == 3)
    def _():
        out[:, 0] = down[:, 0]
        out[:, 1] = far_down[:, 0]


def split_by_quarter(place, kv):
    n, _, quarter, width = kv.shape
    part = width // 4
    take = [
        pl.BlockSpec((n, 2, quarter, part), functools.partial(block_at, d)) for d in range(4)
    ]
    pair, single = (n, 2, quarter, part), (n, quarter, part)
    shapes = [pair, pair, pair, single, single]
    return pl.pallas_call(
        split_kernel,
        grid_spec=pltpu.PrefetchScalarGridSpec(
            num_scalar_prefetch=1,
            grid=(1,),
            in_specs=take,
            out_specs=[
                pl.BlockSpec(shape, functools.partial(origin, len(shape))) for shape in shapes
            ],
        ),
        out_shape=[jax.ShapeDtypeStruct(shape, kv.dtype) for shape in shapes],
        compiler_params=PARAMS,
    )(place, kv, kv, kv, kv)


def block_at(d, i, place):
    return (0, 0, 0, lax.rem(place[0] + d, 4))


def merge_quarters(place, parts):
    n, _, quarter, part = parts[0].shape
    return pl.pallas_call(
        merge_kernel,
        grid_spec=pltpu.PrefetchScalarGridSpec(
            num_scalar_prefetch=1,
            grid=(4,),
            in_specs=[
                pl.BlockSpec(x.shape, functools.partial(origin, x.ndim)) for x in parts
            ],
            out_specs=pl.BlockSpec(
                (n, 2, quarter, part), lambda i, place: (0, 0, 0, lax.rem(place[0] + i, 4))
            ),
        ),
        out_shape=jax.ShapeDtypeStruct((n, 2, quarter, 4 * part), parts[0].dtype),
        compiler_params=LARGE,
    )(place, *parts)


def origin(ndim, i, place):
    return (0,) * ndim


def shards(hidden, wq, kv_enc, group_neighbours, gain, d_mixed):
    n_z, n_x = lax.axis_size("dz"), lax.axis_size("dx")
    n_co, n_mp = lax.axis_size("co"), lax.axis_size("mp")
    n_dp = n_z * n_x
    heads = GRP + ("mp",)
    n_heads = lax.axis_size(heads)
    sizes = (lax.axis_size("yl"), n_co, n_mp, n_x)
    me_dp = lax.axis_index(DP)
    neigh_dev = kv_enc.shape[0]
    tok_dev, dec_width = hidden.shape[0], wq.shape[1]
    model = wq.shape[0] * n_dp
    gain = gain.reshape(1, dec_width)
    place = jnp.stack([lax.axis_index("mp"), lax.axis_index("co")]).astype(jnp.int32)
    flat_ids = group_neighbours.reshape(-1)
    slot_block = jnp.arange(flat_ids.shape[0], dtype=jnp.int32) // neigh_dev
    owned = me_dp * neigh_dev + jnp.arange(neigh_dev, dtype=jnp.int32)
    matches = flat_ids[None, :] == owned[:, None]
    target = jnp.sum(jnp.where(matches, slot_block[None, :], 0), axis=1)
    source = lax.dynamic_slice_in_dim(flat_ids, me_dp * neigh_dev, neigh_dev) // neigh_dev

    line = lax.all_gather(hidden, LINE, axis=0)
    own, first, last, far_keys, far_values = split_by_quarter(place, kv_enc)
    weight = exchange(copies(wq, n_dp), DP).reshape(-1, dec_width)
    for _ in range(2):
        far_keys, far_values = shift(far_keys, "mp", 1), shift(far_values, "mp", -1)
    line, far_keys, far_values, first, last = lax.optimization_barrier(
        (line, far_keys, far_values, first, last)
    )
    other = shift(line, "co", 1)
    kv = (own, shift(first, "mp", 1), shift(last, "mp", -1), far_keys, far_values)

    (slots,) = pl.pallas_call(
        functools.partial(query_kernel, sizes),
        in_specs=[SMEM, SMEM, VMEM, VMEM, VMEM],
        out_specs=[VMEM],
        out_shape=[jax.ShapeDtypeStruct((n_dp, GROUP_LEN, dec_width), BF)],
        scratch_shapes=[pltpu.VMEM((tok_dev, dec_width), F32)],
        compiler_params=PARAMS,
    )(place, source, line, other, weight)
    queries = exchange(slots, DP)

    wide = (n_dp, EXTRA, GROUP_LEN // EXTRA * dec_width + NEIGHBOURS * GROUP_LEN)
    span = kv_enc.shape[2] * n_mp
    slots, probs = call(
        owner_forward_kernel,
        (target,),
        (queries, *kv),
        [(wide, BF), ((neigh_dev, span, 2 * GROUP_LEN), F32)],
    )
    arrived = exchange(slots, DP)
    attended, shares, stats = call(
        combine_kernel,
        (source,),
        (arrived, d_mixed, gain),
        [((tok_dev, dec_width), F32), ((16, 128), F32), ((8, 128), F32)],
    )
    moved = exchange(copies(stats, n_heads), heads)
    mixed, slots = call(
        functools.partial(grad_kernel, model),
        (source,),
        (moved, attended, shares, d_mixed, gain),
        [((tok_dev, dec_width), BF), (wide, BF)],
    )
    arrived = exchange(slots, DP)
    slots, own, up, down, first, last = call(
        owner_backward_kernel,
        (target,),
        (arrived, queries, probs, *kv),
        [((n_dp, GROUP_LEN, dec_width), BF)]
        + [(own.shape, BF)] * 3
        + [(far_keys.shape, BF)] * 2,
        LARGE,
    )
    up, down = shift(up, "mp", -1), shift(down, "mp", 1)
    arrived = exchange(slots, DP)
    blocks = (n_x, n_z, wq.shape[0], dec_width)
    far = pl.BlockSpec(memory_space=pl.ANY)
    grad_q, partial = pl.pallas_call(
        functools.partial(weight_kernel, sizes),
        in_specs=[SMEM, SMEM, VMEM, far, far],
        out_specs=[VMEM, VMEM],
        out_shape=[
            jax.ShapeDtypeStruct((tok_dev, dec_width), BF),
            jax.ShapeDtypeStruct(blocks, BF),
        ],
        scratch_shapes=[
            pltpu.VMEM(line.shape, line.dtype),
            pltpu.VMEM(line.shape, line.dtype),
            pltpu.SemaphoreType.DMA((2,)),
        ],
        compiler_params=LARGE,
    )(place, source, arrived, line, other)
    partial, up, down = lax.optimization_barrier((partial, up, down))
    far_up = shift(second_step(first, up), "mp", -1)
    far_down = shift(second_step(last, down), "mp", 1)
    column = exchange(partial.reshape(n_x * n_z, -1, dec_width), "dx").reshape(blocks)
    column, far_up, far_down = lax.optimization_barrier((column, far_up, far_down))
    grad_kv = merge_quarters(place, (own, up, down, far_up, far_down))
    (column,) = call(add_kernel, (), (column,), [(blocks[1:], BF)])
    grad_wq = jnp.sum(exchange(column, "dz"), axis=0, dtype=F32).astype(BF)
    return (mixed, grad_q, grad_kv, grad_wq)


def solution(mesh):
    cut = Mesh(mesh.devices.reshape(2, 2, 8, 4, 4), GRP + DP + ("mp",))
    heads = GRP + ("mp",)
    placed = (P(DP, heads), P(DP, heads), P(DP, None, "mp", GRP), P(), P(heads), P(DP, heads))
    return jax.shard_map(
        shards,
        mesh=cut,
        in_specs=placed,
        out_specs=(P(DP, heads), P(DP, heads), P(DP, None, "mp", GRP), P(DP, heads)),
        check_vma=False,
    )
```
